32 devices in a mesh: section: 2 (over x), seq: 2 (over y), fsdp: 8 (over z, core).
Axes of the slice: x: 2, y: 2, z: 4, core: 2. Of those that a mesh axis runs over, the one named last changes fastest.
Arguments:
- tokens: bfloat16 [8, 2, 512, 1024], P('fsdp', None, 'seq'), may hold values from -6 to 6
- cotangent: bfloat16 [8, 2, 512, 1024], P('fsdp', None, 'seq'), may hold values from -6 to 6
- norm_gains: float32 [2, 2, 1024], P('section'), may hold values from 0.5 to 1.5
- head_gains: float32 [2, 64], replicated, may hold values from 0.5 to 1.5
- conv_kernel: float32 [3, 1024], replicated, may hold values from -0.1 to 0.1
- mix_in: bfloat16 [2, 1024, 2048], P('section', 'fsdp'), may hold values from -0.1875 to 0.1875
- mix_out: bfloat16 [2, 1024, 1024], P('section', 'fsdp'), may hold values from -2 to 2
- w_gate: bfloat16 [2, 1024, 4608], P('section', 'fsdp'), may hold values from -0.1875 to 0.1875
- w_up: bfloat16 [2, 1024, 4608], P('section', 'fsdp'), may hold values from -0.1875 to 0.1875
- w_down: bfloat16 [2, 4608, 1024], P('section', 'fsdp'), may hold values from -0.09375 to 0.09375
- conv_c: bfloat16 [1024, 1024], P(('section', 'fsdp')), may hold values from -0.1875 to 0.1875
Outputs:
- ends: float32 [2, 8, 2, 512, 1024], P('section', 'fsdp', None, 'seq')
- grad_norm_gains: float32 [2, 2, 1024], replicated
- grad_head_gains: float32 [2, 64], replicated
- grad_conv_kernel: float32 [3, 1024], replicated
- grad_mix_in: float32 [2, 1024, 2048], P('section', ('seq', 'fsdp'))
- grad_mix_out: float32 [2, 1024, 1024], P('section', ('seq', 'fsdp'))
- grad_w_gate: float32 [2, 1024, 4608], P('section', ('seq', 'fsdp'))
- grad_w_up: float32 [2, 1024, 4608], P('section', ('seq', 'fsdp'))
- grad_w_down: float32 [2, 4608, 1024], P('section', ('seq', 'fsdp'))
- grad_conv_c: float32 [1024, 1024], P(('section', 'seq', 'fsdp'))
The draws below stay inside these ranges and needn't reach their ends.
All inputs are finite; a program needn't handle non-finite values.
Results may differ from the reference program's by a relative error of at most 0.025.
Values may be sent and summed in bfloat16 or wider, within the bound.
No kernel may reach another device: no remote copies, remote signals or barrier semaphores. Data moves between devices by JAX's collectives and lax.ppermute only.
A program may use at most 448 MiB of HBM per device.

```python
import jax
import jax.numpy as jnp
from jax import lax

D = 1024
FF = 4608
HEADS = 16
KV_HEADS = 8
HEAD = 64
LENGTH = 1024
STRETCHES = 2
SEQS = 8
CL = 512


def block_scale(key, extent, cuts, smallest, largest):
    factor_of = 1.0
    for dim, blocks in cuts:
        draws = jax.random.uniform(jax.random.fold_in(jax.random.fold_in(key, 6), dim), (blocks,), jnp.float32, smallest / len(cuts), largest / len(cuts))
        factor_of = factor_of * jnp.repeat(jnp.exp(draws), extent[dim] // blocks).reshape((-1,) + (1,) * (len(extent) - 1 - dim))
    return factor_of


def scatter_about(rng, shape, deviation, bound, cuts=(), kind=jnp.bfloat16):
    values = jax.random.normal(rng, shape, jnp.float32) * deviation
    if len(cuts) > 0:
        values = block_scale(rng, shape, cuts, -0.22, 0.18) * values
    return jnp.clip(values, min=-bound, max=bound).astype(kind)


def setup_inputs(seed: int = 0) -> dict:
    splits = jax.random.split(jax.random.key(seed), 12)
    return {
        "tokens": scatter_about(splits[0], (SEQS, STRETCHES, CL, D), 1.0, 6.0, ((0, 8), (2, 2))),
        "cotangent": scatter_about(splits[1], (SEQS, STRETCHES, CL, D), 1.0, 6.0, ((0, 8), (2, 2))),
        "norm_gains": jnp.clip(1.0 + 0.1 * jax.random.normal(splits[2], (2, 2, D), jnp.float32), 0.5, 1.5),
        "head_gains": jnp.clip(1.0 + 0.1 * jax.random.normal(splits[3], (2, HEAD), jnp.float32), 0.5, 1.5),
        "conv_kernel": jnp.clip(jax.random.uniform(splits[4], (3, D), jnp.float32, -0.1, 0.1), -0.1, 0.1),
        "mix_in": scatter_about(splits[5], (2, D, 2 * D), D ** -0.5, 0.1875, ((0, 2), (1, 8))),
        "mix_out": scatter_about(splits[6], (2, D, D), (max(D // 128, 1)) ** -0.5, 2.0, ((0, 2), (1, 8))),
        "w_gate": scatter_about(splits[7], (2, D, FF), D ** -0.5, 0.1875, ((0, 2), (1, 8))),
        "w_up": scatter_about(splits[8], (2, D, FF), D ** -0.5, 0.1875, ((0, 2), (1, 8))),
        "w_down": scatter_about(splits[9], (2, FF, D), FF ** -0.5, 0.09375, ((0, 2), (1, 8))),
        "conv_c": scatter_about(splits[10], (D, D), D ** -0.5, 0.1875, ((0, 16),)),
    }


EPSILON = 1e-05
THETA = 1000000.0
NEGATIVE = -1e+30

@jax.custom_vjp
def low(v):
    return lax.optimization_barrier(v.astype(jnp.bfloat16)).astype(jnp.float32)

@jax.custom_vjp
def low_back(v):
    return v

def low_keep(v):
    return (low(v), None)

def low_pass(kept, grad):
    return (grad,)

def back_keep(v):
    return (v, None)

def back_low(kept, grad):
    return (low(grad),)
low.defvjp(low_keep, low_pass)
low_back.defvjp(back_keep, back_low)

def matmul(left, right):
    return jnp.dot(left, right, precision=lax.Precision.HIGHEST, preferred_element_type=jnp.float32)

def rms_scale(value):
    return lax.rsqrt(lax.optimization_barrier(jnp.mean(value * value, axis=-1, keepdims=True)) + EPSILON)

def rotate(value, positions):
    half = value.shape[-1] // 2
    frequency = THETA ** (-jnp.arange(half, dtype=jnp.float32) * 2.0 / value.shape[-1])
    angle = positions.astype(jnp.float32)[:, None] * frequency[None, :]
    cosine = jnp.cos(angle)[:, None, :]
    sine = jnp.sin(angle)[:, None, :]
    first, second = (value[..., :half], value[..., half:])
    return jnp.concatenate([first * cosine - second * sine, second * cosine + first * sine], axis=-1)

def feed_forward(params, hidden, layer):
    normed = low(hidden * rms_scale(hidden) * params['norm_gains'][layer, 1])
    gate = low_back(matmul(normed, params['w_gate'][layer]))
    upward = low_back(matmul(normed, params['w_up'][layer]))
    active = low(jax.nn.silu(gate) * upward)
    return hidden + low_back(matmul(active, params['w_down'][layer]))

def attention_layer(params, inputs):
    count = inputs.shape[0]
    heads_per = HEADS // KV_HEADS
    normed = low(inputs * rms_scale(inputs) * params['norm_gains'][0, 0])
    mixed = low_back(low(matmul(normed, params['mix_in'][0])))
    mixed = mixed.reshape(count, KV_HEADS, (heads_per + 2) * HEAD)
    query = mixed[:, :, :heads_per * HEAD].reshape(count, KV_HEADS, heads_per, HEAD)
    keys = mixed[:, :, heads_per * HEAD:(heads_per + 1) * HEAD]
    values = mixed[:, :, (heads_per + 1) * HEAD:]
    positions = jnp.arange(count)
    query = query * rms_scale(query) * params['head_gains'][0]
    keys = keys * rms_scale(keys) * params['head_gains'][1]
    query = low(rotate(query.reshape(count, HEADS, HEAD), positions)).reshape(count, KV_HEADS, heads_per, HEAD)
    keys = low(rotate(keys, positions))
    scores = low_back(jnp.einsum('tgjd,sgd->gjts', query, keys, precision=lax.Precision.HIGHEST) * HEAD ** (-0.5))
    scores = jnp.where(positions[:, None] >= positions[None, :], scores, NEGATIVE)
    probs = low(jax.nn.softmax(scores, axis=-1))
    heads = jnp.einsum('gjts,sgd->tgjd', probs, values, precision=lax.Precision.HIGHEST).reshape(count, HEADS * HEAD)
    heads = low_back(low(heads))
    return feed_forward(params, inputs + low_back(matmul(heads, params['mix_out'][0])), 0)

def conv_layer(params, inputs):
    normed = low(inputs * rms_scale(inputs) * params['norm_gains'][1, 0])
    paired = low_back(matmul(normed, params['mix_in'][1]))
    gate = low_back(low(matmul(normed, params['conv_c'])))
    product = low_back(low(paired[:, :D] * paired[:, D:]))
    kernel = params['conv_kernel']
    once = jnp.concatenate([jnp.zeros_like(product[:1]), product[:-1]], axis=0)
    twice = jnp.concatenate([jnp.zeros_like(product[:2]), product[:-2]], axis=0)
    state = kernel[0] * twice + kernel[1] * once + kernel[2] * product
    heads = low_back(low(gate * state))
    return feed_forward(params, inputs + low_back(matmul(heads, params['mix_out'][1])), 1)

def blocks(params, inputs):
    linked = low_back(low(attention_layer(params, inputs)))
    return conv_layer(params, linked)

def reference(tokens, cotangent, norm_gains, head_gains, conv_kernel, mix_in, mix_out, w_gate, w_up, w_down, conv_c):
    params = {'norm_gains': norm_gains.astype(jnp.float32), 'head_gains': head_gains.astype(jnp.float32), 'conv_kernel': conv_kernel.astype(jnp.float32), 'mix_in': mix_in.astype(jnp.float32), 'mix_out': mix_out.astype(jnp.float32), 'w_gate': w_gate.astype(jnp.float32), 'w_up': w_up.astype(jnp.float32), 'w_down': w_down.astype(jnp.float32), 'conv_c': conv_c.astype(jnp.float32)}
    inputs = tokens.astype(jnp.float32).reshape(SEQS, LENGTH, D)
    seeds = cotangent.astype(jnp.float32).reshape(SEQS, LENGTH, D)

    def single(total, couple):
        result, pullback = jax.vjp(blocks, params, couple[0])
        grads, dinputs = pullback(couple[1])
        return (jax.tree.map(jnp.add, total, grads), (dinputs, result))
    zeros = jax.tree.map(jnp.zeros_like, params)
    total, (dinputs, results) = lax.scan(single, zeros, (inputs, seeds))
    ends = jnp.stack([dinputs, results]).reshape(2, SEQS, STRETCHES, LENGTH // STRETCHES, D)
    return (ends, total['norm_gains'], total['head_gains'], total['conv_kernel'], total['mix_in'], total['mix_out'], total['w_gate'], total['w_up'], total['w_down'], total['conv_c'])
```

```python
import functools

import jax
import jax.numpy as jnp
from jax import lax
from jax.experimental import pallas as pl
from jax.experimental.pallas import tpu as pltpu
from jax.sharding import PartitionSpec as P

HEADS = 16
KV_HEADS = 8
HEAD = 64
PAIR = 2 * HEAD
GROUP = 2 * PAIR

EPSILON = 1e-05
THETA = 1000000.0
NEGATIVE = -1e30
BF16 = jnp.bfloat16
F32 = jnp.float32
VMEM_LIMIT = 56 * 1024 * 1024


def rms_scale(value):
    return lax.rsqrt(jnp.mean(value * value, axis=-1, keepdims=True) + EPSILON)


def norm_back(grad_out, value, scale, gain):
    inner = grad_out * gain
    return scale * (inner - value * scale * scale * jnp.mean(inner * value, axis=-1, keepdims=True))


def matmul(left, right):
    return jnp.dot(left, right, preferred_element_type=F32)


def matmul_t(left, right):
    return lax.dot_general(left, right, (((1,), (1,)), ((), ())), preferred_element_type=F32)


def outer_sum(left, right):
    return lax.dot_general(left, right, (((0,), (0,)), ((), ())), preferred_element_type=F32)


def params():
    return pltpu.CompilerParams(vmem_limit_bytes=VMEM_LIMIT)


def group_mean(value):
    row = lax.broadcasted_iota(jnp.int32, (PAIR, PAIR), 0) // HEAD
    col = lax.broadcasted_iota(jnp.int32, (PAIR, PAIR), 1) // HEAD
    ones = jnp.where(row == col, 1.0 / HEAD, 0.0).astype(F32)
    return jnp.dot(value, ones, precision=lax.Precision.HIGHEST, preferred_element_type=F32)


def lane_swap(value):
    lane = lax.broadcasted_iota(jnp.int32, value.shape, 1) % HEAD
    return jnp.where(
        lane < HEAD // 2, pltpu.roll(value, PAIR - HEAD // 2, 1), pltpu.roll(value, HEAD // 2, 1)
    )


def project_kernel(x_ref, w_ref, cos_ref, sin_ref, gain_ref, raw_ref, q_ref, kv_ref):
    raw = jnp.dot(x_ref[...], w_ref[...], preferred_element_type=F32).astype(BF16)
    raw_ref[...] = raw
    for part, out in ((0, q_ref), (1, kv_ref)):
        vec = raw[:, part * PAIR : (part + 1) * PAIR].astype(F32)
        normed = vec * lax.rsqrt(group_mean(vec * vec) + EPSILON) * gain_ref[part : part + 1, :]
        turned = normed * cos_ref[...] + lane_swap(normed) * sin_ref[...]
        if part == 1:
            lane = lax.broadcasted_iota(jnp.int32, vec.shape, 1)
            turned = jnp.where(lane < HEAD, turned, vec)
        out[...] = turned.astype(BF16)


def project(normed, weight, cosine, sine, gain_rows):
    tokens, width = normed.shape
    whole = lambda g: (0, 0)
    column = lambda g: (0, g)
    return pl.pallas_call(
        project_kernel,
        grid=(KV_HEADS,),
        in_specs=[
            pl.BlockSpec((tokens, width), whole),
            pl.BlockSpec((width, GROUP), column),
            pl.BlockSpec((tokens, PAIR), whole),
            pl.BlockSpec((tokens, PAIR), whole),
            pl.BlockSpec((8, PAIR), whole),
        ],
        out_specs=[
            pl.BlockSpec((tokens, GROUP), column),
            pl.BlockSpec((tokens, PAIR), column),
            pl.BlockSpec((tokens, PAIR), column),
        ],
        out_shape=[
            jax.ShapeDtypeStruct((tokens, KV_HEADS * GROUP), BF16),
            jax.ShapeDtypeStruct((tokens, KV_HEADS * PAIR), BF16),
            jax.ShapeDtypeStruct((tokens, KV_HEADS * PAIR), BF16),
        ],
        compiler_params=params(),
        cost_estimate=pl.CostEstimate(
            flops=2 * tokens * width * KV_HEADS * GROUP, bytes_accessed=12 << 20, transcendentals=0
        ),
    )(normed, weight, cosine, sine, gain_rows)


def attend_kernel(rows, stretches, part_ref, q_ref, own_ref, peer_ref, out_ref):
    second = part_ref[0] == 1
    for stretch in range(stretches):
        blocks = []
        for s in range(stretch + 1):
            blocks += [own_ref[s * rows : (s + 1) * rows, :], peer_ref[s * rows : (s + 1) * rows, :]]
        pack = jnp.concatenate(blocks, axis=0)
        keys, values = (pack[:, :HEAD], pack[:, HEAD:])
        count = pack.shape[0]
        row = lax.broadcasted_iota(jnp.int32, (rows, count), 0)
        col = lax.broadcasted_iota(jnp.int32, (rows, count), 1) - stretch * 2 * rows
        allowed = (col <= row) | ((col >= rows) & second)
        for j in range(2):
            query = q_ref[stretch * rows : (stretch + 1) * rows, j * HEAD : (j + 1) * HEAD]
            scores = matmul_t(query, keys) * HEAD ** (-0.5)
            scores = jnp.where(allowed, scores, NEGATIVE)
            exponent = jnp.exp(scores - jnp.max(scores, axis=1, keepdims=True))
            total = jnp.sum(exponent, axis=1, keepdims=True)
            probs = (exponent * (1.0 / total)).astype(BF16)
            out_ref[stretch * rows : (stretch + 1) * rows, j * HEAD : (j + 1) * HEAD] = jnp.dot(
                probs, values, preferred_element_type=F32
            ).astype(BF16)


def attend(part, query, own, peer, rows, stretches):
    tokens = query.shape[0]
    column = lambda g: (0, g)
    return pl.pallas_call(
        functools.partial(attend_kernel, rows, stretches),
        grid=(KV_HEADS,),
        in_specs=[pl.BlockSpec(memory_space=pltpu.SMEM)]
        + [pl.BlockSpec((tokens, PAIR), column)] * 3,
        out_specs=pl.BlockSpec((tokens, PAIR), column),
        out_shape=jax.ShapeDtypeStruct((tokens, KV_HEADS * PAIR), BF16),
        compiler_params=params(),
        cost_estimate=pl.CostEstimate(
            flops=10_000_000_000, bytes_accessed=4 << 20, transcendentals=7_000_000
        ),
    )(part, query, own, peer)


def attend_back_kernel(
    rows, stretches, part_ref, q_ref, own_ref, peer_ref, grad_ref, dq_ref, down_ref, dpeer_ref
):
    second = part_ref[0] == 1
    for stretch in reversed(range(stretches)):
        blocks = []
        for s in range(stretch + 1):
            blocks += [own_ref[s * rows : (s + 1) * rows, :], peer_ref[s * rows : (s + 1) * rows, :]]
        pack = jnp.concatenate(blocks, axis=0)
        keys, values = (pack[:, :HEAD], pack[:, HEAD:])
        count = pack.shape[0]
        col = lax.broadcasted_iota(jnp.int32, (count, rows), 0) - stretch * 2 * rows
        row = lax.broadcasted_iota(jnp.int32, (count, rows), 1)
        allowed = (col <= row) | ((col >= rows) & second)
        span = slice(stretch * rows, (stretch + 1) * rows)
        dkeys, dvalues, dquery = (0.0, 0.0, [])
        for j in range(2):
            query = q_ref[span, j * HEAD : (j + 1) * HEAD]
            grad = grad_ref[span, j * HEAD : (j + 1) * HEAD]
            scores = matmul_t(keys, query) * HEAD ** (-0.5)
            scores = jnp.where(allowed, scores, NEGATIVE)
            exponent = jnp.exp(scores - jnp.max(scores, axis=0, keepdims=True))
            probs = exponent * (1.0 / jnp.sum(exponent, axis=0, keepdims=True))
            dprobs = matmul_t(values, grad)
            dscores = probs * (dprobs - jnp.sum(probs * dprobs, axis=0, keepdims=True))
            dscores = dscores.astype(BF16)
            dvalues += jnp.dot(probs.astype(BF16), grad, preferred_element_type=F32)
            dkeys += jnp.dot(dscores, query, preferred_element_type=F32) * HEAD ** (-0.5)
            dquery.append(outer_sum(dscores, keys) * HEAD ** (-0.5))
        dq_ref[span, :] = jnp.concatenate(dquery, axis=1)
        both = jnp.concatenate([dkeys, dvalues], axis=1)
        for s in range(stretch + 1):
            for place, out in ((2 * s, down_ref), (2 * s + 1, dpeer_ref)):
                piece = both[place * rows : (place + 1) * rows]
                span_s = slice(s * rows, (s + 1) * rows)
                if stretch == stretches - 1:
                    out[span_s, :] = piece
                else:
                    out[span_s, :] += piece


def attend_back(part, query, own, peer, grad, rows, stretches):
    tokens = query.shape[0]
    column = lambda g: (0, g)
    shape = jax.ShapeDtypeStruct((tokens, KV_HEADS * PAIR), F32)
    return pl.pallas_call(
        functools.partial(attend_back_kernel, rows, stretches),
        grid=(KV_HEADS,),
        in_specs=[pl.BlockSpec(memory_space=pltpu.SMEM)]
        + [pl.BlockSpec((tokens, PAIR), column)] * 4,
        out_specs=[pl.BlockSpec((tokens, PAIR), column)] * 3,
        out_shape=[shape] * 3,
        compiler_params=params(),
        cost_estimate=pl.CostEstimate(
            flops=25_000_000_000, bytes_accessed=12 << 20, transcendentals=7_000_000
        ),
    )(part, query, own, peer, grad)


def project_back_kernel(
    raw_ref, dq_ref, own_ref, recv_ref, cos_ref, sin_ref, gain_ref, w_ref, pack_ref, normed_ref, head_ref
):
    first = pl.program_id(0) == 0
    grads = []
    for part in range(2):
        vec = raw_ref[:, part * PAIR : (part + 1) * PAIR].astype(F32)
        if part == 0:
            grad = dq_ref[...]
        else:
            grad = own_ref[...] + recv_ref[...].astype(F32)
        gain = gain_ref[part : part + 1, :]
        scale = lax.rsqrt(group_mean(vec * vec) + EPSILON)
        turned = grad * cos_ref[...] - lane_swap(grad) * sin_ref[...]
        gain_sum = jnp.sum(turned * vec * scale, axis=0, keepdims=True)
        inner = turned * gain
        back = scale * (inner - vec * scale * scale * group_mean(inner * vec))
        if part == 1:
            lane = lax.broadcasted_iota(jnp.int32, vec.shape, 1)
            back = jnp.where(lane < HEAD, back, grad)
        back = back.astype(BF16)
        pack_ref[:, part * PAIR : (part + 1) * PAIR] = back
        grads.append((back, gain_sum))
    total = matmul_t(grads[0][0], w_ref[:, :PAIR]) + matmul_t(grads[1][0], w_ref[:, PAIR:])

    @pl.when(first)
    def _():
        normed_ref[...] = total
        head_ref[...] = jnp.zeros_like(head_ref)

    @pl.when(jnp.logical_not(first))
    def _():
        normed_ref[...] += total

    for part in range(2):
        head_ref[part : part + 1, :] += grads[part][1]


def project_back(raw, dquery, own, recv, cosine, sine, gain_rows, weight):
    tokens = raw.shape[0]
    width = weight.shape[0]
    whole = lambda g: (0, 0)
    column = lambda g: (0, g)
    return pl.pallas_call(
        project_back_kernel,
        grid=(KV_HEADS,),
        in_specs=[
            pl.BlockSpec((tokens, GROUP), column),
            pl.BlockSpec((tokens, PAIR), column),
            pl.BlockSpec((tokens, PAIR), column),
            pl.BlockSpec((tokens, PAIR), column),
            pl.BlockSpec((tokens, PAIR), whole),
            pl.BlockSpec((tokens, PAIR), whole),
            pl.BlockSpec((8, PAIR), whole),
            pl.BlockSpec((width, GROUP), column),
        ],
        out_specs=[
            pl.BlockSpec((tokens, GROUP), column),
            pl.BlockSpec((tokens, width), whole),
            pl.BlockSpec((8, PAIR), whole),
        ],
        out_shape=[
            jax.ShapeDtypeStruct((tokens, KV_HEADS * GROUP), BF16),
            jax.ShapeDtypeStruct((tokens, width), F32),
            jax.ShapeDtypeStruct((8, PAIR), F32),
        ],
        compiler_params=params(),
        cost_estimate=pl.CostEstimate(
            flops=2 * tokens * width * KV_HEADS * GROUP, bytes_accessed=16 << 20, transcendentals=0
        ),
    )(raw, dquery, own, recv, cosine, sine, gain_rows, weight)


def forward_kernel(x_ref, base_ref, g_ref, u_ref, d_ref, out_ref, act_ref, one_ref, two_ref):
    gate = jnp.dot(x_ref[...], g_ref[...], preferred_element_type=F32)
    upward = jnp.dot(x_ref[...], u_ref[...], preferred_element_type=F32)
    sigma = jax.nn.sigmoid(gate)
    silu = gate * sigma
    active = (silu * upward).astype(BF16)
    act_ref[...] = active
    one_ref[...] = (upward * sigma * (1.0 + gate * (1.0 - sigma))).astype(BF16)
    two_ref[...] = silu.astype(BF16)
    down = jnp.dot(active, d_ref[...], preferred_element_type=F32)

    @pl.when(pl.program_id(0) == 0)
    def _():
        out_ref[...] = base_ref[...] + down

    @pl.when(pl.program_id(0) > 0)
    def _():
        out_ref[...] += down


def backward_kernel(grad_ref, one_ref, two_ref, g_ref, u_ref, d_ref, out_ref, dg_ref, du_ref):
    active = matmul_t(grad_ref[...], d_ref[...])
    dgate = (active * one_ref[...].astype(F32)).astype(BF16)
    dup = (active * two_ref[...].astype(F32)).astype(BF16)
    dg_ref[...] = dgate
    du_ref[...] = dup
    total = matmul_t(dgate, g_ref[...]) + matmul_t(dup, u_ref[...])

    @pl.when(pl.program_id(0) == 0)
    def _():
        out_ref[...] = total

    @pl.when(pl.program_id(0) > 0)
    def _():
        out_ref[...] += total


def hidden_chunk(hidden):
    return next(size for size in (512, 384, 256, 128, hidden) if hidden % size == 0)


def ff_forward(normed, base, gate, upward, down):
    tokens, width = normed.shape
    hidden = gate.shape[1]
    chunk = hidden_chunk(hidden)
    whole = lambda j: (0, 0)
    column = lambda j: (0, j)
    saved = jax.ShapeDtypeStruct((tokens, hidden), BF16)
    return pl.pallas_call(
        forward_kernel,
        grid=(hidden // chunk,),
        in_specs=[
            pl.BlockSpec((tokens, width), whole),
            pl.BlockSpec((tokens, width), whole),
            pl.BlockSpec((width, chunk), column),
            pl.BlockSpec((width, chunk), column),
            pl.BlockSpec((chunk, width), lambda j: (j, 0)),
        ],
        out_specs=[pl.BlockSpec((tokens, width), whole)]
        + [pl.BlockSpec((tokens, chunk), column)] * 3,
        out_shape=[jax.ShapeDtypeStruct((tokens, width), F32), saved, saved, saved],
        compiler_params=params(),
        cost_estimate=pl.CostEstimate(
            flops=6 * tokens * width * hidden,
            bytes_accessed=6 * hidden * (width + tokens),
            transcendentals=tokens * hidden,
        ),
    )(normed, base, gate, upward, down)


def ff_backward(grad, one, two, gate, upward, down):
    tokens, width = grad.shape
    hidden = gate.shape[1]
    chunk = hidden_chunk(hidden)
    whole = lambda j: (0, 0)
    column = lambda j: (0, j)
    saved = jax.ShapeDtypeStruct((tokens, hidden), BF16)
    return pl.pallas_call(
        backward_kernel,
        grid=(hidden // chunk,),
        in_specs=[
            pl.BlockSpec((tokens, width), whole),
            pl.BlockSpec((tokens, chunk), column),
            pl.BlockSpec((tokens, chunk), column),
            pl.BlockSpec((width, chunk), column),
            pl.BlockSpec((width, chunk), column),
            pl.BlockSpec((chunk, width), lambda j: (j, 0)),
        ],
        out_specs=[pl.BlockSpec((tokens, width), whole)]
        + [pl.BlockSpec((tokens, chunk), column)] * 2,
        out_shape=[jax.ShapeDtypeStruct((tokens, width), F32), saved, saved],
        compiler_params=params(),
        cost_estimate=pl.CostEstimate(
            flops=6 * tokens * width * hidden,
            bytes_accessed=6 * hidden * (width + tokens),
            transcendentals=0,
        ),
    )(grad, one, two, gate, upward, down)


def local(
    tokens,
    cotangent,
    norm_gains,
    head_gains,
    conv_kernel,
    mix_in,
    mix_out,
    w_gate,
    w_up,
    w_down,
    conv_c,
):
    first = lax.axis_index("section") == 0
    part = lax.axis_index("seq")
    place = lax.axis_index("fsdp")
    fsdp = lax.axis_size("fsdp")
    chips = fsdp // 2
    chip, core = (place // 2, place % 2)
    stretches, rows, width = tokens.shape[1:]
    hidden = w_gate.shape[2]
    total = stretches * rows
    block = 2 * rows
    gains = norm_gains[0]

    cores = [(i, i ^ 1) for i in range(fsdp)]
    swap = [(0, 1), (1, 0)]

    def to_core(value):
        return lax.ppermute(value, "fsdp", cores)

    def to_peer(value):
        return lax.ppermute(value, "seq", swap)

    def along(value, steps):
        return lax.ppermute(value, "fsdp", [(i, (i + 2 * steps) % fsdp) for i in range(fsdp)])

    def gather(shards):
        results, sent = ([], [])
        for number, shard in enumerate(shards):
            depth, columns = shard.shape
            half = depth // 2
            mine = lax.dynamic_slice_in_dim(shard, part * half, half, 0)
            if number >= 1:
                tied = sent[0] if number == 1 else sent[number - 2]
                mine, unused = lax.optimization_barrier((mine, tied))
            arrived = [along(mine, step) for step in range(1, chips)]
            sent.append(arrived)
            crossed = [to_peer(piece) for piece in arrived]
            held = jnp.zeros((chips, 2, half, columns), BF16)
            held = lax.dynamic_update_slice(
                held, shard.reshape(1, 2, half, columns), (chip, 0, 0, 0)
            )
            for step, near, far in zip(range(1, chips), arrived, crossed):
                source = (chip - step) % chips
                held = lax.dynamic_update_slice(held, near[None, None], (source, part, 0, 0))
                held = lax.dynamic_update_slice(held, far[None, None], (source, 1 - part, 0, 0))
            other = to_core(held)
            full = jnp.broadcast_to(held[:, None], (chips, 2, 2, half, columns))
            full = lax.dynamic_update_slice(full, other[:, None], (0, 1 - core, 0, 0, 0))
            results.append(full.reshape(fsdp * depth, columns))
        return results

    def core_columns(value, which, cut):
        wide = value.reshape(value.shape[0], 2, chips, 2, cut)
        return lax.dynamic_index_in_dim(wide, which, 3, keepdims=False).reshape(
            value.shape[0], chips * 2 * cut
        )

    def reduce(left, right):
        cut = left.shape[1] // (2 * fsdp)
        columns = right.shape[1]
        leaving = outer_sum(core_columns(left, 1 - core, cut), right).astype(BF16)
        staying = outer_sum(core_columns(left, core, cut), right)
        both = (staying + to_core(leaving).astype(F32)).astype(BF16)
        both = both.reshape(2, chips, cut, columns)
        crossing = lax.dynamic_index_in_dim(both, 1 - part, 0, keepdims=False)
        own = lax.dynamic_index_in_dim(both, part, 0, keepdims=False)
        own = (own.astype(F32) + to_peer(crossing).astype(F32)).astype(BF16)
        result = lax.dynamic_index_in_dim(own, chip, 0, keepdims=False).astype(F32)
        for step in range(1, chips):
            piece = lax.dynamic_index_in_dim(own, (chip + step) % chips, 0, keepdims=False)
            result = result + along(piece, step).astype(F32)
        return result

    def reduce_small(value):
        value = value + to_core(value)
        value = value + to_peer(value)
        step = 2
        while step < fsdp:
            value = value + lax.ppermute(value, "fsdp", [(i, i ^ step) for i in range(fsdp)])
            step *= 2
        return value

    def zeros(*shape, kind=BF16):
        return jnp.zeros(shape, kind)

    c_low = lax.ppermute(conv_c, "section", [(0, 1)])
    shards = (mix_in[0], mix_out[0], w_gate[0], w_up[0], w_down[0])

    positions = (
        jnp.arange(stretches)[:, None] * block + part * rows + jnp.arange(rows)[None, :]
    ).reshape(total)
    part_ref = part.astype(jnp.int32).reshape(1)

    def rope():
        lane = jnp.arange(PAIR)
        frequency = THETA ** (-(lane % (HEAD // 2)).astype(F32) * 2.0 / HEAD)
        angle = positions.astype(F32)[:, None] * frequency[None, :]
        sign = jnp.where(lane % HEAD < HEAD // 2, -1.0, 1.0)
        return (jnp.cos(angle), jnp.sin(angle) * sign[None, :])

    def gain_rows():
        return jnp.zeros((8, PAIR), F32).at[:2].set(jnp.tile(head_gains, (1, 2)))

    def attention_forward():
        w_in, w_out, gate, upward, down = gather(shards)
        source = tokens[0].reshape(total, width).astype(F32)
        normed = (source * rms_scale(source) * gains[0]).astype(BF16)
        cosine, sine = rope()
        raw, query, own = project(normed, w_in, cosine, sine, gain_rows())
        peer = to_peer(own)
        heads = attend(part_ref, query, own, peer, rows, stretches)
        resid = source + matmul(heads, w_out)
        normed_two = (resid * rms_scale(resid) * gains[1]).astype(BF16)
        result, active, one, two = ff_forward(normed_two, resid, gate, upward, down)
        weights = (w_in, w_out, gate, upward, down, zeros(width, width))
        kept = (normed, raw, query, own, peer, heads, resid, normed_two, active, one, two)
        return (weights, kept, cosine, sine, result.astype(BF16))

    def conv_gather():
        both = jnp.concatenate([c_low, conv_c], axis=1)
        w_in, c_wide, w_out, gate, upward, down = gather((shards[0], both, *shards[1:]))
        w_c = jnp.concatenate([c_wide[:, :width], c_wide[:, width:]], axis=0)
        weights = (w_in, w_out, gate, upward, down, w_c)
        flat = lambda: zeros(total, width)
        wide = lambda: zeros(total, hidden)
        kept = (
            flat(), zeros(total, KV_HEADS * GROUP), flat(), flat(), flat(), flat(),
            zeros(total, width, kind=F32), flat(), wide(), wide(), wide(),
        )
        table = lambda: zeros(total, PAIR, kind=F32)
        return (weights, kept, table(), table(), flat())

    weights, kept, cosine, sine, link = lax.cond(first, attention_forward, conv_gather)
    link = lax.ppermute(link, "section", [(0, 1)])

    def tail_of(value, start):
        return to_peer(value.reshape(stretches, rows, width)[:, start : start + 2])

    def conv_both():
        w_in, w_out, gate, upward, down, w_c = weights
        source = link.astype(F32)
        scale_one = rms_scale(source)
        normed = (source * scale_one * gains[0]).astype(BF16)
        pair = matmul(normed, w_in)
        left, right = (pair[:, :width], pair[:, width:])
        product = (left * right).astype(BF16)
        tails = tail_of(product, rows - 2).astype(F32)
        conv_gate = matmul(normed, w_c).astype(BF16).astype(F32)
        early = jnp.concatenate([jnp.zeros_like(tails[:1]), tails[:-1]], axis=0)
        before = jnp.where(part == 0, early, tails)
        inner = product.astype(F32).reshape(stretches, rows, width)
        longer = jnp.concatenate([before, inner], axis=1)
        taps = [longer[:, i : i + rows] for i in range(3)]
        state = sum(conv_kernel[i] * taps[i] for i in range(3)).reshape(total, width)
        heads = (conv_gate * state).astype(BF16)
        resid = source + matmul(heads, w_out)
        scale_two = rms_scale(resid)
        normed_two = (resid * scale_two * gains[1]).astype(BF16)
        result, active, one, two = ff_forward(normed_two, resid, gate, upward, down)

        grad_ff = cotangent[0].reshape(total, width)
        grad_two, dgate, dup = ff_backward(grad_ff, one, two, gate, upward, down)
        gain_two = jnp.sum(grad_two * resid * scale_two, axis=0)
        grad_resid = grad_ff.astype(F32) + norm_back(grad_two, resid, scale_two, gains[1])
        dmix = grad_resid.astype(BF16)
        dheads = matmul_t(dmix, w_out).astype(BF16).astype(F32)
        dgate_c = (dheads * state).astype(BF16)
        dstate = (dheads * conv_gate).reshape(stretches, rows, width)
        fronts = tail_of(dstate, 0)
        late = jnp.concatenate([fronts[1:], jnp.zeros_like(fronts[:1])], axis=0)
        after = jnp.where(part == 0, fronts, late)
        further = jnp.concatenate([dstate, after], axis=1)
        dproduct = sum(conv_kernel[2 - i] * further[:, i : i + rows] for i in range(3))
        dproduct = dproduct.reshape(total, width).astype(BF16).astype(F32)
        kernel_grad = jnp.stack([jnp.sum(dstate * taps[i], axis=(0, 1)) for i in range(3)])
        dproj = jnp.concatenate([dproduct * right, dproduct * left], axis=1).astype(BF16)
        grad_one = matmul_t(dproj, w_in) + matmul_t(dgate_c, w_c)
        gain_one = jnp.sum(grad_one * source * scale_one, axis=0)
        grad_source = grad_resid + norm_back(grad_one, source, scale_one, gains[0])
        small = jnp.concatenate(
            [gain_one[None], gain_two[None], kernel_grad, jnp.zeros((3, width), F32)], axis=0
        )
        moved = (normed, dproj, dgate_c, heads, dmix, normed_two, dgate, dup, active)
        return (result, moved, small, grad_source.astype(BF16))

    def attention_idle():
        flat = lambda: zeros(total, width)
        wide = lambda: zeros(total, hidden)
        moved = (
            flat(), zeros(total, 2 * width), flat(), flat(), flat(), flat(), wide(), wide(), wide(),
        )
        return (zeros(total, width, kind=F32), moved, zeros(8, width, kind=F32), flat())

    outputs, moved, conv_small, grad_link = lax.cond(first, attention_idle, conv_both)
    grad_link = lax.ppermute(grad_link, "section", [(1, 0)])

    def attention_back():
        w_in, w_out, gate, upward, down, unused = weights
        normed, raw, query, own, peer, heads, resid, normed_two, active, one, two = kept
        shard_down = reduce(active, grad_link)
        grad_two, dgate, dup = ff_backward(grad_link, one, two, gate, upward, down)
        shard_gate = reduce(normed_two, dgate)
        shard_up = reduce(normed_two, dup)
        scale_two = rms_scale(resid)
        gain_two = jnp.sum(grad_two * resid * scale_two, axis=0)
        grad_resid = grad_link.astype(F32) + norm_back(grad_two, resid, scale_two, gains[1])
        dmix = grad_resid.astype(BF16)
        shard_out = reduce(heads, dmix)
        dheads = matmul_t(dmix, w_out).astype(BF16)
        dquery, down_kv, peer_kv = attend_back(part_ref, query, own, peer, dheads, rows, stretches)
        recv = to_peer(peer_kv.astype(BF16))
        dproj, grad_one, head_rows = project_back(
            raw, dquery, down_kv, recv, cosine, sine, gain_rows(), w_in
        )
        shard_in = reduce(normed, dproj)
        source = tokens[0].reshape(total, width).astype(F32)
        scale_one = rms_scale(source)
        gain_one = jnp.sum(grad_one * source * scale_one, axis=0)
        grad_source = grad_resid + norm_back(grad_one, source, scale_one, gains[0])
        head_grad = jnp.stack([head_rows[0, :HEAD] + head_rows[0, HEAD:], head_rows[1, :HEAD]])
        head_row = jnp.pad(head_grad.reshape(1, PAIR), ((0, 0), (0, width - PAIR)))
        small = jnp.concatenate(
            [gain_one[None], gain_two[None], jnp.zeros((3, width), F32), head_row,
             jnp.zeros((2, width), F32)], axis=0
        )
        small = reduce_small(small)
        shards = (shard_in, shard_out, shard_gate, shard_up, shard_down)
        return (grad_source, shards, zeros(2 * conv_cut, width, kind=F32), small)

    conv_cut = width // (4 * fsdp)

    def conv_weights():
        normed, dproj, dgate_c, heads, dmix, normed_two, dgate, dup, active = moved
        grad_ff = cotangent[0].reshape(total, width)
        shard_down = reduce(active, grad_ff)
        shard_gate = reduce(normed_two, dgate)
        shard_up = reduce(normed_two, dup)
        shard_out = reduce(heads, dmix)
        shard_in = reduce(normed, dproj)
        turned = normed.reshape(total, 2, 2 * fsdp, conv_cut)
        turned = jnp.transpose(turned, (0, 2, 1, 3)).reshape(total, width)
        shard_c = reduce(turned, dgate_c)
        small = reduce_small(conv_small)
        shards = (shard_in, shard_out, shard_gate, shard_up, shard_down)
        return (outputs, shards, shard_c, small)

    ends, shards_out, shard_c, small = lax.cond(first, attention_back, conv_weights)
    mail = lax.ppermute(
        jnp.concatenate([shard_c, small], axis=0), "section", swap
    )
    c_shard = jnp.where(first, mail[:conv_cut], shard_c[conv_cut:])
    theirs = mail[2 * conv_cut :]
    merged_a, merged_c = (jnp.where(first, small, theirs), jnp.where(first, theirs, small))
    grad_norm = jnp.stack([merged_a[:2], merged_c[:2]])
    grad_head = merged_a[5, :PAIR].reshape(2, HEAD)
    return (
        ends.reshape(1, 1, stretches, rows, width),
        grad_norm,
        grad_head,
        merged_c[2:5],
        *[shard[None] for shard in shards_out],
        c_shard,
    )


def solution(mesh):
    return jax.shard_map(
        local,
        mesh=mesh,
        in_specs=(
            P("fsdp", None, "seq", None),
            P("fsdp", None, "seq", None),
            P("section", None, None),
            P(),
            P(),
            P("section", "fsdp", None),
            P("section", "fsdp", None),
            P("section", "fsdp", None),
            P("section", "fsdp", None),
            P("section", "fsdp", None),
            P(("section", "fsdp"), None),
        ),
        out_specs=(
            P("section", "fsdp", None, "seq", None),
            P(),
            P(),
            P(),
            P("section", ("seq", "fsdp"), None),
            P("section", ("seq", "fsdp"), None),
            P("section", ("seq", "fsdp"), None),
            P("section", ("seq", "fsdp"), None),
            P("section", ("seq", "fsdp"), None),
            P(("section", "seq", "fsdp"), None),
        ),
        check_vma=False,
    )
```

```python
import functools

import jax
import jax.numpy as jnp
from jax import lax
from jax.experimental import pallas as pl
from jax.experimental.pallas import tpu as pltpu
from jax.sharding import PartitionSpec as P

HEADS = 16
KV_HEADS = 8
HEAD = 64
PAIR = 2 * HEAD
GROUP = 2 * PAIR

EPSILON = 1e-05
THETA = 1000000.0
NEGATIVE = -1e30
BF16 = jnp.bfloat16
F32 = jnp.float32
VMEM_LIMIT = 56 * 1024 * 1024


def rms_scale(value):
    return lax.rsqrt(jnp.mean(value * value, axis=-1, keepdims=True) + EPSILON)


def norm_back(grad_out, value, scale, gain):
    inner = grad_out * gain
    return scale * (inner - value * scale * scale * jnp.mean(inner * value, axis=-1, keepdims=True))


def matmul(left, right):
    return jnp.dot(left, right, preferred_element_type=F32)


def matmul_t(left, right):
    return lax.dot_general(left, right, (((1,), (1,)), ((), ())), preferred_element_type=F32)


def outer_sum(left, right):
    return lax.dot_general(left, right, (((0,), (0,)), ((), ())), preferred_element_type=F32)


def params():
    return pltpu.CompilerParams(vmem_limit_bytes=VMEM_LIMIT)


def light():
    return pl.CostEstimate(flops=1 << 20, bytes_accessed=1 << 20, transcendentals=0)


def group_mean(value):
    row = lax.broadcasted_iota(jnp.int32, (PAIR, PAIR), 0) // HEAD
    col = lax.broadcasted_iota(jnp.int32, (PAIR, PAIR), 1) // HEAD
    ones = jnp.where(row == col, 1.0 / HEAD, 0.0).astype(F32)
    return jnp.dot(value, ones, precision=lax.Precision.HIGHEST, preferred_element_type=F32)


def lane_swap(value):
    lane = lax.broadcasted_iota(jnp.int32, value.shape, 1) % HEAD
    return jnp.where(
        lane < HEAD // 2, pltpu.roll(value, PAIR - HEAD // 2, 1), pltpu.roll(value, HEAD // 2, 1)
    )


def project_kernel(x_ref, w_ref, cos_ref, sin_ref, gain_ref, raw_ref, q_ref, kv_ref):
    raw = jnp.dot(x_ref[...], w_ref[...], preferred_element_type=F32).astype(BF16)
    raw_ref[...] = raw
    for part, out in ((0, q_ref), (1, kv_ref)):
        vec = raw[:, part * PAIR : (part + 1) * PAIR].astype(F32)
        normed = vec * lax.rsqrt(group_mean(vec * vec) + EPSILON) * gain_ref[part : part + 1, :]
        turned = normed * cos_ref[...] + lane_swap(normed) * sin_ref[...]
        if part == 1:
            lane = lax.broadcasted_iota(jnp.int32, vec.shape, 1)
            turned = jnp.where(lane < HEAD, turned, vec)
        out[...] = turned.astype(BF16)


def project(normed, weight, cosine, sine, gain_rows):
    tokens, width = normed.shape
    whole = lambda g: (0, 0)
    column = lambda g: (0, g)
    return pl.pallas_call(
        project_kernel,
        grid=(KV_HEADS,),
        in_specs=[
            pl.BlockSpec((tokens, width), whole),
            pl.BlockSpec((width, GROUP), column),
            pl.BlockSpec((tokens, PAIR), whole),
            pl.BlockSpec((tokens, PAIR), whole),
            pl.BlockSpec((8, PAIR), whole),
        ],
        out_specs=[
            pl.BlockSpec((tokens, GROUP), column),
            pl.BlockSpec((tokens, PAIR), column),
            pl.BlockSpec((tokens, PAIR), column),
        ],
        out_shape=[
            jax.ShapeDtypeStruct((tokens, KV_HEADS * GROUP), BF16),
            jax.ShapeDtypeStruct((tokens, KV_HEADS * PAIR), BF16),
            jax.ShapeDtypeStruct((tokens, KV_HEADS * PAIR), BF16),
        ],
        compiler_params=params(),
        cost_estimate=light(),
    )(normed, weight, cosine, sine, gain_rows)


def attend_kernel(rows, stretches, part_ref, q_ref, own_ref, peer_ref, out_ref):
    second = part_ref[0] == 1
    for stretch in range(stretches):
        blocks = []
        for s in range(stretch + 1):
            blocks += [own_ref[s * rows : (s + 1) * rows, :], peer_ref[s * rows : (s + 1) * rows, :]]
        pack = jnp.concatenate(blocks, axis=0)
        keys, values = (pack[:, :HEAD], pack[:, HEAD:])
        count = pack.shape[0]
        row = lax.broadcasted_iota(jnp.int32, (rows, count), 0)
        col = lax.broadcasted_iota(jnp.int32, (rows, count), 1) - stretch * 2 * rows
        allowed = (col <= row) | ((col >= rows) & second)
        for j in range(2):
            query = q_ref[stretch * rows : (stretch + 1) * rows, j * HEAD : (j + 1) * HEAD]
            scores = matmul_t(query, keys) * HEAD ** (-0.5)
            scores = jnp.where(allowed, scores, NEGATIVE)
            exponent = jnp.exp(scores - jnp.max(scores, axis=1, keepdims=True))
            total = jnp.sum(exponent, axis=1, keepdims=True)
            probs = (exponent * (1.0 / total)).astype(BF16)
            out_ref[stretch * rows : (stretch + 1) * rows, j * HEAD : (j + 1) * HEAD] = jnp.dot(
                probs, values, preferred_element_type=F32
            ).astype(BF16)


def attend(part, query, own, peer, rows, stretches):
    tokens = query.shape[0]
    column = lambda g: (0, g)
    return pl.pallas_call(
        functools.partial(attend_kernel, rows, stretches),
        grid=(KV_HEADS,),
        in_specs=[pl.BlockSpec(memory_space=pltpu.SMEM)]
        + [pl.BlockSpec((tokens, PAIR), column)] * 3,
        out_specs=pl.BlockSpec((tokens, PAIR), column),
        out_shape=jax.ShapeDtypeStruct((tokens, KV_HEADS * PAIR), BF16),
        compiler_params=params(),
        cost_estimate=light(),
    )(part, query, own, peer)


def attend_back_kernel(
    rows, stretches, part_ref, q_ref, own_ref, peer_ref, grad_ref, dq_ref, down_ref, dpeer_ref
):
    second = part_ref[0] == 1
    for stretch in reversed(range(stretches)):
        blocks = []
        for s in range(stretch + 1):
            blocks += [own_ref[s * rows : (s + 1) * rows, :], peer_ref[s * rows : (s + 1) * rows, :]]
        pack = jnp.concatenate(blocks, axis=0)
        keys, values = (pack[:, :HEAD], pack[:, HEAD:])
        count = pack.shape[0]
        col = lax.broadcasted_iota(jnp.int32, (count, rows), 0) - stretch * 2 * rows
        row = lax.broadcasted_iota(jnp.int32, (count, rows), 1)
        allowed = (col <= row) | ((col >= rows) & second)
        span = slice(stretch * rows, (stretch + 1) * rows)
        dkeys, dvalues, dquery = (0.0, 0.0, [])
        for j in range(2):
            query = q_ref[span, j * HEAD : (j + 1) * HEAD]
            grad = grad_ref[span, j * HEAD : (j + 1) * HEAD]
            scores = matmul_t(keys, query) * HEAD ** (-0.5)
            scores = jnp.where(allowed, scores, NEGATIVE)
            exponent = jnp.exp(scores - jnp.max(scores, axis=0, keepdims=True))
            probs = exponent * (1.0 / jnp.sum(exponent, axis=0, keepdims=True))
            dprobs = matmul_t(values, grad)
            dscores = probs * (dprobs - jnp.sum(probs * dprobs, axis=0, keepdims=True))
            dscores = dscores.astype(BF16)
            dvalues += jnp.dot(probs.astype(BF16), grad, preferred_element_type=F32)
            dkeys += jnp.dot(dscores, query, preferred_element_type=F32) * HEAD ** (-0.5)
            dquery.append(outer_sum(dscores, keys) * HEAD ** (-0.5))
        dq_ref[span, :] = jnp.concatenate(dquery, axis=1)
        both = jnp.concatenate([dkeys, dvalues], axis=1)
        for s in range(stretch + 1):
            for place, out in ((2 * s, down_ref), (2 * s + 1, dpeer_ref)):
                piece = both[place * rows : (place + 1) * rows]
                span_s = slice(s * rows, (s + 1) * rows)
                if stretch == stretches - 1:
                    out[span_s, :] = piece
                else:
                    out[span_s, :] += piece


def attend_back(part, query, own, peer, grad, rows, stretches):
    tokens = query.shape[0]
    column = lambda g: (0, g)
    shape = jax.ShapeDtypeStruct((tokens, KV_HEADS * PAIR), F32)
    return pl.pallas_call(
        functools.partial(attend_back_kernel, rows, stretches),
        grid=(KV_HEADS,),
        in_specs=[pl.BlockSpec(memory_space=pltpu.SMEM)]
        + [pl.BlockSpec((tokens, PAIR), column)] * 4,
        out_specs=[pl.BlockSpec((tokens, PAIR), column)] * 3,
        out_shape=[shape] * 3,
        compiler_params=params(),
        cost_estimate=light(),
    )(part, query, own, peer, grad)


def project_back_kernel(
    raw_ref, dq_ref, own_ref, recv_ref, cos_ref, sin_ref, gain_ref, w_ref, pack_ref, normed_ref, head_ref
):
    first = pl.program_id(0) == 0
    grads = []
    for part in range(2):
        vec = raw_ref[:, part * PAIR : (part + 1) * PAIR].astype(F32)
        if part == 0:
            grad = dq_ref[...]
        else:
            grad = own_ref[...] + recv_ref[...].astype(F32)
        gain = gain_ref[part : part + 1, :]
        scale = lax.rsqrt(group_mean(vec * vec) + EPSILON)
        turned = grad * cos_ref[...] - lane_swap(grad) * sin_ref[...]
        gain_sum = jnp.sum(turned * vec * scale, axis=0, keepdims=True)
        inner = turned * gain
        back = scale * (inner - vec * scale * scale * group_mean(inner * vec))
        if part == 1:
            lane = lax.broadcasted_iota(jnp.int32, vec.shape, 1)
            back = jnp.where(lane < HEAD, back, grad)
        back = back.astype(BF16)
        pack_ref[:, part * PAIR : (part + 1) * PAIR] = back
        grads.append((back, gain_sum))
    total = matmul_t(grads[0][0], w_ref[:, :PAIR]) + matmul_t(grads[1][0], w_ref[:, PAIR:])

    @pl.when(first)
    def _():
        normed_ref[...] = total
        head_ref[...] = jnp.zeros_like(head_ref)

    @pl.when(jnp.logical_not(first))
    def _():
        normed_ref[...] += total

    for part in range(2):
        head_ref[part : part + 1, :] += grads[part][1]


def project_back(raw, dquery, own, recv, cosine, sine, gain_rows, weight):
    tokens = raw.shape[0]
    width = weight.shape[0]
    whole = lambda g: (0, 0)
    column = lambda g: (0, g)
    return pl.pallas_call(
        project_back_kernel,
        grid=(KV_HEADS,),
        in_specs=[
            pl.BlockSpec((tokens, GROUP), column),
            pl.BlockSpec((tokens, PAIR), column),
            pl.BlockSpec((tokens, PAIR), column),
            pl.BlockSpec((tokens, PAIR), column),
            pl.BlockSpec((tokens, PAIR), whole),
            pl.BlockSpec((tokens, PAIR), whole),
            pl.BlockSpec((8, PAIR), whole),
            pl.BlockSpec((width, GROUP), column),
        ],
        out_specs=[
            pl.BlockSpec((tokens, GROUP), column),
            pl.BlockSpec((tokens, width), whole),
            pl.BlockSpec((8, PAIR), whole),
        ],
        out_shape=[
            jax.ShapeDtypeStruct((tokens, KV_HEADS * GROUP), BF16),
            jax.ShapeDtypeStruct((tokens, width), F32),
            jax.ShapeDtypeStruct((8, PAIR), F32),
        ],
        compiler_params=params(),
        cost_estimate=light(),
    )(raw, dquery, own, recv, cosine, sine, gain_rows, weight)


def flat(ref):
    value = ref[...]
    return value.reshape(-1, value.shape[-1])


def forward_kernel(x_ref, base_ref, g_ref, u_ref, d_ref, out_ref, act_ref, one_ref, two_ref):
    gate_part, up_part, down_part = (flat(g_ref), flat(u_ref), flat(d_ref))
    down = 0.0
    for span in spans(act_ref.shape[1]):
        gate = jnp.dot(x_ref[...], gate_part[:, span], preferred_element_type=F32)
        upward = jnp.dot(x_ref[...], up_part[:, span], preferred_element_type=F32)
        sigma = jax.nn.sigmoid(gate)
        silu = gate * sigma
        active = (silu * upward).astype(BF16)
        act_ref[:, span] = active
        one_ref[:, span] = (upward * sigma * (1.0 + gate * (1.0 - sigma))).astype(BF16)
        two_ref[:, span] = silu.astype(BF16)
        down += jnp.dot(active, down_part[span], preferred_element_type=F32)

    @pl.when(pl.program_id(0) == 0)
    def _():
        out_ref[...] = base_ref[...] + down

    @pl.when(pl.program_id(0) > 0)
    def _():
        out_ref[...] += down


def backward_kernel(grad_ref, one_ref, two_ref, g_ref, u_ref, d_ref, out_ref, dg_ref, du_ref):
    gate_part, up_part, down_part = (flat(g_ref), flat(u_ref), flat(d_ref))
    total = 0.0
    for span in spans(dg_ref.shape[1]):
        active = matmul_t(grad_ref[...], down_part[span])
        dgate = (active * one_ref[:, span].astype(F32)).astype(BF16)
        dup = (active * two_ref[:, span].astype(F32)).astype(BF16)
        dg_ref[:, span] = dgate
        du_ref[:, span] = dup
        total += matmul_t(dgate, gate_part[:, span]) + matmul_t(dup, up_part[:, span])

    @pl.when(pl.program_id(0) == 0)
    def _():
        out_ref[...] = total

    @pl.when(pl.program_id(0) > 0)
    def _():
        out_ref[...] += total


def store_outer(left_ref, dgate, dup, span, outs):
    half = left_ref.shape[0] // 2
    for right, leave_ref, stay_ref in ((dgate, *outs[:2]), (dup, *outs[2:])):
        product = jnp.dot(left_ref[...], right, preferred_element_type=F32).astype(BF16)
        leave_ref[:, span] = product[:half]
        stay_ref[:, span] = product[half:]


def backward_outer_kernel(grad_ref, left_ref, one_ref, two_ref, g_ref, u_ref, d_ref, out_ref, *outs):
    gate_part, up_part, down_part = (flat(g_ref), flat(u_ref), flat(d_ref))
    total = 0.0
    for span in spans(one_ref.shape[1]):
        active = matmul_t(grad_ref[...], down_part[span])
        dgate = (active * one_ref[:, span].astype(F32)).astype(BF16)
        dup = (active * two_ref[:, span].astype(F32)).astype(BF16)
        store_outer(left_ref, dgate, dup, span, outs)
        total += matmul_t(dgate, gate_part[:, span]) + matmul_t(dup, up_part[:, span])

    @pl.when(pl.program_id(0) == 0)
    def _():
        out_ref[...] = total

    @pl.when(pl.program_id(0) > 0)
    def _():
        out_ref[...] += total


def outer_kernel(left_ref, dg_ref, du_ref, *outs):
    store_outer(left_ref, dg_ref[...], du_ref[...], slice(None), outs)


def spans(chunk):
    starts = list(range(0, max(chunk - 511, 1), 512))
    return [slice(a, b) for a, b in zip(starts, starts[1:] + [chunk])]


def sub_chunk(chunk):
    return next(size for size in (512, 384, 256, 128, chunk) if chunk % size == 0)


CHUNKS = 4


def can_pack(devices, width, hidden):
    gate_rows, down_rows = (width // devices, hidden // devices)
    return (
        devices % CHUNKS == 0
        and hidden % (CHUNKS * 128) == 0
        and hidden // CHUNKS >= width
        and gate_rows % 16 == 0
        and down_rows % 16 == 0
    )


def pack_halves(gate, upward, down):
    rows, hidden = gate.shape
    chunk = hidden // CHUNKS
    down = jnp.pad(down, ((0, -down.shape[0] % rows), (0, chunk - down.shape[1])))
    cut = lambda w: jnp.transpose(w.reshape(rows, CHUNKS, chunk), (1, 0, 2)).reshape(-1, chunk)
    return jnp.concatenate([down, cut(gate), cut(upward)], axis=0)


def weight_specs(weights, tokens, width, hidden):
    if len(weights) == 3:
        chunk = sub_chunk(hidden)
        column = lambda j: (0, j)
        return (
            chunk,
            [
                pl.BlockSpec((width, chunk), column),
                pl.BlockSpec((width, chunk), column),
                pl.BlockSpec((chunk, width), lambda j: (j, 0)),
            ],
            weights,
        )
    devices = weights[0].shape[0]
    rows, down_rows, chunk = (width // devices, hidden // devices, hidden // CHUNKS)
    skip = -(-down_rows // rows)
    return (
        chunk,
        [
            pl.BlockSpec((devices, rows, chunk), lambda j: (0, skip + j, 0)),
            pl.BlockSpec((devices, rows, chunk), lambda j: (0, skip + CHUNKS + j, 0)),
            pl.BlockSpec((devices // CHUNKS, down_rows, width), lambda j: (j, 0, 0)),
        ],
        (weights[0],) * 3,
    )


def ff_forward(normed, base, weights, hidden):
    tokens, width = normed.shape
    chunk, specs, operands = weight_specs(weights, tokens, width, hidden)
    whole = lambda j: (0, 0)
    column = lambda j: (0, j)
    saved = jax.ShapeDtypeStruct((tokens, hidden), BF16)
    return pl.pallas_call(
        forward_kernel,
        grid=(hidden // chunk,),
        in_specs=[pl.BlockSpec((tokens, width), whole), pl.BlockSpec((tokens, width), whole)]
        + specs,
        out_specs=[pl.BlockSpec((tokens, width), whole)]
        + [pl.BlockSpec((tokens, chunk), column)] * 3,
        out_shape=[jax.ShapeDtypeStruct((tokens, width), F32), saved, saved, saved],
        compiler_params=params(),
        cost_estimate=light(),
    )(normed, base, *operands)


def ff_backward(grad, one, two, weights, hidden):
    tokens, width = grad.shape
    chunk, specs, operands = weight_specs(weights, tokens, width, hidden)
    whole = lambda j: (0, 0)
    column = lambda j: (0, j)
    saved = jax.ShapeDtypeStruct((tokens, hidden), BF16)
    return pl.pallas_call(
        backward_kernel,
        grid=(hidden // chunk,),
        in_specs=[
            pl.BlockSpec((tokens, width), whole),
            pl.BlockSpec((tokens, chunk), column),
            pl.BlockSpec((tokens, chunk), column),
        ]
        + specs,
        out_specs=[pl.BlockSpec((tokens, width), whole)]
        + [pl.BlockSpec((tokens, chunk), column)] * 2,
        out_shape=[jax.ShapeDtypeStruct((tokens, width), F32), saved, saved],
        compiler_params=params(),
        cost_estimate=light(),
    )(grad, one, two, *operands)


def ff_backward_outer(grad, left, one, two, weights, hidden):
    tokens, width = grad.shape
    chunk, specs, operands = weight_specs(weights, tokens, width, hidden)
    whole = lambda j: (0, 0)
    column = lambda j: (0, j)
    half = left.shape[0] // 2
    return pl.pallas_call(
        backward_outer_kernel,
        grid=(hidden // chunk,),
        in_specs=[
            pl.BlockSpec((tokens, width), whole),
            pl.BlockSpec(left.shape, whole),
            pl.BlockSpec((tokens, chunk), column),
            pl.BlockSpec((tokens, chunk), column),
        ]
        + specs,
        out_specs=[pl.BlockSpec((tokens, width), whole)]
        + [pl.BlockSpec((half, chunk), column)] * 4,
        out_shape=[jax.ShapeDtypeStruct((tokens, width), F32)]
        + [jax.ShapeDtypeStruct((half, hidden), BF16)] * 4,
        compiler_params=params(),
        cost_estimate=light(),
    )(grad, left, one, two, *operands)


def ff_outer(left, dgate, dup):
    tokens, hidden = dgate.shape
    chunk = sub_chunk(hidden)
    column = lambda j: (0, j)
    half = left.shape[0] // 2
    return pl.pallas_call(
        outer_kernel,
        grid=(hidden // chunk,),
        in_specs=[pl.BlockSpec(left.shape, lambda j: (0, 0))]
        + [pl.BlockSpec((tokens, chunk), column)] * 2,
        out_specs=[pl.BlockSpec((half, chunk), column)] * 4,
        out_shape=[jax.ShapeDtypeStruct((half, hidden), BF16)] * 4,
        compiler_params=params(),
        cost_estimate=light(),
    )(left, dgate, dup)


def local(
    tokens,
    cotangent,
    norm_gains,
    head_gains,
    conv_kernel,
    mix_in,
    mix_out,
    w_gate,
    w_up,
    w_down,
    conv_c,
):
    first = lax.axis_index("section") == 0
    part = lax.axis_index("seq")
    place = lax.axis_index("fsdp")
    fsdp = lax.axis_size("fsdp")
    chips = fsdp // 2
    chip, core = (place // 2, place % 2)
    stretches, rows, width = tokens.shape[1:]
    hidden = w_gate.shape[2]
    total = stretches * rows
    block = 2 * rows
    gains = norm_gains[0]

    cores = [(i, i ^ 1) for i in range(fsdp)]
    swap = [(0, 1), (1, 0)]

    def after(value, *earlier):
        return lax.optimization_barrier((value, *earlier))[0] if earlier else value

    def to_core(value):
        return lax.ppermute(value, "fsdp", cores)

    def to_peer(value):
        return lax.ppermute(value, "seq", swap)

    def along(value, steps):
        return lax.ppermute(value, "fsdp", [(i, (i + 2 * steps) % fsdp) for i in range(fsdp)])

    def gather(shards):
        results, sent = ([], [])
        for number, shard in enumerate(shards):
            depth, columns = shard.shape
            half = depth // 2
            mine = lax.dynamic_slice_in_dim(shard, part * half, half, 0)
            if number >= 1:
                tied = sent[0] if number == 1 else sent[number - 2]
                mine, unused = lax.optimization_barrier((mine, tied))
            arrived = [along(mine, step) for step in range(1, chips)]
            sent.append(arrived)
            crossed = [to_peer(piece) for piece in arrived]
            held = jnp.zeros((chips, 2, half, columns), BF16)
            held = lax.dynamic_update_slice(
                held, shard.reshape(1, 2, half, columns), (chip, 0, 0, 0)
            )
            for step, near, far in zip(range(1, chips), arrived, crossed):
                source = (chip - step) % chips
                held = lax.dynamic_update_slice(held, near[None, None], (source, part, 0, 0))
                held = lax.dynamic_update_slice(held, far[None, None], (source, 1 - part, 0, 0))
            other = to_core(held)
            full = jnp.broadcast_to(held[:, None], (chips, 2, 2, half, columns))
            full = lax.dynamic_update_slice(full, other[:, None], (0, 1 - core, 0, 0, 0))
            results.append(full.reshape(fsdp * depth, columns))
        return results

    def turned(value):
        cut = value.shape[1] // (2 * fsdp)
        wide = value.reshape(value.shape[0], 2, chips, 2, cut)
        sides = [
            lax.dynamic_index_in_dim(wide, side, 3, keepdims=False) for side in (1 - core, core)
        ]
        return jnp.concatenate(
            [jnp.transpose(side.reshape(-1, 2 * chips * cut)) for side in sides], axis=0
        )

    def blocks(both):
        return both.astype(BF16).reshape(2, chips, -1, both.shape[1])

    def core_sum(left, right):
        half = left.shape[0] // 2
        leaving = matmul(left[:half], right).astype(BF16)
        return blocks(matmul(left[half:], right) + to_core(leaving).astype(F32))

    def core_add(leaving, staying):
        return blocks(staying.astype(F32) + leaving.astype(F32))

    def only(section, value, move):
        pairs = []
        for side in range(2):
            for i in range(fsdp):
                source = (section * 2 + side) * fsdp + i
                if move == "seq":
                    target = (section * 2 + 1 - side) * fsdp + i
                elif move == "core":
                    target = (section * 2 + side) * fsdp + (i ^ 1)
                else:
                    target = (section * 2 + side) * fsdp + (i + 2 * move) % fsdp
                pairs.append((source, target))
        return lax.ppermute(value, ("section", "seq", "fsdp"), pairs)

    def sides(both):
        return [
            lax.dynamic_index_in_dim(both, side, 0, keepdims=False) for side in (1 - part, part)
        ]

    def crossed(staying, came):
        return (staying.astype(F32) + came.astype(F32)).astype(BF16)

    def pieces(own):
        return [
            lax.dynamic_index_in_dim(own, (chip + step) % chips, 0, keepdims=False)
            for step in range(chips)
        ]

    def fence(*groups):
        return lax.optimization_barrier(groups)

    def together(values, *others):
        return lax.optimization_barrier((*values, *others))[: len(values)]

    def reduce_small(value):
        value = value + to_core(value)
        value = value + to_peer(value)
        step = 2
        while step < fsdp:
            value = value + lax.ppermute(value, "fsdp", [(i, i ^ step) for i in range(fsdp)])
            step *= 2
        return value

    def zeros(*shape, kind=BF16):
        return jnp.zeros(shape, kind)

    conv_cut = width // (4 * fsdp)
    c_low = lax.ppermute(conv_c, "section", [(0, 1)])

    def half_of(shard):
        return lax.dynamic_slice_in_dim(shard, part * (shard.shape[0] // 2), shard.shape[0] // 2, 0)

    halves = (half_of(w_gate[0]), half_of(w_up[0]), half_of(w_down[0]))
    if can_pack(2 * fsdp, width, hidden):
        wide_weights = (lax.all_gather(pack_halves(*halves), ("fsdp", "seq"), axis=0),)
    else:
        wide_weights = tuple(
            lax.all_gather(half, ("fsdp", "seq"), axis=0, tiled=True) for half in halves
        )

    positions = (
        jnp.arange(stretches)[:, None] * block + part * rows + jnp.arange(rows)[None, :]
    ).reshape(total)
    part_ref = part.astype(jnp.int32).reshape(1)

    def rope():
        lane = jnp.arange(PAIR)
        frequency = THETA ** (-(lane % (HEAD // 2)).astype(F32) * 2.0 / HEAD)
        angle = positions.astype(F32)[:, None] * frequency[None, :]
        sign = jnp.where(lane % HEAD < HEAD // 2, -1.0, 1.0)
        return (jnp.cos(angle), jnp.sin(angle) * sign[None, :])

    def gain_rows():
        return jnp.zeros((8, PAIR), F32).at[:2].set(jnp.tile(head_gains, (1, 2)))

    def attention_mixer():
        w_in, w_out = gather((mix_in[0], mix_out[0]))
        source = tokens[0].reshape(total, width).astype(F32)
        normed = (source * rms_scale(source) * gains[0]).astype(BF16)
        cosine, sine = rope()
        raw, query, own = project(normed, w_in, cosine, sine, gain_rows())
        peer = to_peer(own)
        heads = attend(part_ref, query, own, peer, rows, stretches)
        resid = source + matmul(heads, w_out)
        normed_two = (resid * rms_scale(resid) * gains[1]).astype(BF16)
        weights = (w_in, w_out, zeros(width, width))
        kept = (normed, raw, query, own, peer, heads, resid, normed_two)
        return (weights, kept, cosine, sine)

    def conv_gather():
        both = jnp.concatenate([c_low, conv_c], axis=1)
        w_in, c_wide, w_out = gather((mix_in[0], both, mix_out[0]))
        w_c = jnp.concatenate([c_wide[:, :width], c_wide[:, width:]], axis=0)
        flat = lambda: zeros(total, width)
        kept = (
            flat(), zeros(total, KV_HEADS * GROUP), flat(), flat(), flat(), flat(),
            zeros(total, width, kind=F32), flat(),
        )
        table = lambda: zeros(total, PAIR, kind=F32)
        return ((w_in, w_out, w_c), kept, table(), table())

    weights, kept, cosine, sine = lax.cond(first, attention_mixer, conv_gather)

    def attention_hidden():
        result, *saved = ff_forward(kept[-1], kept[-2], wide_weights, hidden)
        return (result.astype(BF16), *saved)

    def conv_wait():
        return (zeros(total, width), *[zeros(total, hidden) for _ in range(3)])

    link, active, one, two = lax.cond(first, attention_hidden, conv_wait)
    link = lax.ppermute(link, "section", [(0, 1)])

    def tail_of(value, start):
        return to_peer(value.reshape(stretches, rows, width)[:, start : start + 2])

    def conv_both():
        w_in, w_out, w_c = weights
        source = link.astype(F32)
        scale_one = rms_scale(source)
        normed = (source * scale_one * gains[0]).astype(BF16)
        pair = matmul(normed, w_in)
        left, right = (pair[:, :width], pair[:, width:])
        product = (left * right).astype(BF16)
        tails = tail_of(product, rows - 2).astype(F32)
        conv_gate = matmul(normed, w_c).astype(BF16).astype(F32)
        early = jnp.concatenate([jnp.zeros_like(tails[:1]), tails[:-1]], axis=0)
        before = jnp.where(part == 0, early, tails)
        inner = product.astype(F32).reshape(stretches, rows, width)
        longer = jnp.concatenate([before, inner], axis=1)
        taps = [longer[:, i : i + rows] for i in range(3)]
        state = sum(conv_kernel[i] * taps[i] for i in range(3)).reshape(total, width)
        heads = (conv_gate * state).astype(BF16)
        resid = source + matmul(heads, w_out)
        scale_two = rms_scale(resid)
        normed_two = (resid * scale_two * gains[1]).astype(BF16)
        result, active, one, two = ff_forward(normed_two, resid, wide_weights, hidden)

        grad_ff = cotangent[0].reshape(total, width)
        grad_two, dgate, dup = ff_backward(grad_ff, one, two, wide_weights, hidden)
        gain_two = jnp.sum(grad_two * resid * scale_two, axis=0)
        grad_resid = grad_ff.astype(F32) + norm_back(grad_two, resid, scale_two, gains[1])
        dmix = grad_resid.astype(BF16)
        dheads = matmul_t(dmix, w_out).astype(BF16).astype(F32)
        dgate_c = (dheads * state).astype(BF16)
        dstate = (dheads * conv_gate).reshape(stretches, rows, width)
        fronts = tail_of(dstate, 0)
        late = jnp.concatenate([fronts[1:], jnp.zeros_like(fronts[:1])], axis=0)
        after = jnp.where(part == 0, fronts, late)
        further = jnp.concatenate([dstate, after], axis=1)
        dproduct = sum(conv_kernel[2 - i] * further[:, i : i + rows] for i in range(3))
        dproduct = dproduct.reshape(total, width).astype(BF16).astype(F32)
        kernel_grad = jnp.stack([jnp.sum(dstate * taps[i], axis=(0, 1)) for i in range(3)])
        dproj = jnp.concatenate([dproduct * right, dproduct * left], axis=1).astype(BF16)
        grad_one = matmul_t(dproj, w_in) + matmul_t(dgate_c, w_c)
        gain_one = jnp.sum(grad_one * source * scale_one, axis=0)
        grad_source = grad_resid + norm_back(grad_one, source, scale_one, gains[0])
        small = jnp.concatenate(
            [gain_one[None], gain_two[None], kernel_grad, jnp.zeros((3, width), F32)], axis=0
        )
        lefts = (normed, heads, normed_two, active)
        moved = (dproj, dgate_c, dmix, dgate, dup)
        return (result, lefts, moved, small, grad_source.astype(BF16))

    def attention_idle():
        flat = lambda: zeros(total, width)
        wide = lambda: zeros(total, hidden)
        lefts = (kept[0], kept[5], kept[7], active)
        moved = (zeros(total, 2 * width), flat(), flat(), wide(), wide())
        return (zeros(total, width, kind=F32), lefts, moved, zeros(8, width, kind=F32), flat())

    outputs, lefts, moved, conv_small, grad_link = lax.cond(first, attention_idle, conv_both)
    normed, heads, normed_two, active_both = together(lefts, grad_link)
    grad_link = lax.ppermute(grad_link, "section", [(1, 0)])
    conv_dproj, dgate_c, conv_dmix, conv_dgate, conv_dup = moved
    left_down, left_two, left_heads, left_normed = [
        turned(value) for value in (active_both, normed_two, heads, normed)
    ]
    grad_ff = jnp.where(first, grad_link, cotangent[0].reshape(total, width))
    down = sides(core_sum(left_down, grad_ff))
    groups = [[i for i in range(fsdp) if i % 2 == side] for side in range(2)]

    def cross(half):
        return to_peer(half[0])

    def along_all(own):
        return lax.all_to_all(own, "fsdp", 0, 0, axis_index_groups=groups, tiled=True)

    def scattered(came):
        return jnp.sum(came.astype(F32), axis=0)

    def halves_of(leaving, staying):
        return sides(core_add(to_core(leaving), staying))

    def attention_ff():
        grad_two, *products = ff_backward_outer(grad_ff, left_two, one, two, wide_weights, hidden)
        return (grad_two, halves_of(*products[:2]), *products[2:])

    def conv_ff():
        products = ff_outer(left_two, conv_dgate, conv_dup)
        return (zeros(total, width, kind=F32), halves_of(*products[:2]), *products[2:])

    step, down = fence(first, down)
    down_came = cross(down)
    result = lax.cond(step, attention_ff, conv_ff)
    down_came, (grad_two, gate, up_leaving, up_staying) = fence(down_came, result)

    def attention_core():
        unused, raw, query, own, peer, unused, resid, unused = kept
        scale_two = rms_scale(resid)
        gain_two = jnp.sum(grad_two * resid * scale_two, axis=0)
        grad_resid = grad_link.astype(F32) + norm_back(grad_two, resid, scale_two, gains[1])
        dmix = grad_resid.astype(BF16)
        dheads = matmul_t(dmix, weights[1]).astype(BF16)
        up = halves_of(up_leaving, up_staying)
        grads = attend_back(part_ref, query, own, peer, dheads, rows, stretches)
        blank = zeros(chips, 2 * conv_cut, width)
        return (
            up, gain_two, grad_resid, dmix, *grads[:2], grads[2].astype(BF16), [blank, blank],
        )

    def conv_core():
        mixed = normed.reshape(total, 2, 2 * fsdp, conv_cut)
        mixed = jnp.transpose(mixed, (0, 2, 1, 3)).reshape(total, width)
        lone = sides(core_sum(turned(mixed), dgate_c))
        flat = lambda: zeros(total, width, kind=F32)
        up = halves_of(up_leaving, up_staying)
        return (
            up, zeros(width, kind=F32), flat(), conv_dmix, flat(), flat(), zeros(total, width), lone,
        )

    down = crossed(down[1], down_came)
    step, down, gate = fence(first, down, gate)
    down_came, gate_came = (along_all(down), cross(gate))
    result = lax.cond(step, attention_core, conv_core)
    down_came, gate_came, result = fence(down_came, gate_came, result)
    up, gain_two, grad_resid, dmix, dquery, down_kv, peer_kv, lone = result

    def joined(*halves):
        return [jnp.concatenate(parts, axis=2) for parts in zip(*halves)]

    def attention_project():
        dproj, grad_one, head_rows = project_back(
            kept[1], dquery, down_kv, recv, cosine, sine, gain_rows(), weights[0]
        )
        inward = sides(core_sum(left_normed, dproj))
        return (joined(inward, outward), grad_one, head_rows)

    def conv_project():
        inward = sides(core_sum(left_normed, conv_dproj))
        return (joined(inward, outward), zeros(total, width, kind=F32), zeros(8, PAIR, kind=F32))

    gate = crossed(gate[1], gate_came)
    gate, up, lone, peer_kv = fence(gate, up, lone, peer_kv)
    recv = only(0, peer_kv, "seq")
    outward = sides(core_sum(left_heads, dmix))
    gate_came = along_all(gate)
    step, up, lone, recv, outward = fence(first, up, lone, recv, outward)
    up_came = cross(up)
    lone_came = only(1, lone[0], "seq")
    result = lax.cond(step, attention_project, conv_project)
    gate_came, up_came, lone_came, result = fence(gate_came, up_came, lone_came, result)
    mix, grad_one, head_rows = result

    def attention_ends():
        source = tokens[0].reshape(total, width).astype(F32)
        scale_one = rms_scale(source)
        gain_one = jnp.sum(grad_one * source * scale_one, axis=0)
        grad_source = grad_resid + norm_back(grad_one, source, scale_one, gains[0])
        head_grad = jnp.stack([head_rows[0, :HEAD] + head_rows[0, HEAD:], head_rows[1, :HEAD]])
        head_row = jnp.pad(head_grad.reshape(1, PAIR), ((0, 0), (0, width - PAIR)))
        small = jnp.concatenate(
            [gain_one[None], gain_two[None], jnp.zeros((3, width), F32), head_row,
             jnp.zeros((2, width), F32)], axis=0
        )
        return (grad_source, reduce_small(small))

    def conv_ends():
        return (outputs, reduce_small(conv_small))

    up = crossed(up[1], up_came)
    lone = pieces(crossed(lone[1], lone_came))
    step, up, mix = fence(first, up, mix)
    up_came, mix_came = (along_all(up), cross(mix))
    result = lax.cond(step, attention_ends, conv_ends)
    up_came, mix_came, (ends, small) = fence(up_came, mix_came, result)
    mix_came = along_all(crossed(mix[1], mix_came))
    lone_came = [only(1, piece, count) for count, piece in enumerate(lone[1:], 1)]
    shard_c = sum((piece.astype(F32) for piece in lone_came), lone[0].astype(F32))
    shard_mix = scattered(mix_came)
    shards_out = (
        shard_mix[:, : 2 * width], shard_mix[:, 2 * width :],
        scattered(gate_came), scattered(up_came), scattered(down_came),
    )
    mail = lax.ppermute(
        jnp.concatenate([shard_c, small], axis=0), "section", swap
    )
    c_shard = jnp.where(first, mail[:conv_cut], shard_c[conv_cut:])
    theirs = mail[2 * conv_cut :]
    merged_a, merged_c = (jnp.where(first, small, theirs), jnp.where(first, theirs, small))
    grad_norm = jnp.stack([merged_a[:2], merged_c[:2]])
    grad_head = merged_a[5, :PAIR].reshape(2, HEAD)
    return (
        ends.reshape(1, 1, stretches, rows, width),
        grad_norm,
        grad_head,
        merged_c[2:5],
        *[shard[None] for shard in shards_out],
        c_shard,
    )


def solution(mesh):
    return jax.shard_map(
        local,
        mesh=mesh,
        in_specs=(
            P("fsdp", None, "seq", None),
            P("fsdp", None, "seq", None),
            P("section", None, None),
            P(),
            P(),
            P("section", "fsdp", None),
            P("section", "fsdp", None),
            P("section", "fsdp", None),
            P("section", "fsdp", None),
            P("section", "fsdp", None),
            P(("section", "fsdp"), None),
        ),
        out_specs=(
            P("section", "fsdp", None, "seq", None),
            P(),
            P(),
            P(),
            P("section", ("seq", "fsdp"), None),
            P("section", ("seq", "fsdp"), None),
            P("section", ("seq", "fsdp"), None),
            P("section", ("seq", "fsdp"), None),
            P("section", ("seq", "fsdp"), None),
            P(("section", "seq", "fsdp"), None),
        ),
        check_vma=False,
    )
```

```python
import functools

import jax
import jax.numpy as jnp
from jax import lax
from jax.experimental import pallas as pl
from jax.experimental.pallas import tpu as pltpu
from jax.sharding import PartitionSpec as P

HEADS = 16
KV_HEADS = 8
HEAD = 64
PAIR = 2 * HEAD
GROUP = 2 * PAIR

EPSILON = 1e-05
THETA = 1000000.0
NEGATIVE = -1e30
BF16 = jnp.bfloat16
F32 = jnp.float32
VMEM_LIMIT = 56 * 1024 * 1024


def rms_scale(value):
    return lax.rsqrt(jnp.mean(value * value, axis=-1, keepdims=True) + EPSILON)


def norm_back(grad_out, value, scale, gain):
    inner = grad_out * gain
    return scale * (inner - value * scale * scale * jnp.mean(inner * value, axis=-1, keepdims=True))


def matmul(left, right):
    return jnp.dot(left, right, preferred_element_type=F32)


def matmul_t(left, right):
    return lax.dot_general(left, right, (((1,), (1,)), ((), ())), preferred_element_type=F32)


def outer_sum(left, right):
    return lax.dot_general(left, right, (((0,), (0,)), ((), ())), preferred_element_type=F32)


def params():
    return pltpu.CompilerParams(vmem_limit_bytes=VMEM_LIMIT)


def light():
    return pl.CostEstimate(flops=1 << 20, bytes_accessed=1 << 20, transcendentals=0)


def group_mean(value):
    row = lax.broadcasted_iota(jnp.int32, (PAIR, PAIR), 0) // HEAD
    col = lax.broadcasted_iota(jnp.int32, (PAIR, PAIR), 1) // HEAD
    ones = jnp.where(row == col, 1.0 / HEAD, 0.0).astype(F32)
    return jnp.dot(value, ones, precision=lax.Precision.HIGHEST, preferred_element_type=F32)


def lane_swap(value):
    lane = lax.broadcasted_iota(jnp.int32, value.shape, 1) % HEAD
    return jnp.where(
        lane < HEAD // 2, pltpu.roll(value, PAIR - HEAD // 2, 1), pltpu.roll(value, HEAD // 2, 1)
    )


def project_kernel(x_ref, w_ref, cos_ref, sin_ref, gain_ref, raw_ref, q_ref, kv_ref):
    raw = jnp.dot(x_ref[...], w_ref[...], preferred_element_type=F32).astype(BF16)
    raw_ref[...] = raw
    for part, out in ((0, q_ref), (1, kv_ref)):
        vec = raw[:, part * PAIR : (part + 1) * PAIR].astype(F32)
        normed = vec * lax.rsqrt(group_mean(vec * vec) + EPSILON) * gain_ref[part : part + 1, :]
        turned = normed * cos_ref[...] + lane_swap(normed) * sin_ref[...]
        if part == 1:
            lane = lax.broadcasted_iota(jnp.int32, vec.shape, 1)
            turned = jnp.where(lane < HEAD, turned, vec)
        out[...] = turned.astype(BF16)


def project(normed, weight, cosine, sine, gain_rows):
    tokens, width = normed.shape
    whole = lambda g: (0, 0)
    column = lambda g: (0, g)
    return pl.pallas_call(
        project_kernel,
        grid=(KV_HEADS,),
        in_specs=[
            pl.BlockSpec((tokens, width), whole),
            pl.BlockSpec((width, GROUP), column),
            pl.BlockSpec((tokens, PAIR), whole),
            pl.BlockSpec((tokens, PAIR), whole),
            pl.BlockSpec((8, PAIR), whole),
        ],
        out_specs=[
            pl.BlockSpec((tokens, GROUP), column),
            pl.BlockSpec((tokens, PAIR), column),
            pl.BlockSpec((tokens, PAIR), column),
        ],
        out_shape=[
            jax.ShapeDtypeStruct((tokens, KV_HEADS * GROUP), BF16),
            jax.ShapeDtypeStruct((tokens, KV_HEADS * PAIR), BF16),
            jax.ShapeDtypeStruct((tokens, KV_HEADS * PAIR), BF16),
        ],
        compiler_params=params(),
        cost_estimate=light(),
    )(normed, weight, cosine, sine, gain_rows)


def attend_kernel(rows, stretches, part_ref, q_ref, own_ref, peer_ref, out_ref):
    second = part_ref[0] == 1
    for stretch in range(stretches):
        blocks = []
        for s in range(stretch + 1):
            blocks += [own_ref[s * rows : (s + 1) * rows, :], peer_ref[s * rows : (s + 1) * rows, :]]
        pack = jnp.concatenate(blocks, axis=0)
        keys, values = (pack[:, :HEAD], pack[:, HEAD:])
        count = pack.shape[0]
        row = lax.broadcasted_iota(jnp.int32, (rows, count), 0)
        col = lax.broadcasted_iota(jnp.int32, (rows, count), 1) - stretch * 2 * rows
        allowed = (col <= row) | ((col >= rows) & second)
        for j in range(2):
            query = q_ref[stretch * rows : (stretch + 1) * rows, j * HEAD : (j + 1) * HEAD]
            scores = matmul_t(query, keys) * HEAD ** (-0.5)
            scores = jnp.where(allowed, scores, NEGATIVE)
            exponent = jnp.exp(scores - jnp.max(scores, axis=1, keepdims=True))
            total = jnp.sum(exponent, axis=1, keepdims=True)
            probs = (exponent * (1.0 / total)).astype(BF16)
            out_ref[stretch * rows : (stretch + 1) * rows, j * HEAD : (j + 1) * HEAD] = jnp.dot(
                probs, values, preferred_element_type=F32
            ).astype(BF16)


def attend(part, query, own, peer, rows, stretches):
    tokens = query.shape[0]
    column = lambda g: (0, g)
    return pl.pallas_call(
        functools.partial(attend_kernel, rows, stretches),
        grid=(KV_HEADS,),
        in_specs=[pl.BlockSpec(memory_space=pltpu.SMEM)]
        + [pl.BlockSpec((tokens, PAIR), column)] * 3,
        out_specs=pl.BlockSpec((tokens, PAIR), column),
        out_shape=jax.ShapeDtypeStruct((tokens, KV_HEADS * PAIR), BF16),
        compiler_params=params(),
        cost_estimate=light(),
    )(part, query, own, peer)


def attend_back_kernel(
    rows, stretches, part_ref, q_ref, own_ref, peer_ref, grad_ref, dq_ref, down_ref, dpeer_ref
):
    second = part_ref[0] == 1
    sums = {}
    for stretch in reversed(range(stretches)):
        blocks = []
        for s in range(stretch + 1):
            blocks += [own_ref[s * rows : (s + 1) * rows, :], peer_ref[s * rows : (s + 1) * rows, :]]
        pack = jnp.concatenate(blocks, axis=0)
        keys, values = (pack[:, :HEAD], pack[:, HEAD:])
        count = pack.shape[0]
        col = lax.broadcasted_iota(jnp.int32, (count, rows), 0) - stretch * 2 * rows
        row = lax.broadcasted_iota(jnp.int32, (count, rows), 1)
        allowed = (col <= row) | ((col >= rows) & second)
        span = slice(stretch * rows, (stretch + 1) * rows)
        dkeys, dvalues, dquery = (0.0, 0.0, [])
        for j in range(2):
            query = q_ref[span, j * HEAD : (j + 1) * HEAD]
            grad = grad_ref[span, j * HEAD : (j + 1) * HEAD]
            scores = matmul_t(keys, query) * HEAD ** (-0.5)
            scores = jnp.where(allowed, scores, NEGATIVE)
            exponent = jnp.exp(scores - jnp.max(scores, axis=0, keepdims=True))
            probs = exponent * (1.0 / jnp.sum(exponent, axis=0, keepdims=True))
            dprobs = matmul_t(values, grad)
            dscores = probs * (dprobs - jnp.sum(probs * dprobs, axis=0, keepdims=True))
            dscores = dscores.astype(BF16)
            dvalues += jnp.dot(probs.astype(BF16), grad, preferred_element_type=F32)
            dkeys += jnp.dot(dscores, query, preferred_element_type=F32) * HEAD ** (-0.5)
            dquery.append(outer_sum(dscores, keys) * HEAD ** (-0.5))
        dq_ref[span, :] = jnp.concatenate(dquery, axis=1)
        both = jnp.concatenate([dkeys, dvalues], axis=1)
        for s in range(stretch + 1):
            for side in range(2):
                piece = both[(2 * s + side) * rows : (2 * s + side + 1) * rows]
                sums[s, side] = sums[s, side] + piece if (s, side) in sums else piece
    for (s, side), value in sums.items():
        out = (down_ref, dpeer_ref)[side]
        out[s * rows : (s + 1) * rows, :] = value.astype(out.dtype)


def attend_back(part, query, own, peer, grad, rows, stretches, groups):
    tokens = query.shape[0]
    count = len(groups)
    column = lambda g: (0, g + groups.start)
    shape = lambda kind: jax.ShapeDtypeStruct((tokens, count * PAIR), kind)
    return pl.pallas_call(
        functools.partial(attend_back_kernel, rows, stretches),
        grid=(count,),
        in_specs=[pl.BlockSpec(memory_space=pltpu.SMEM)]
        + [pl.BlockSpec((tokens, PAIR), column)] * 4,
        out_specs=[pl.BlockSpec((tokens, PAIR), lambda g: (0, g))] * 3,
        out_shape=[shape(F32), shape(F32), shape(BF16)],
        compiler_params=params(),
        cost_estimate=light(),
    )(part, query, own, peer, grad)


def project_back_kernel(
    raw_ref, dq_ref, own_ref, recv_ref, cos_ref, sin_ref, gain_ref, w_ref, pack_ref, normed_ref, head_ref
):
    first = pl.program_id(0) == 0
    grads = []
    for part in range(2):
        vec = raw_ref[:, part * PAIR : (part + 1) * PAIR].astype(F32)
        if part == 0:
            grad = dq_ref[...]
        else:
            grad = own_ref[...] + recv_ref[...].astype(F32)
        gain = gain_ref[part : part + 1, :]
        scale = lax.rsqrt(group_mean(vec * vec) + EPSILON)
        turned = grad * cos_ref[...] - lane_swap(grad) * sin_ref[...]
        gain_sum = jnp.sum(turned * vec * scale, axis=0, keepdims=True)
        inner = turned * gain
        back = scale * (inner - vec * scale * scale * group_mean(inner * vec))
        if part == 1:
            lane = lax.broadcasted_iota(jnp.int32, vec.shape, 1)
            back = jnp.where(lane < HEAD, back, grad)
        back = back.astype(BF16)
        pack_ref[:, part * PAIR : (part + 1) * PAIR] = back
        grads.append((back, gain_sum))
    total = matmul_t(grads[0][0], w_ref[:, :PAIR]) + matmul_t(grads[1][0], w_ref[:, PAIR:])

    @pl.when(first)
    def _():
        normed_ref[...] = total
        head_ref[...] = jnp.zeros_like(head_ref)

    @pl.when(jnp.logical_not(first))
    def _():
        normed_ref[...] += total

    for part in range(2):
        head_ref[part : part + 1, :] += grads[part][1]


def project_back(raw, dquery, own, recv, cosine, sine, gain_rows, weight):
    tokens = raw.shape[0]
    width = weight.shape[0]
    whole = lambda g: (0, 0)
    column = lambda g: (0, g)
    return pl.pallas_call(
        project_back_kernel,
        grid=(KV_HEADS,),
        in_specs=[
            pl.BlockSpec((tokens, GROUP), column),
            pl.BlockSpec((tokens, PAIR), column),
            pl.BlockSpec((tokens, PAIR), column),
            pl.BlockSpec((tokens, PAIR), column),
            pl.BlockSpec((tokens, PAIR), whole),
            pl.BlockSpec((tokens, PAIR), whole),
            pl.BlockSpec((8, PAIR), whole),
            pl.BlockSpec((width, GROUP), column),
        ],
        out_specs=[
            pl.BlockSpec((tokens, GROUP), column),
            pl.BlockSpec((tokens, width), whole),
            pl.BlockSpec((8, PAIR), whole),
        ],
        out_shape=[
            jax.ShapeDtypeStruct((tokens, KV_HEADS * GROUP), BF16),
            jax.ShapeDtypeStruct((tokens, width), F32),
            jax.ShapeDtypeStruct((8, PAIR), F32),
        ],
        compiler_params=params(),
        cost_estimate=light(),
    )(raw, dquery, own, recv, cosine, sine, gain_rows, weight)


LANES = 128


def wide(ref, columns):
    if len(ref.shape) == 2:
        return ref[...]
    count = columns // LANES
    rows = ref.shape[1] // count
    parts = [ref[:, i * rows : (i + 1) * rows, :].reshape(-1, LANES) for i in range(count)]
    return jnp.concatenate(parts, axis=1)


def forward_kernel(x_ref, base_ref, g_ref, u_ref, d_ref, out_ref, act_ref, one_ref, two_ref):
    chunk, width = (act_ref.shape[1], out_ref.shape[1])
    gate_part, up_part, down_part = (wide(g_ref, chunk), wide(u_ref, chunk), wide(d_ref, width))
    down = 0.0
    for span in spans(act_ref.shape[1]):
        gate = jnp.dot(x_ref[...], gate_part[:, span], preferred_element_type=F32)
        upward = jnp.dot(x_ref[...], up_part[:, span], preferred_element_type=F32)
        sigma = jax.nn.sigmoid(gate)
        silu = gate * sigma
        active = (silu * upward).astype(BF16)
        act_ref[:, span] = active
        one_ref[:, span] = (upward * sigma * (1.0 + gate * (1.0 - sigma))).astype(BF16)
        two_ref[:, span] = silu.astype(BF16)
        down += jnp.dot(active, down_part[span], preferred_element_type=F32)

    @pl.when(pl.program_id(0) == 0)
    def _():
        out_ref[...] = base_ref[...] + down

    @pl.when(pl.program_id(0) > 0)
    def _():
        out_ref[...] += down


def store_outer(left_ref, dgate, dup, span, outs):
    half = left_ref.shape[0] // 2
    for right, leave_ref, stay_ref in ((dgate, *outs[:2]), (dup, *outs[2:])):
        product = jnp.dot(left_ref[...], right, preferred_element_type=F32).astype(BF16)
        leave_ref[:, span] = product[:half]
        stay_ref[:, span] = product[half:]


def backward_outer_kernel(grad_ref, left_ref, one_ref, two_ref, g_ref, u_ref, d_ref, out_ref, *outs):
    chunk, width = (one_ref.shape[1], out_ref.shape[1])
    gate_part, up_part, down_part = (wide(g_ref, chunk), wide(u_ref, chunk), wide(d_ref, width))
    total = 0.0
    for span in spans(one_ref.shape[1]):
        active = matmul_t(grad_ref[...], down_part[span])
        dgate = (active * one_ref[:, span].astype(F32)).astype(BF16)
        dup = (active * two_ref[:, span].astype(F32)).astype(BF16)
        store_outer(left_ref, dgate, dup, span, outs)
        total += matmul_t(dgate, gate_part[:, span]) + matmul_t(dup, up_part[:, span])

    @pl.when(pl.program_id(0) == 0)
    def _():
        out_ref[...] = total

    @pl.when(pl.program_id(0) > 0)
    def _():
        out_ref[...] += total


def outer_kernel(left_ref, dg_ref, du_ref, *outs):
    store_outer(left_ref, dg_ref[...], du_ref[...], slice(None), outs)


def both_ways_kernel(x_ref, grad_ref, g_ref, u_ref, d_ref, out_ref, act_ref, dg_ref, du_ref):
    chunk, width = (act_ref.shape[1], out_ref.shape[1])
    gate_part, up_part, down_part = (wide(g_ref, chunk), wide(u_ref, chunk), wide(d_ref, width))
    total = 0.0
    for span in spans(act_ref.shape[1]):
        gate = jnp.dot(x_ref[...], gate_part[:, span], preferred_element_type=F32)
        upward = jnp.dot(x_ref[...], up_part[:, span], preferred_element_type=F32)
        dactive = matmul_t(grad_ref[...], down_part[span])
        sigma = jax.nn.sigmoid(gate)
        silu = gate * sigma
        act_ref[:, span] = (silu * upward).astype(BF16)
        dgate = (dactive * upward * sigma * (1.0 + gate * (1.0 - sigma))).astype(BF16)
        dup = (dactive * silu).astype(BF16)
        dg_ref[:, span] = dgate
        du_ref[:, span] = dup
        total += matmul_t(dgate, gate_part[:, span]) + matmul_t(dup, up_part[:, span])

    @pl.when(pl.program_id(0) == 0)
    def _():
        out_ref[...] = total

    @pl.when(pl.program_id(0) > 0)
    def _():
        out_ref[...] += total


def down_kernel(base_ref, act_ref, d_ref, out_ref):
    down = jnp.dot(act_ref[...], wide(d_ref, out_ref.shape[1]), preferred_element_type=F32)

    @pl.when(pl.program_id(0) == 0)
    def _():
        out_ref[...] = base_ref[...] + down

    @pl.when(pl.program_id(0) > 0)
    def _():
        out_ref[...] += down


def spans(chunk):
    starts = list(range(0, max(chunk - 511, 1), 512))
    return [slice(a, b) for a, b in zip(starts, starts[1:] + [chunk])]


def sub_chunk(chunk):
    return next(size for size in (512, 384, 256, 128, chunk) if chunk % size == 0)


CHUNKS = 4


def can_pack(devices, width, hidden):
    gate_rows, down_rows = (width // devices, hidden // devices)
    return (
        devices % CHUNKS == 0
        and hidden % (CHUNKS * LANES) == 0
        and width % LANES == 0
        and gate_rows % 16 == 0
        and down_rows % 16 == 0
    )


def pack_halves(gate, upward, down):
    cut = lambda w: jnp.transpose(w.reshape(w.shape[0], -1, LANES), (1, 0, 2)).reshape(-1, LANES)
    return jnp.concatenate([cut(gate), cut(upward), cut(down)], axis=0)


def weight_specs(weights, tokens, width, hidden):
    if len(weights) == 3:
        chunk = sub_chunk(hidden)
        column = lambda j: (0, j)
        return (
            chunk,
            [
                pl.BlockSpec((width, chunk), column),
                pl.BlockSpec((width, chunk), column),
                pl.BlockSpec((chunk, width), lambda j: (j, 0)),
            ],
            weights,
        )
    devices = weights[0].shape[0]
    chunk = hidden // CHUNKS
    tall = width // devices * (hidden // LANES)
    piece = tall // CHUNKS
    return (
        chunk,
        [
            pl.BlockSpec((devices, piece, LANES), lambda j: (0, j, 0)),
            pl.BlockSpec((devices, piece, LANES), lambda j: (0, CHUNKS + j, 0)),
            pl.BlockSpec((devices // CHUNKS, tall, LANES), lambda j: (j, 2, 0)),
        ],
        (weights[0],) * 3,
    )


def ff_forward(normed, base, weights, hidden):
    tokens, width = normed.shape
    chunk, specs, operands = weight_specs(weights, tokens, width, hidden)
    whole = lambda j: (0, 0)
    column = lambda j: (0, j)
    saved = jax.ShapeDtypeStruct((tokens, hidden), BF16)
    return pl.pallas_call(
        forward_kernel,
        grid=(hidden // chunk,),
        in_specs=[pl.BlockSpec((tokens, width), whole), pl.BlockSpec((tokens, width), whole)]
        + specs,
        out_specs=[pl.BlockSpec((tokens, width), whole)]
        + [pl.BlockSpec((tokens, chunk), column)] * 3,
        out_shape=[jax.ShapeDtypeStruct((tokens, width), F32), saved, saved, saved],
        compiler_params=params(),
        cost_estimate=light(),
    )(normed, base, *operands)


def ff_both_ways(normed, grad, weights, hidden):
    tokens, width = normed.shape
    chunk, specs, operands = weight_specs(weights, tokens, width, hidden)
    whole = lambda j: (0, 0)
    column = lambda j: (0, j)
    saved = jax.ShapeDtypeStruct((tokens, hidden), BF16)
    return pl.pallas_call(
        both_ways_kernel,
        grid=(hidden // chunk,),
        in_specs=[pl.BlockSpec((tokens, width), whole), pl.BlockSpec((tokens, width), whole)]
        + specs,
        out_specs=[pl.BlockSpec((tokens, width), whole)]
        + [pl.BlockSpec((tokens, chunk), column)] * 3,
        out_shape=[jax.ShapeDtypeStruct((tokens, width), F32), saved, saved, saved],
        compiler_params=params(),
        cost_estimate=light(),
    )(normed, grad, *operands)


def ff_down(base, active, weights, hidden):
    tokens, width = base.shape
    chunk, specs, operands = weight_specs(weights, tokens, width, hidden)
    whole = lambda j: (0, 0)
    return pl.pallas_call(
        down_kernel,
        grid=(hidden // chunk,),
        in_specs=[
            pl.BlockSpec((tokens, width), whole),
            pl.BlockSpec((tokens, chunk), lambda j: (0, j)),
            specs[2],
        ],
        out_specs=pl.BlockSpec((tokens, width), whole),
        out_shape=jax.ShapeDtypeStruct((tokens, width), F32),
        compiler_params=params(),
        cost_estimate=light(),
    )(base, active, operands[2])


def ff_backward_outer(grad, left, one, two, weights, hidden):
    tokens, width = grad.shape
    chunk, specs, operands = weight_specs(weights, tokens, width, hidden)
    whole = lambda j: (0, 0)
    column = lambda j: (0, j)
    half = left.shape[0] // 2
    return pl.pallas_call(
        backward_outer_kernel,
        grid=(hidden // chunk,),
        in_specs=[
            pl.BlockSpec((tokens, width), whole),
            pl.BlockSpec(left.shape, whole),
            pl.BlockSpec((tokens, chunk), column),
            pl.BlockSpec((tokens, chunk), column),
        ]
        + specs,
        out_specs=[pl.BlockSpec((tokens, width), whole)]
        + [pl.BlockSpec((half, chunk), column)] * 4,
        out_shape=[jax.ShapeDtypeStruct((tokens, width), F32)]
        + [jax.ShapeDtypeStruct((half, hidden), BF16)] * 4,
        compiler_params=params(),
        cost_estimate=light(),
    )(grad, left, one, two, *operands)


def ff_outer(left, dgate, dup):
    tokens, hidden = dgate.shape
    chunk = sub_chunk(hidden)
    column = lambda j: (0, j)
    half = left.shape[0] // 2
    return pl.pallas_call(
        outer_kernel,
        grid=(hidden // chunk,),
        in_specs=[pl.BlockSpec(left.shape, lambda j: (0, 0))]
        + [pl.BlockSpec((tokens, chunk), column)] * 2,
        out_specs=[pl.BlockSpec((half, chunk), column)] * 4,
        out_shape=[jax.ShapeDtypeStruct((half, hidden), BF16)] * 4,
        compiler_params=params(),
        cost_estimate=light(),
    )(left, dgate, dup)


def local(
    tokens,
    cotangent,
    norm_gains,
    head_gains,
    conv_kernel,
    mix_in,
    mix_out,
    w_gate,
    w_up,
    w_down,
    conv_c,
):
    first = lax.axis_index("section") == 0
    part = lax.axis_index("seq")
    place = lax.axis_index("fsdp")
    fsdp = lax.axis_size("fsdp")
    chips = fsdp // 2
    chip, core = (place // 2, place % 2)
    stretches, rows, width = tokens.shape[1:]
    hidden = w_gate.shape[2]
    total = stretches * rows
    block = 2 * rows
    gains = norm_gains[0]

    cores = [(i, i ^ 1) for i in range(fsdp)]
    swap = [(0, 1), (1, 0)]

    def after(value, *earlier):
        return lax.optimization_barrier((value, *earlier))[0] if earlier else value

    def to_core(value):
        return lax.ppermute(value, "fsdp", cores)

    def to_peer(value):
        return lax.ppermute(value, "seq", swap)

    def exchange(value, offset, section=None):
        if section is None:
            return lax.ppermute(value, "fsdp", [(i, i ^ offset) for i in range(fsdp)])
        pairs = [
            ((section * 2 + side) * fsdp + i, (section * 2 + side) * fsdp + (i ^ offset))
            for side in range(2)
            for i in range(fsdp)
        ]
        return lax.ppermute(value, ("section", "seq", "fsdp"), pairs)

    def gather(shards):
        results = []
        for shard in shards:
            depth, columns = shard.shape
            half = depth // 2
            mine = lax.dynamic_slice_in_dim(shard, part * half, half, 0)
            if results:
                mine = after(mine, results[-1])
            batches = [([0], mine[None])]
            for bit in reversed(range(chips.bit_length() - 1)):
                offsets = [offset ^ (1 << bit) for known, rows_of in batches for offset in known]
                block_of = jnp.concatenate([rows_of for known, rows_of in batches], axis=0)
                batches.append((offsets, exchange(block_of, 2 << bit)))
            arrived = batches[1:]
            held = jnp.zeros((chips, 2, half, columns), BF16)
            held = lax.dynamic_update_slice(
                held, shard.reshape(1, 2, half, columns), (chip, 0, 0, 0)
            )
            for known, near in arrived:
                far = to_peer(near)
                for index, offset in enumerate(known):
                    for value, where in ((near, part), (far, 1 - part)):
                        held = lax.dynamic_update_slice(
                            held, value[index][None, None], (chip ^ offset, where, 0, 0)
                        )
            other = to_core(held)
            full = jnp.broadcast_to(held[:, None], (chips, 2, 2, half, columns))
            full = lax.dynamic_update_slice(full, other[:, None], (0, 1 - core, 0, 0, 0))
            results.append(full.reshape(fsdp * depth, columns))
        return results

    def turned(value):
        cut = value.shape[1] // (2 * fsdp)
        wide = value.reshape(value.shape[0], 2, chips, 2, cut)
        sides = [
            lax.dynamic_index_in_dim(wide, side, 3, keepdims=False) for side in (1 - core, core)
        ]
        return jnp.concatenate(
            [jnp.transpose(side.reshape(-1, 2 * chips * cut)) for side in sides], axis=0
        )

    def blocks(both):
        return both.astype(BF16).reshape(2, chips, -1, both.shape[1])

    def core_sum(left, right):
        half = left.shape[0] // 2
        leaving = matmul(left[:half], right).astype(BF16)
        return blocks(matmul(left[half:], right) + to_core(leaving).astype(F32))

    def core_add(leaving, staying):
        return blocks(staying.astype(F32) + leaving.astype(F32))

    def only(section, value, move):
        pairs = []
        for side in range(2):
            for i in range(fsdp):
                source = (section * 2 + side) * fsdp + i
                if move == "seq":
                    target = (section * 2 + 1 - side) * fsdp + i
                elif move == "core":
                    target = (section * 2 + side) * fsdp + (i ^ 1)
                else:
                    target = (section * 2 + side) * fsdp + (i + 2 * move) % fsdp
                pairs.append((source, target))
        return lax.ppermute(value, ("section", "seq", "fsdp"), pairs)

    def sides(both):
        return [
            lax.dynamic_index_in_dim(both, side, 0, keepdims=False) for side in (1 - part, part)
        ]

    def crossed(staying, came):
        return (staying.astype(F32) + came.astype(F32)).astype(BF16)

    def fence(*groups):
        return lax.optimization_barrier(groups)

    def together(values, *others):
        return lax.optimization_barrier((*values, *others))[: len(values)]

    def zeros(*shape, kind=BF16):
        return jnp.zeros(shape, kind)

    conv_cut = width // (4 * fsdp)
    c_low = lax.ppermute(conv_c, "section", [(0, 1)])

    def half_of(shard):
        return lax.dynamic_slice_in_dim(shard, part * (shard.shape[0] // 2), shard.shape[0] // 2, 0)

    halves = (half_of(w_gate[0]), half_of(w_up[0]), half_of(w_down[0]))
    if can_pack(2 * fsdp, width, hidden):
        wide_weights = (lax.all_gather(pack_halves(*halves), ("fsdp", "seq"), axis=0),)
    else:
        wide_weights = tuple(
            lax.all_gather(half, ("fsdp", "seq"), axis=0, tiled=True) for half in halves
        )

    positions = (
        jnp.arange(stretches)[:, None] * block + part * rows + jnp.arange(rows)[None, :]
    ).reshape(total)
    part_ref = part.astype(jnp.int32).reshape(1)

    def rope():
        lane = jnp.arange(PAIR)
        frequency = THETA ** (-(lane % (HEAD // 2)).astype(F32) * 2.0 / HEAD)
        angle = positions.astype(F32)[:, None] * frequency[None, :]
        sign = jnp.where(lane % HEAD < HEAD // 2, -1.0, 1.0)
        return (jnp.cos(angle), jnp.sin(angle) * sign[None, :])

    def gain_rows():
        return jnp.zeros((8, PAIR), F32).at[:2].set(jnp.tile(head_gains, (1, 2)))

    def attention_mixer():
        w_in, w_out = gather((mix_in[0], mix_out[0]))
        source = tokens[0].reshape(total, width).astype(F32)
        normed = (source * rms_scale(source) * gains[0]).astype(BF16)
        cosine, sine = rope()
        raw, query, own = project(normed, w_in, cosine, sine, gain_rows())
        peer = to_peer(own)
        heads = attend(part_ref, query, own, peer, rows, stretches)
        resid = source + matmul(heads, w_out)
        normed_two = (resid * rms_scale(resid) * gains[1]).astype(BF16)
        weights = (w_in, w_out, zeros(width, width))
        kept = (normed, raw, query, own, peer, heads, resid, normed_two)
        return (weights, kept, cosine, sine)

    def conv_gather():
        both = jnp.concatenate([c_low, conv_c], axis=1)
        w_in, c_wide, w_out = gather((mix_in[0], both, mix_out[0]))
        w_c = jnp.concatenate([c_wide[:, :width], c_wide[:, width:]], axis=0)
        flat = lambda: zeros(total, width)
        kept = (
            flat(), zeros(total, KV_HEADS * GROUP), flat(), flat(), flat(), flat(),
            zeros(total, width, kind=F32), flat(),
        )
        table = lambda: zeros(total, PAIR, kind=F32)
        return ((w_in, w_out, w_c), kept, table(), table())

    weights, kept, cosine, sine = lax.cond(first, attention_mixer, conv_gather)

    def attention_hidden():
        result, *saved = ff_forward(kept[-1], kept[-2], wide_weights, hidden)
        return (result.astype(BF16), *saved)

    def conv_wait():
        return (zeros(total, width), *[zeros(total, hidden) for _ in range(3)])

    link, active, one, two = lax.cond(first, attention_hidden, conv_wait)
    link = lax.ppermute(link, "section", [(0, 1)])

    def tail_of(value, start):
        return to_peer(value.reshape(stretches, rows, width)[:, start : start + 2])

    def conv_both():
        w_in, w_out, w_c = weights
        source = link.astype(F32)
        scale_one = rms_scale(source)
        normed = (source * scale_one * gains[0]).astype(BF16)
        pair = matmul(normed, w_in)
        left, right = (pair[:, :width], pair[:, width:])
        product = (left * right).astype(BF16)
        tails = tail_of(product, rows - 2).astype(F32)
        conv_gate = matmul(normed, w_c).astype(BF16).astype(F32)
        early = jnp.concatenate([jnp.zeros_like(tails[:1]), tails[:-1]], axis=0)
        before = jnp.where(part == 0, early, tails)
        inner = product.astype(F32).reshape(stretches, rows, width)
        longer = jnp.concatenate([before, inner], axis=1)
        taps = [longer[:, i : i + rows] for i in range(3)]
        state = sum(conv_kernel[i] * taps[i] for i in range(3)).reshape(total, width)
        heads = (conv_gate * state).astype(BF16)
        resid = source + matmul(heads, w_out)
        scale_two = rms_scale(resid)
        normed_two = (resid * scale_two * gains[1]).astype(BF16)
        grad_ff = cotangent[0].reshape(total, width)
        grad_two, active, dgate, dup = ff_both_ways(normed_two, grad_ff, wide_weights, hidden)
        gain_two = jnp.sum(grad_two * resid * scale_two, axis=0)
        grad_resid = grad_ff.astype(F32) + norm_back(grad_two, resid, scale_two, gains[1])
        dmix = grad_resid.astype(BF16)
        dheads = matmul_t(dmix, w_out).astype(BF16).astype(F32)
        dgate_c = (dheads * state).astype(BF16)
        dstate = (dheads * conv_gate).reshape(stretches, rows, width)
        fronts = tail_of(dstate, 0)
        late = jnp.concatenate([fronts[1:], jnp.zeros_like(fronts[:1])], axis=0)
        after = jnp.where(part == 0, fronts, late)
        further = jnp.concatenate([dstate, after], axis=1)
        dproduct = sum(conv_kernel[2 - i] * further[:, i : i + rows] for i in range(3))
        dproduct = dproduct.reshape(total, width).astype(BF16).astype(F32)
        kernel_grad = jnp.stack([jnp.sum(dstate * taps[i], axis=(0, 1)) for i in range(3)])
        dproj = jnp.concatenate([dproduct * right, dproduct * left], axis=1).astype(BF16)
        grad_one = matmul_t(dproj, w_in) + matmul_t(dgate_c, w_c)
        gain_one = jnp.sum(grad_one * source * scale_one, axis=0)
        grad_source = grad_resid + norm_back(grad_one, source, scale_one, gains[0])
        small = jnp.concatenate(
            [jnp.zeros((2, width), F32), gain_one[None], gain_two[None], kernel_grad,
             jnp.zeros((1, width), F32)], axis=0
        )
        lefts = (normed, heads, normed_two, active)
        moved = (dproj, dgate_c, dmix, dgate, dup)
        return (resid, lefts, moved, small, grad_source.astype(BF16))

    def attention_idle():
        flat = lambda: zeros(total, width)
        wide = lambda: zeros(total, hidden)
        lefts = (kept[0], kept[5], kept[7], active)
        moved = (zeros(total, 2 * width), flat(), flat(), wide(), wide())
        return (zeros(total, width, kind=F32), lefts, moved, zeros(8, width, kind=F32), flat())

    conv_resid, lefts, moved, conv_small, grad_link = lax.cond(first, attention_idle, conv_both)
    normed, heads, normed_two, active_both = together(lefts, grad_link)
    grad_link = lax.ppermute(grad_link, "section", [(1, 0)])
    conv_dproj, dgate_c, conv_dmix, conv_dgate, conv_dup = moved
    left_down, left_two, left_heads, left_normed = [
        turned(value) for value in (active_both, normed_two, heads, normed)
    ]
    grad_ff = jnp.where(first, grad_link, cotangent[0].reshape(total, width))
    down = sides(core_sum(left_down, grad_ff))
    groups = [[i for i in range(fsdp) if i % 2 == side] for side in range(2)]

    def cross(half):
        return to_peer(half[0])

    def along_all(own):
        return [lax.all_to_all(own, "fsdp", 0, 0, axis_index_groups=groups, tiled=True)]

    class Halving:
        def __init__(self, own):
            self.held, self.bit = (own, 0)
            self.split()

        def split(self):
            count, *shape = self.held.shape
            wide = self.held.reshape(count // 2, 2, *shape)
            side = (chip >> self.bit) % 2
            self.leaving, self.staying = [
                lax.dynamic_index_in_dim(wide, which, 1, keepdims=False)
                for which in (1 - side, side)
            ]

        def send(self, section=None):
            return exchange(self.leaving, 2 << self.bit, section)

        def add(self, came):
            last = self.staying.shape[0] == 1
            self.held = self.staying.astype(F32) + came.astype(F32)
            self.bit += 1
            if not last:
                self.held = self.held.astype(BF16)
                self.split()
            return self

    def scattered(came):
        return sum(jnp.sum(part.astype(F32), axis=0) for part in came)

    def halves_of(leaving, staying):
        return sides(core_add(to_core(leaving), staying))

    def attention_ff():
        grad_two, *products = ff_backward_outer(grad_ff, left_two, one, two, wide_weights, hidden)
        return (grad_two, halves_of(*products[:2]), *products[2:])

    def conv_ff():
        products = ff_outer(left_two, conv_dgate, conv_dup)
        return (zeros(total, width, kind=F32), halves_of(*products[:2]), *products[2:])

    step, down = fence(first, down)
    down_came = cross(down)
    result = lax.cond(step, attention_ff, conv_ff)
    down_came, (grad_two, gate, up_leaving, up_staying) = fence(down_came, result)

    def attention_core():
        unused, raw, query, own, peer, unused, resid, unused = kept
        scale_two = rms_scale(resid)
        gain_two = jnp.sum(grad_two * resid * scale_two, axis=0)
        grad_resid = grad_link.astype(F32) + norm_back(grad_two, resid, scale_two, gains[1])
        dmix = grad_resid.astype(BF16)
        dheads = matmul_t(dmix, weights[1]).astype(BF16)
        up, dheads = fence(halves_of(up_leaving, up_staying), dheads)
        grads = []
        for groups in (range(KV_HEADS // 2), range(KV_HEADS // 2, KV_HEADS)):
            if grads:
                grads, dheads = fence(grads, dheads)
            grads.append(attend_back(part_ref, query, own, peer, dheads, rows, stretches, groups))
        recv = [to_peer(half[2]) for half in grads]
        dquery, down_kv = [
            jnp.concatenate([half[i] for half in grads], axis=1) for i in range(2)
        ]
        recv = jnp.concatenate(recv, axis=1)
        blank = zeros(chips, 2 * conv_cut, width)
        return (up, gain_two, grad_resid, dmix, dquery, down_kv, recv, [blank, blank])

    def conv_core():
        mixed = normed.reshape(total, 2, 2 * fsdp, conv_cut)
        mixed = jnp.transpose(mixed, (0, 2, 1, 3)).reshape(total, width)
        lone = sides(core_sum(turned(mixed), dgate_c))
        output = ff_down(conv_resid, active_both, wide_weights, hidden)
        flat = lambda: zeros(total, width, kind=F32)
        up = halves_of(up_leaving, up_staying)
        return (
            up, zeros(width, kind=F32), output, conv_dmix, flat(), flat(), zeros(total, width), lone,
        )

    down = crossed(down[1], down_came)
    step, down, gate = fence(first, down, gate)
    down_came, gate_came = (along_all(down), cross(gate))
    result = lax.cond(step, attention_core, conv_core)
    down_came, gate_came, result = fence(down_came, gate_came, result)
    up, gain_two, grad_resid, dmix, dquery, down_kv, recv, lone = result

    def joined(*halves):
        return [jnp.concatenate(parts, axis=2) for parts in zip(*halves)]

    def attention_project():
        dproj, grad_one, head_rows = project_back(
            kept[1], dquery, down_kv, recv, cosine, sine, gain_rows(), weights[0]
        )
        inward = sides(core_sum(left_normed, dproj))
        outward = sides(core_sum(left_heads, dmix))
        source = tokens[0].reshape(total, width).astype(F32)
        scale_one = rms_scale(source)
        gain_one = jnp.sum(grad_one * source * scale_one, axis=0)
        grad_source = grad_resid + norm_back(grad_one, source, scale_one, gains[0])
        head_grad = jnp.stack([head_rows[0, :HEAD] + head_rows[0, HEAD:], head_rows[1, :HEAD]])
        head_row = jnp.pad(head_grad.reshape(1, PAIR), ((0, 0), (0, width - PAIR)))
        small = jnp.concatenate(
            [gain_one[None], gain_two[None], jnp.zeros((5, width), F32), head_row], axis=0
        )
        return (joined(inward, outward), grad_source, small + to_core(small))

    def conv_project():
        outward = sides(core_sum(left_heads, dmix))
        inward = sides(core_sum(left_normed, conv_dproj))
        output = grad_resid
        small = conv_small + to_core(conv_small)
        return (joined(inward, outward), output, small)

    gate = crossed(gate[1], gate_came)
    step, gate, up, lone = fence(first, gate, up, lone)
    gate_came, up_came, lone_came = (along_all(gate), cross(up), only(1, lone[0], "seq"))
    result = lax.cond(step, attention_project, conv_project)
    gate_came, up_came, lone_came, result = fence(gate_came, up_came, lone_came, result)
    mix, ends, small = result

    up = Halving(crossed(up[1], up_came))
    lone = Halving(crossed(lone[1], lone_came))
    mix_came = cross(mix)
    up_came, lone_came = (up.send(), lone.send(1))
    small = small + lax.ppermute(small, "section", swap)
    up_came, lone_came, small = fence(up_came, lone_came, small)
    up, lone, small_came = (up.add(up_came), lone.add(lone_came), to_peer(small))
    bits = chips.bit_length() - 1
    for bit in range(1, bits):
        up_came, lone_came = (up.send(), lone.send(1))
        if bit == 1:
            mix_came, small_came = fence(mix_came, small_came)
            mix = Halving(crossed(mix[1], mix_came))
            small = small + small_came
            mix_came, small_came = (mix.send(), exchange(small, 2))
        up_came, lone_came, mix_came, small_came = fence(
            up_came, lone_came, mix_came, small_came
        )
        up, lone, mix = (up.add(up_came), lone.add(lone_came), mix.add(mix_came))
        small = small + small_came
        mix_came, small_came = (mix.send(), exchange(small, 2 << bit))
    mail = lax.ppermute(lone.held[0, :conv_cut], "section", [(1, 0)])
    mail, mix_came, small_came = fence(mail, mix_came, small_came)
    small = small + small_came
    shard_mix = mix.add(mix_came).held[0]
    c_shard = jnp.where(first, mail, lone.held[0, conv_cut:])
    shards_out = (
        shard_mix[:, : 2 * width], shard_mix[:, 2 * width :],
        scattered(gate_came), up.held[0], scattered(down_came),
    )
    return (
        ends.reshape(1, 1, stretches, rows, width),
        small[:4].reshape(2, 2, width),
        small[7, :PAIR].reshape(2, HEAD),
        small[4:7],
        *[shard[None] for shard in shards_out],
        c_shard,
    )


def solution(mesh):
    return jax.shard_map(
        local,
        mesh=mesh,
        in_specs=(
            P("fsdp", None, "seq", None),
            P("fsdp", None, "seq", None),
            P("section", None, None),
            P(),
            P(),
            P("section", "fsdp", None),
            P("section", "fsdp", None),
            P("section", "fsdp", None),
            P("section", "fsdp", None),
            P("section", "fsdp", None),
            P(("section", "fsdp"), None),
        ),
        out_specs=(
            P("section", "fsdp", None, "seq", None),
            P(),
            P(),
            P(),
            P("section", ("seq", "fsdp"), None),
            P("section", ("seq", "fsdp"), None),
            P("section", ("seq", "fsdp"), None),
            P("section", ("seq", "fsdp"), None),
            P("section", ("seq", "fsdp"), None),
            P(("section", "seq", "fsdp"), None),
        ),
        check_vma=False,
    )
```

```python
import functools

import jax
import jax.numpy as jnp
from jax import lax
from jax.experimental import pallas as pl
from jax.experimental.pallas import tpu as pltpu
from jax.sharding import PartitionSpec as P

HEADS = 16
KV_HEADS = 8
HEAD = 64
PAIR = 2 * HEAD
GROUP = 2 * PAIR

EPSILON = 1e-05
THETA = 1000000.0
NEGATIVE = -1e30
SCALE = HEAD ** (-0.5)
BF16 = jnp.bfloat16
F32 = jnp.float32
VMEM_LIMIT = 56 * 1024 * 1024


def rms_scale(value):
    return lax.rsqrt(jnp.mean(value * value, axis=-1, keepdims=True) + EPSILON)


def norm_back(grad_out, value, scale, gain):
    inner = grad_out * gain
    return scale * (inner - value * scale * scale * jnp.mean(inner * value, axis=-1, keepdims=True))


def matmul(left, right):
    return jnp.dot(left, right, preferred_element_type=F32)


def matmul_t(left, right):
    return lax.dot_general(left, right, (((1,), (1,)), ((), ())), preferred_element_type=F32)


def outer_sum(left, right):
    return lax.dot_general(left, right, (((0,), (0,)), ((), ())), preferred_element_type=F32)


def params():
    return pltpu.CompilerParams(vmem_limit_bytes=VMEM_LIMIT)


def light():
    return pl.CostEstimate(flops=1 << 20, bytes_accessed=1 << 20, transcendentals=0)


def group_mean(value):
    row = lax.broadcasted_iota(jnp.int32, (PAIR, PAIR), 0) // HEAD
    col = lax.broadcasted_iota(jnp.int32, (PAIR, PAIR), 1) // HEAD
    ones = jnp.where(row == col, 1.0 / HEAD, 0.0).astype(F32)
    return jnp.dot(value, ones, precision=lax.Precision.HIGHEST, preferred_element_type=F32)


def lane_swap(value):
    lane = lax.broadcasted_iota(jnp.int32, value.shape, 1) % HEAD
    return jnp.where(
        lane < HEAD // 2, pltpu.roll(value, PAIR - HEAD // 2, 1), pltpu.roll(value, HEAD // 2, 1)
    )


def project_kernel(x_ref, w_ref, cos_ref, sin_ref, gain_ref, raw_ref, q_ref, kv_ref):
    raw = jnp.dot(x_ref[...], w_ref[...], preferred_element_type=F32).astype(BF16)
    raw_ref[...] = raw
    for part, out in ((0, q_ref), (1, kv_ref)):
        vec = raw[:, part * PAIR : (part + 1) * PAIR].astype(F32)
        normed = vec * lax.rsqrt(group_mean(vec * vec) + EPSILON) * gain_ref[part : part + 1, :]
        turned = normed * cos_ref[...] + lane_swap(normed) * sin_ref[...]
        if part == 1:
            lane = lax.broadcasted_iota(jnp.int32, vec.shape, 1)
            turned = jnp.where(lane < HEAD, turned, vec)
        out[...] = turned.astype(BF16)


def project(normed, weight, cosine, sine, gain_rows):
    tokens, width = normed.shape
    whole = lambda g: (0, 0)
    column = lambda g: (0, g)
    return pl.pallas_call(
        project_kernel,
        grid=(KV_HEADS,),
        in_specs=[
            pl.BlockSpec((tokens, width), whole),
            pl.BlockSpec((width, GROUP), column),
            pl.BlockSpec((tokens, PAIR), whole),
            pl.BlockSpec((tokens, PAIR), whole),
            pl.BlockSpec((8, PAIR), whole),
        ],
        out_specs=[
            pl.BlockSpec((tokens, GROUP), column),
            pl.BlockSpec((tokens, PAIR), column),
            pl.BlockSpec((tokens, PAIR), column),
        ],
        out_shape=[
            jax.ShapeDtypeStruct((tokens, KV_HEADS * GROUP), BF16),
            jax.ShapeDtypeStruct((tokens, KV_HEADS * PAIR), BF16),
            jax.ShapeDtypeStruct((tokens, KV_HEADS * PAIR), BF16),
        ],
        compiler_params=params(),
        cost_estimate=light(),
    )(normed, weight, cosine, sine, gain_rows)


def attend_kernel(rows, stretches, part_ref, q_ref, own_ref, peer_ref, out_ref):
    second = part_ref[0] == 1
    for stretch in range(stretches):
        blocks = []
        for s in range(stretch + 1):
            blocks += [own_ref[s * rows : (s + 1) * rows, :], peer_ref[s * rows : (s + 1) * rows, :]]
        pack = jnp.concatenate(blocks, axis=0)
        keys, values = (pack[:, :HEAD], pack[:, HEAD:])
        early = stretch * 2 * rows
        row = lax.broadcasted_iota(jnp.int32, (rows, 2 * rows), 0)
        col = lax.broadcasted_iota(jnp.int32, (rows, 2 * rows), 1)
        allowed = (col <= row) | ((col >= rows) & second)
        for j in range(2):
            query = q_ref[stretch * rows : (stretch + 1) * rows, j * HEAD : (j + 1) * HEAD]
            scores = matmul_t(query * SCALE, keys)
            last = jnp.where(allowed, scores[:, early:], NEGATIVE)
            scores = jnp.concatenate([scores[:, :early], last], axis=1) if early else last
            exponent = jnp.exp(scores - jnp.max(scores, axis=1, keepdims=True))
            total = jnp.sum(exponent, axis=1, keepdims=True)
            probs = (exponent * (1.0 / total)).astype(BF16)
            out_ref[stretch * rows : (stretch + 1) * rows, j * HEAD : (j + 1) * HEAD] = jnp.dot(
                probs, values, preferred_element_type=F32
            ).astype(BF16)


def attend(part, query, own, peer, rows, stretches):
    tokens = query.shape[0]
    column = lambda g: (0, g)
    return pl.pallas_call(
        functools.partial(attend_kernel, rows, stretches),
        grid=(KV_HEADS,),
        in_specs=[pl.BlockSpec(memory_space=pltpu.SMEM)]
        + [pl.BlockSpec((tokens, PAIR), column)] * 3,
        out_specs=pl.BlockSpec((tokens, PAIR), column),
        out_shape=jax.ShapeDtypeStruct((tokens, KV_HEADS * PAIR), BF16),
        compiler_params=params(),
        cost_estimate=light(),
    )(part, query, own, peer)


def attend_back_kernel(
    rows, stretches, part_ref, q_ref, own_ref, peer_ref, grad_ref, dq_ref, down_ref, dpeer_ref
):
    second = part_ref[0] == 1
    sums = {}
    for stretch in reversed(range(stretches)):
        blocks = []
        for s in range(stretch + 1):
            blocks += [own_ref[s * rows : (s + 1) * rows, :], peer_ref[s * rows : (s + 1) * rows, :]]
        pack = jnp.concatenate(blocks, axis=0)
        keys, values = (pack[:, :HEAD], pack[:, HEAD:])
        early = stretch * 2 * rows
        col = lax.broadcasted_iota(jnp.int32, (2 * rows, rows), 0)
        row = lax.broadcasted_iota(jnp.int32, (2 * rows, rows), 1)
        allowed = (col <= row) | ((col >= rows) & second)
        span = slice(stretch * rows, (stretch + 1) * rows)
        dkeys, dvalues, dquery = (0.0, 0.0, [])
        for j in range(2):
            query = q_ref[span, j * HEAD : (j + 1) * HEAD] * SCALE
            grad = grad_ref[span, j * HEAD : (j + 1) * HEAD]
            scores = matmul_t(keys, query)
            last = jnp.where(allowed, scores[early:], NEGATIVE)
            scores = jnp.concatenate([scores[:early], last], axis=0) if early else last
            exponent = jnp.exp(scores - jnp.max(scores, axis=0, keepdims=True))
            probs = exponent * (1.0 / jnp.sum(exponent, axis=0, keepdims=True))
            dprobs = matmul_t(values, grad)
            dscores = probs * (dprobs - jnp.sum(probs * dprobs, axis=0, keepdims=True))
            dscores = dscores.astype(BF16)
            dvalues += jnp.dot(probs.astype(BF16), grad, preferred_element_type=F32)
            dkeys += jnp.dot(dscores, query, preferred_element_type=F32)
            dquery.append(outer_sum(dscores, keys) * SCALE)
        dq_ref[span, :] = jnp.concatenate(dquery, axis=1)
        both = jnp.concatenate([dkeys, dvalues], axis=1)
        for s in range(stretch + 1):
            for side in range(2):
                piece = both[(2 * s + side) * rows : (2 * s + side + 1) * rows]
                sums[s, side] = sums[s, side] + piece if (s, side) in sums else piece
    for (s, side), value in sums.items():
        out = (down_ref, dpeer_ref)[side]
        out[s * rows : (s + 1) * rows, :] = value.astype(out.dtype)


def attend_back(part, query, own, peer, grad, rows, stretches, groups):
    tokens = query.shape[0]
    count = len(groups)
    column = lambda g: (0, g + groups.start)
    shape = lambda kind: jax.ShapeDtypeStruct((tokens, count * PAIR), kind)
    return pl.pallas_call(
        functools.partial(attend_back_kernel, rows, stretches),
        grid=(count,),
        in_specs=[pl.BlockSpec(memory_space=pltpu.SMEM)]
        + [pl.BlockSpec((tokens, PAIR), column)] * 4,
        out_specs=[pl.BlockSpec((tokens, PAIR), lambda g: (0, g))] * 3,
        out_shape=[shape(F32), shape(F32), shape(BF16)],
        compiler_params=params(),
        cost_estimate=light(),
    )(part, query, own, peer, grad)


def project_back_kernel(
    raw_ref, dq_ref, own_ref, recv_ref, cos_ref, sin_ref, gain_ref, w_ref, pack_ref, normed_ref, head_ref
):
    first = pl.program_id(0) == 0
    grads = []
    for part in range(2):
        vec = raw_ref[:, part * PAIR : (part + 1) * PAIR].astype(F32)
        if part == 0:
            grad = dq_ref[...]
        else:
            grad = own_ref[...] + recv_ref[...].astype(F32)
        gain = gain_ref[part : part + 1, :]
        scale = lax.rsqrt(group_mean(vec * vec) + EPSILON)
        turned = grad * cos_ref[...] - lane_swap(grad) * sin_ref[...]
        gain_sum = jnp.sum(turned * vec * scale, axis=0, keepdims=True)
        inner = turned * gain
        back = scale * (inner - vec * scale * scale * group_mean(inner * vec))
        if part == 1:
            lane = lax.broadcasted_iota(jnp.int32, vec.shape, 1)
            back = jnp.where(lane < HEAD, back, grad)
        back = back.astype(BF16)
        pack_ref[:, part * PAIR : (part + 1) * PAIR] = back
        grads.append((back, gain_sum))
    total = matmul_t(grads[0][0], w_ref[:, :PAIR]) + matmul_t(grads[1][0], w_ref[:, PAIR:])

    @pl.when(first)
    def _():
        normed_ref[...] = total
        head_ref[...] = jnp.zeros_like(head_ref)

    @pl.when(jnp.logical_not(first))
    def _():
        normed_ref[...] += total

    for part in range(2):
        head_ref[part : part + 1, :] += grads[part][1]


def project_back(raw, dquery, own, recv, cosine, sine, gain_rows, weight):
    tokens = raw.shape[0]
    width = weight.shape[0]
    whole = lambda g: (0, 0)
    column = lambda g: (0, g)
    return pl.pallas_call(
        project_back_kernel,
        grid=(KV_HEADS,),
        in_specs=[
            pl.BlockSpec((tokens, GROUP), column),
            pl.BlockSpec((tokens, PAIR), column),
            pl.BlockSpec((tokens, PAIR), column),
            pl.BlockSpec((tokens, PAIR), column),
            pl.BlockSpec((tokens, PAIR), whole),
            pl.BlockSpec((tokens, PAIR), whole),
            pl.BlockSpec((8, PAIR), whole),
            pl.BlockSpec((width, GROUP), column),
        ],
        out_specs=[
            pl.BlockSpec((tokens, GROUP), column),
            pl.BlockSpec((tokens, width), whole),
            pl.BlockSpec((8, PAIR), whole),
        ],
        out_shape=[
            jax.ShapeDtypeStruct((tokens, KV_HEADS * GROUP), BF16),
            jax.ShapeDtypeStruct((tokens, width), F32),
            jax.ShapeDtypeStruct((8, PAIR), F32),
        ],
        compiler_params=params(),
        cost_estimate=light(),
    )(raw, dquery, own, recv, cosine, sine, gain_rows, weight)


LANES = 128


def wide(ref, columns):
    if len(ref.shape) == 2:
        return ref[...]
    count = columns // LANES
    rows = ref.shape[1] // count
    parts = [ref[:, i * rows : (i + 1) * rows, :].reshape(-1, LANES) for i in range(count)]
    return jnp.concatenate(parts, axis=1)


def forward_kernel(x_ref, base_ref, g_ref, u_ref, d_ref, out_ref, act_ref, one_ref, two_ref):
    chunk, width = (act_ref.shape[1], out_ref.shape[1])
    gate_part, up_part, down_part = (wide(g_ref, chunk), wide(u_ref, chunk), wide(d_ref, width))
    down = 0.0
    for span in spans(act_ref.shape[1]):
        gate = jnp.dot(x_ref[...], gate_part[:, span], preferred_element_type=F32)
        upward = jnp.dot(x_ref[...], up_part[:, span], preferred_element_type=F32)
        sigma = jax.nn.sigmoid(gate)
        silu = gate * sigma
        active = (silu * upward).astype(BF16)
        act_ref[:, span] = active
        one_ref[:, span] = (upward * sigma * (1.0 + gate * (1.0 - sigma))).astype(BF16)
        two_ref[:, span] = silu.astype(BF16)
        down += jnp.dot(active, down_part[span], preferred_element_type=F32)

    @pl.when(pl.program_id(0) == 0)
    def _():
        out_ref[...] = base_ref[...] + down

    @pl.when(pl.program_id(0) > 0)
    def _():
        out_ref[...] += down


def store_outer(left_ref, dgate, dup, span, outs):
    half = left_ref.shape[0] // 2
    for right, leave_ref, stay_ref in ((dgate, *outs[:2]), (dup, *outs[2:])):
        product = jnp.dot(left_ref[...], right, preferred_element_type=F32).astype(BF16)
        leave_ref[:, span] = product[:half]
        stay_ref[:, span] = product[half:]


def backward_outer_kernel(grad_ref, left_ref, one_ref, two_ref, g_ref, u_ref, d_ref, out_ref, *outs):
    chunk, width = (one_ref.shape[1], out_ref.shape[1])
    gate_part, up_part, down_part = (wide(g_ref, chunk), wide(u_ref, chunk), wide(d_ref, width))
    total = 0.0
    for span in spans(one_ref.shape[1]):
        active = matmul_t(grad_ref[...], down_part[span])
        dgate = (active * one_ref[:, span].astype(F32)).astype(BF16)
        dup = (active * two_ref[:, span].astype(F32)).astype(BF16)
        store_outer(left_ref, dgate, dup, span, outs)
        total += matmul_t(dgate, gate_part[:, span]) + matmul_t(dup, up_part[:, span])

    @pl.when(pl.program_id(0) == 0)
    def _():
        out_ref[...] = total

    @pl.when(pl.program_id(0) > 0)
    def _():
        out_ref[...] += total


def outer_kernel(left_ref, dg_ref, du_ref, *outs):
    store_outer(left_ref, dg_ref[...], du_ref[...], slice(None), outs)


def both_ways_kernel(x_ref, grad_ref, g_ref, u_ref, d_ref, out_ref, act_ref, dg_ref, du_ref):
    chunk, width = (act_ref.shape[1], out_ref.shape[1])
    gate_part, up_part, down_part = (wide(g_ref, chunk), wide(u_ref, chunk), wide(d_ref, width))
    total = 0.0
    for span in spans(act_ref.shape[1]):
        gate = jnp.dot(x_ref[...], gate_part[:, span], preferred_element_type=F32)
        upward = jnp.dot(x_ref[...], up_part[:, span], preferred_element_type=F32)
        dactive = matmul_t(grad_ref[...], down_part[span])
        sigma = jax.nn.sigmoid(gate)
        silu = gate * sigma
        act_ref[:, span] = (silu * upward).astype(BF16)
        dgate = (dactive * upward * sigma * (1.0 + gate * (1.0 - sigma))).astype(BF16)
        dup = (dactive * silu).astype(BF16)
        dg_ref[:, span] = dgate
        du_ref[:, span] = dup
        total += matmul_t(dgate, gate_part[:, span]) + matmul_t(dup, up_part[:, span])

    @pl.when(pl.program_id(0) == 0)
    def _():
        out_ref[...] = total

    @pl.when(pl.program_id(0) > 0)
    def _():
        out_ref[...] += total


def down_kernel(base_ref, act_ref, d_ref, out_ref):
    down = jnp.dot(act_ref[...], wide(d_ref, out_ref.shape[1]), preferred_element_type=F32)

    @pl.when(pl.program_id(0) == 0)
    def _():
        out_ref[...] = base_ref[...] + down

    @pl.when(pl.program_id(0) > 0)
    def _():
        out_ref[...] += down


def spans(chunk):
    starts = list(range(0, max(chunk - 511, 1), 512))
    return [slice(a, b) for a, b in zip(starts, starts[1:] + [chunk])]


def sub_chunk(chunk):
    return next(size for size in (512, 384, 256, 128, chunk) if chunk % size == 0)


CHUNKS = 4


def can_pack(devices, width, hidden):
    gate_rows, down_rows = (width // devices, hidden // devices)
    return (
        devices % CHUNKS == 0
        and hidden % (CHUNKS * LANES) == 0
        and width % LANES == 0
        and gate_rows % 16 == 0
        and down_rows % 16 == 0
    )


def pack_halves(gate, upward, down):
    cut = lambda w: jnp.transpose(w.reshape(w.shape[0], -1, LANES), (1, 0, 2)).reshape(-1, LANES)
    return jnp.concatenate([cut(gate), cut(upward), cut(down)], axis=0)


def weight_specs(weights, tokens, width, hidden):
    if len(weights) == 3:
        chunk = sub_chunk(hidden)
        column = lambda j: (0, j)
        return (
            chunk,
            [
                pl.BlockSpec((width, chunk), column),
                pl.BlockSpec((width, chunk), column),
                pl.BlockSpec((chunk, width), lambda j: (j, 0)),
            ],
            weights,
        )
    devices = weights[0].shape[0]
    chunk = hidden // CHUNKS
    tall = width // devices * (hidden // LANES)
    piece = tall // CHUNKS
    return (
        chunk,
        [
            pl.BlockSpec((devices, piece, LANES), lambda j: (0, j, 0)),
            pl.BlockSpec((devices, piece, LANES), lambda j: (0, CHUNKS + j, 0)),
            pl.BlockSpec((devices // CHUNKS, tall, LANES), lambda j: (j, 2, 0)),
        ],
        (weights[0],) * 3,
    )


def ff_forward(normed, base, weights, hidden):
    tokens, width = normed.shape
    chunk, specs, operands = weight_specs(weights, tokens, width, hidden)
    whole = lambda j: (0, 0)
    column = lambda j: (0, j)
    saved = jax.ShapeDtypeStruct((tokens, hidden), BF16)
    return pl.pallas_call(
        forward_kernel,
        grid=(hidden // chunk,),
        in_specs=[pl.BlockSpec((tokens, width), whole), pl.BlockSpec((tokens, width), whole)]
        + specs,
        out_specs=[pl.BlockSpec((tokens, width), whole)]
        + [pl.BlockSpec((tokens, chunk), column)] * 3,
        out_shape=[jax.ShapeDtypeStruct((tokens, width), F32), saved, saved, saved],
        compiler_params=params(),
        cost_estimate=light(),
    )(normed, base, *operands)


def ff_both_ways(normed, grad, weights, hidden):
    tokens, width = normed.shape
    chunk, specs, operands = weight_specs(weights, tokens, width, hidden)
    whole = lambda j: (0, 0)
    column = lambda j: (0, j)
    saved = jax.ShapeDtypeStruct((tokens, hidden), BF16)
    return pl.pallas_call(
        both_ways_kernel,
        grid=(hidden // chunk,),
        in_specs=[pl.BlockSpec((tokens, width), whole), pl.BlockSpec((tokens, width), whole)]
        + specs,
        out_specs=[pl.BlockSpec((tokens, width), whole)]
        + [pl.BlockSpec((tokens, chunk), column)] * 3,
        out_shape=[jax.ShapeDtypeStruct((tokens, width), F32), saved, saved, saved],
        compiler_params=params(),
        cost_estimate=light(),
    )(normed, grad, *operands)


def ff_down(base, active, weights, hidden):
    tokens, width = base.shape
    chunk, specs, operands = weight_specs(weights, tokens, width, hidden)
    whole = lambda j: (0, 0)
    return pl.pallas_call(
        down_kernel,
        grid=(hidden // chunk,),
        in_specs=[
            pl.BlockSpec((tokens, width), whole),
            pl.BlockSpec((tokens, chunk), lambda j: (0, j)),
            specs[2],
        ],
        out_specs=pl.BlockSpec((tokens, width), whole),
        out_shape=jax.ShapeDtypeStruct((tokens, width), F32),
        compiler_params=params(),
        cost_estimate=light(),
    )(base, active, operands[2])


def ff_backward_outer(grad, left, one, two, weights, hidden):
    tokens, width = grad.shape
    chunk, specs, operands = weight_specs(weights, tokens, width, hidden)
    whole = lambda j: (0, 0)
    column = lambda j: (0, j)
    half = left.shape[0] // 2
    return pl.pallas_call(
        backward_outer_kernel,
        grid=(hidden // chunk,),
        in_specs=[
            pl.BlockSpec((tokens, width), whole),
            pl.BlockSpec(left.shape, whole),
            pl.BlockSpec((tokens, chunk), column),
            pl.BlockSpec((tokens, chunk), column),
        ]
        + specs,
        out_specs=[pl.BlockSpec((tokens, width), whole)]
        + [pl.BlockSpec((half, chunk), column)] * 4,
        out_shape=[jax.ShapeDtypeStruct((tokens, width), F32)]
        + [jax.ShapeDtypeStruct((half, hidden), BF16)] * 4,
        compiler_params=params(),
        cost_estimate=light(),
    )(grad, left, one, two, *operands)


def ff_outer(left, dgate, dup):
    tokens, hidden = dgate.shape
    chunk = sub_chunk(hidden)
    column = lambda j: (0, j)
    half = left.shape[0] // 2
    return pl.pallas_call(
        outer_kernel,
        grid=(hidden // chunk,),
        in_specs=[pl.BlockSpec(left.shape, lambda j: (0, 0))]
        + [pl.BlockSpec((tokens, chunk), column)] * 2,
        out_specs=[pl.BlockSpec((half, chunk), column)] * 4,
        out_shape=[jax.ShapeDtypeStruct((half, hidden), BF16)] * 4,
        compiler_params=params(),
        cost_estimate=light(),
    )(left, dgate, dup)


def local(
    tokens,
    cotangent,
    norm_gains,
    head_gains,
    conv_kernel,
    mix_in,
    mix_out,
    w_gate,
    w_up,
    w_down,
    conv_c,
):
    first = lax.axis_index("section") == 0
    part = lax.axis_index("seq")
    place = lax.axis_index("fsdp")
    fsdp = lax.axis_size("fsdp")
    chips = fsdp // 2
    chip, core = (place // 2, place % 2)
    stretches, rows, width = tokens.shape[1:]
    hidden = w_gate.shape[2]
    total = stretches * rows
    block = 2 * rows
    gains = norm_gains[0]

    cores = [(i, i ^ 1) for i in range(fsdp)]
    swap = [(0, 1), (1, 0)]

    def after(value, *earlier):
        return lax.optimization_barrier((value, *earlier))[0] if earlier else value

    def to_core(value):
        return lax.ppermute(value, "fsdp", cores)

    def to_peer(value):
        return lax.ppermute(value, "seq", swap)

    def exchange(value, offset):
        return lax.ppermute(value, "fsdp", [(i, i ^ offset) for i in range(fsdp)])

    def gather(shards):
        results = []
        for shard in shards:
            depth, columns = shard.shape
            half = depth // 2
            mine = lax.dynamic_slice_in_dim(shard, part * half, half, 0)
            if results:
                mine = after(mine, results[-1])
            batches = [([0], mine[None])]
            for bit in reversed(range(chips.bit_length() - 1)):
                offsets = [offset ^ (1 << bit) for known, rows_of in batches for offset in known]
                block_of = jnp.concatenate([rows_of for known, rows_of in batches], axis=0)
                batches.append((offsets, exchange(block_of, 2 << bit)))
            arrived = batches[1:]
            held = jnp.zeros((chips, 2, half, columns), BF16)
            held = lax.dynamic_update_slice(
                held, shard.reshape(1, 2, half, columns), (chip, 0, 0, 0)
            )
            for known, near in arrived:
                far = to_peer(near)
                for index, offset in enumerate(known):
                    for value, where in ((near, part), (far, 1 - part)):
                        held = lax.dynamic_update_slice(
                            held, value[index][None, None], (chip ^ offset, where, 0, 0)
                        )
            other = to_core(held)
            full = jnp.broadcast_to(held[:, None], (chips, 2, 2, half, columns))
            full = lax.dynamic_update_slice(full, other[:, None], (0, 1 - core, 0, 0, 0))
            results.append(full.reshape(fsdp * depth, columns))
        return results

    def turned(value):
        cut = value.shape[1] // (2 * fsdp)
        wide = value.reshape(value.shape[0], 2, chips, 2, cut)
        sides = [
            lax.dynamic_index_in_dim(wide, side, 3, keepdims=False) for side in (1 - core, core)
        ]
        return jnp.concatenate(
            [jnp.transpose(side.reshape(-1, 2 * chips * cut)) for side in sides], axis=0
        )

    def blocks(both):
        return both.astype(BF16).reshape(2, chips, -1, both.shape[1])

    def core_sum(left, right):
        half = left.shape[0] // 2
        leaving = matmul(left[:half], right).astype(BF16)
        return blocks(matmul(left[half:], right) + to_core(leaving).astype(F32))

    def core_add(leaving, staying):
        return blocks(staying.astype(F32) + leaving.astype(F32))

    def sides(both):
        return [
            lax.dynamic_index_in_dim(both, side, 0, keepdims=False) for side in (1 - part, part)
        ]

    def crossed(staying, came):
        return (staying.astype(F32) + came.astype(F32)).astype(BF16)

    def fence(*groups):
        return lax.optimization_barrier(groups)

    def together(values, *others):
        return lax.optimization_barrier((*values, *others))[: len(values)]

    def zeros(*shape, kind=BF16):
        return jnp.zeros(shape, kind)

    conv_cut = width // (4 * fsdp)
    c_low = lax.ppermute(conv_c, "section", [(0, 1)])

    def half_of(shard):
        return lax.dynamic_slice_in_dim(shard, part * (shard.shape[0] // 2), shard.shape[0] // 2, 0)

    halves = (half_of(w_gate[0]), half_of(w_up[0]), half_of(w_down[0]))
    if can_pack(2 * fsdp, width, hidden):
        wide_weights = (lax.all_gather(pack_halves(*halves), ("fsdp", "seq"), axis=0),)
    else:
        wide_weights = tuple(
            lax.all_gather(half, ("fsdp", "seq"), axis=0, tiled=True) for half in halves
        )

    positions = (
        jnp.arange(stretches)[:, None] * block + part * rows + jnp.arange(rows)[None, :]
    ).reshape(total)
    part_ref = part.astype(jnp.int32).reshape(1)

    def rope():
        lane = jnp.arange(PAIR)
        frequency = THETA ** (-(lane % (HEAD // 2)).astype(F32) * 2.0 / HEAD)
        angle = positions.astype(F32)[:, None] * frequency[None, :]
        sign = jnp.where(lane % HEAD < HEAD // 2, -1.0, 1.0)
        return (jnp.cos(angle), jnp.sin(angle) * sign[None, :])

    def gain_rows():
        return jnp.zeros((8, PAIR), F32).at[:2].set(jnp.tile(head_gains, (1, 2)))

    def attention_mixer():
        w_in, w_out = gather((mix_in[0], mix_out[0]))
        source = tokens[0].reshape(total, width).astype(F32)
        normed = (source * rms_scale(source) * gains[0]).astype(BF16)
        cosine, sine = rope()
        raw, query, own = project(normed, w_in, cosine, sine, gain_rows())
        peer = to_peer(own)
        heads = attend(part_ref, query, own, peer, rows, stretches)
        resid = source + matmul(heads, w_out)
        normed_two = (resid * rms_scale(resid) * gains[1]).astype(BF16)
        weights = (w_in, w_out, zeros(width, width))
        kept = (normed, raw, query, own, peer, heads, resid, normed_two)
        return (weights, kept, cosine, sine)

    def conv_gather():
        both = jnp.concatenate([c_low, conv_c], axis=1)
        w_in, c_wide, w_out = gather((mix_in[0], both, mix_out[0]))
        w_c = jnp.concatenate([c_wide[:, :width], c_wide[:, width:]], axis=0)
        flat = lambda: zeros(total, width)
        kept = (
            flat(), zeros(total, KV_HEADS * GROUP), flat(), flat(), flat(), flat(),
            zeros(total, width, kind=F32), flat(),
        )
        table = lambda: zeros(total, PAIR, kind=F32)
        return ((w_in, w_out, w_c), kept, table(), table())

    weights, kept, cosine, sine = lax.cond(first, attention_mixer, conv_gather)

    def attention_hidden():
        result, *saved = ff_forward(kept[-1], kept[-2], wide_weights, hidden)
        return (result.astype(BF16), *saved)

    def conv_wait():
        return (zeros(total, width), *[zeros(total, hidden) for _ in range(3)])

    link, active, one, two = lax.cond(first, attention_hidden, conv_wait)
    link = lax.ppermute(link, "section", [(0, 1)])

    def tail_of(value, start):
        return to_peer(value.reshape(stretches, rows, width)[:, start : start + 2])

    def conv_both():
        w_in, w_out, w_c = weights
        source = link.astype(F32)
        scale_one = rms_scale(source)
        normed = (source * scale_one * gains[0]).astype(BF16)
        pair = matmul(normed, w_in)
        left, right = (pair[:, :width], pair[:, width:])
        product = (left * right).astype(BF16)
        tails = tail_of(product, rows - 2).astype(F32)
        conv_gate = matmul(normed, w_c).astype(BF16).astype(F32)
        early = jnp.concatenate([jnp.zeros_like(tails[:1]), tails[:-1]], axis=0)
        before = jnp.where(part == 0, early, tails)
        inner = product.astype(F32).reshape(stretches, rows, width)
        longer = jnp.concatenate([before, inner], axis=1)
        taps = [longer[:, i : i + rows] for i in range(3)]
        state = sum(conv_kernel[i] * taps[i] for i in range(3)).reshape(total, width)
        heads = (conv_gate * state).astype(BF16)
        resid = source + matmul(heads, w_out)
        scale_two = rms_scale(resid)
        normed_two = (resid * scale_two * gains[1]).astype(BF16)
        grad_ff = cotangent[0].reshape(total, width)
        grad_two, active, dgate, dup = ff_both_ways(normed_two, grad_ff, wide_weights, hidden)
        gain_two = jnp.sum(grad_two * resid * scale_two, axis=0)
        grad_resid = grad_ff.astype(F32) + norm_back(grad_two, resid, scale_two, gains[1])
        dmix = grad_resid.astype(BF16)
        dheads = matmul_t(dmix, w_out).astype(BF16).astype(F32)
        dgate_c = (dheads * state).astype(BF16)
        dstate = (dheads * conv_gate).reshape(stretches, rows, width)
        fronts = tail_of(dstate, 0)
        late = jnp.concatenate([fronts[1:], jnp.zeros_like(fronts[:1])], axis=0)
        after = jnp.where(part == 0, fronts, late)
        further = jnp.concatenate([dstate, after], axis=1)
        dproduct = sum(conv_kernel[2 - i] * further[:, i : i + rows] for i in range(3))
        dproduct = dproduct.reshape(total, width).astype(BF16).astype(F32)
        kernel_grad = jnp.stack([jnp.sum(dstate * taps[i], axis=(0, 1)) for i in range(3)])
        dproj = jnp.concatenate([dproduct * right, dproduct * left], axis=1).astype(BF16)
        grad_one = matmul_t(dproj, w_in) + matmul_t(dgate_c, w_c)
        gain_one = jnp.sum(grad_one * source * scale_one, axis=0)
        grad_source = grad_resid + norm_back(grad_one, source, scale_one, gains[0])
        small = jnp.concatenate(
            [jnp.zeros((2, width), F32), gain_one[None], gain_two[None], kernel_grad,
             jnp.zeros((1, width), F32)], axis=0
        )
        lefts = (normed, heads, normed_two, active)
        moved = (dproj, dgate_c, dmix, dgate, dup)
        return (resid, lefts, moved, small, grad_source.astype(BF16))

    def attention_idle():
        flat = lambda: zeros(total, width)
        wide = lambda: zeros(total, hidden)
        lefts = (kept[0], kept[5], kept[7], active)
        moved = (zeros(total, 2 * width), flat(), flat(), wide(), wide())
        back = cotangent[0].reshape(total, width)
        return (zeros(total, width, kind=F32), lefts, moved, zeros(8, width, kind=F32), back)

    conv_resid, lefts, moved, conv_small, grad_link = lax.cond(first, attention_idle, conv_both)
    normed, heads, normed_two, active_both = together(lefts, grad_link)
    grad_ff = lax.ppermute(grad_link, "section", swap)
    conv_dproj, dgate_c, conv_dmix, conv_dgate, conv_dup = moved
    left_down, left_two, left_heads, left_normed = [
        turned(value) for value in (active_both, normed_two, heads, normed)
    ]
    middle = width // 2
    down = [
        sides(core_sum(left_down, grad_ff[:, cut]))
        for cut in (slice(0, middle), slice(middle, None))
    ]
    groups = [[i for i in range(fsdp) if i % 2 == side] for side in range(2)]

    def cross(half):
        return to_peer(half[0])

    def along_all(own):
        return [lax.all_to_all(own, "fsdp", 0, 0, axis_index_groups=groups, tiled=True)]

    class Halving:
        def __init__(self, own):
            self.held, self.bit = (own, 0)
            self.split()

        def split(self):
            count, *shape = self.held.shape
            wide = self.held.reshape(count // 2, 2, *shape)
            side = (chip >> self.bit) % 2
            self.leaving, self.staying = [
                lax.dynamic_index_in_dim(wide, which, 1, keepdims=False)
                for which in (1 - side, side)
            ]

        def send(self):
            return exchange(self.leaving, 2 << self.bit)

        def add(self, came):
            last = self.staying.shape[0] == 1
            self.held = self.staying.astype(F32) + came.astype(F32)
            self.bit += 1
            if not last:
                self.held = self.held.astype(BF16)
                self.split()
            return self

    def scattered(came):
        return sum(jnp.sum(part.astype(F32), axis=0) for part in came)

    def halves_of(leaving, staying):
        return sides(core_add(to_core(leaving), staying))

    def attention_ff():
        grad_two, *products = ff_backward_outer(grad_ff, left_two, one, two, wide_weights, hidden)
        return (grad_two, halves_of(*products[:2]), *products[2:])

    def conv_ff():
        products = ff_outer(left_two, conv_dgate, conv_dup)
        output = ff_down(conv_resid, active_both, wide_weights, hidden)
        return (output, halves_of(*products[:2]), *products[2:])

    step, down = fence(first, down)
    down_came = [cross(half) for half in down]
    result = lax.cond(step, attention_ff, conv_ff)
    down_came, (grad_two, gate, up_leaving, up_staying) = fence(down_came, result)

    def sum_down():
        return jnp.concatenate(
            [crossed(half[1], came) for half, came in zip(down, down_came)], axis=2
        )

    def attention_core():
        unused, raw, query, own, peer, unused, resid, unused = kept
        scale_two = rms_scale(resid)
        gain_two = jnp.sum(grad_two * resid * scale_two, axis=0)
        grad_resid = grad_ff.astype(F32) + norm_back(grad_two, resid, scale_two, gains[1])
        dmix = grad_resid.astype(BF16)
        dheads = matmul_t(dmix, weights[1]).astype(BF16)
        up, dheads, own_down = fence(halves_of(up_leaving, up_staying), dheads, sum_down())
        came = along_all(own_down)
        half = KV_HEADS // 2
        back = functools.partial(attend_back, part_ref, query, own, peer)
        low, dheads = fence(back(dheads, rows, stretches, range(half)), dheads)
        low_recv = to_peer(low[2])
        low_recv, high = fence(low_recv, back(dheads, rows, stretches, range(half, KV_HEADS)))
        high_recv = to_peer(high[2])
        dquery, down_kv = [jnp.concatenate([low[i], high[i]], axis=1) for i in range(2)]
        recv = jnp.concatenate([low_recv, high_recv], axis=1)
        came, recv = fence(came, recv)
        shard = scattered(came)
        blank = zeros(2 * conv_cut, width, kind=F32)
        return (shard, up, gain_two, grad_resid, dmix, dquery, down_kv, recv, blank)

    def conv_core():
        mixed = normed.reshape(total, 2, 2 * fsdp, conv_cut)
        mixed = jnp.transpose(mixed, (0, 2, 1, 3)).reshape(total, width)
        lone = sides(core_sum(turned(mixed), dgate_c))
        came = along_all(sum_down())
        blanks = [zeros(total, width, kind=kind) for kind in (F32, F32, BF16)]
        up = halves_of(up_leaving, up_staying)
        peer, up, blanks, output = fence(to_peer(lone[0]), up, blanks, grad_two)
        came, lone = fence(came, crossed(lone[1], peer))
        shard, lone = (scattered(came), scattered(along_all(lone)))
        return (shard, up, zeros(width, kind=F32), output, conv_dmix, *blanks, lone)

    step, gate = fence(first, gate)
    gate_came = cross(gate)
    result = lax.cond(step, attention_core, conv_core)
    gate_came, result = fence(gate_came, result)
    shard_down, up, gain_two, grad_resid, dmix, dquery, down_kv, recv, lone = result

    def attention_project():
        dproj, grad_one, head_rows = project_back(
            kept[1], dquery, down_kv, recv, cosine, sine, gain_rows(), weights[0]
        )
        inward = sides(core_sum(left_normed, dproj))
        outward = sides(core_sum(left_heads, dmix))
        source = tokens[0].reshape(total, width).astype(F32)
        scale_one = rms_scale(source)
        gain_one = jnp.sum(grad_one * source * scale_one, axis=0)
        grad_source = grad_resid + norm_back(grad_one, source, scale_one, gains[0])
        head_grad = jnp.stack([head_rows[0, :HEAD] + head_rows[0, HEAD:], head_rows[1, :HEAD]])
        head_row = jnp.pad(head_grad.reshape(1, PAIR), ((0, 0), (0, width - PAIR)))
        small = jnp.concatenate(
            [gain_one[None], gain_two[None], jnp.zeros((5, width), F32), head_row], axis=0
        )
        return ([inward, outward], grad_source, small + to_core(small))

    def conv_project():
        outward = sides(core_sum(left_heads, dmix))
        inward = sides(core_sum(left_normed, conv_dproj))
        output = grad_resid
        small = conv_small + to_core(conv_small)
        return ([inward, outward], output, small)

    gate = crossed(gate[1], gate_came)
    step, gate, up = fence(first, gate, up)
    gate_came, up_came = (along_all(gate), cross(up))
    result = lax.cond(step, attention_project, conv_project)
    gate_came, up_came, result = fence(gate_came, up_came, result)
    mix, ends, small = result

    up = Halving(crossed(up[1], up_came))
    mix_came = [cross(half) for half in mix]
    up_came = up.send()
    up_came, small_came = fence(up_came, to_peer(small))
    up, small = (up.add(up_came), small + small_came)
    small_came = exchange(small, 2)
    bits = chips.bit_length() - 1
    for bit in range(1, bits):
        if bit == 1:
            mix_came, small_came = fence(mix_came, small_came)
            mix = [Halving(crossed(half[1], came)) for half, came in zip(mix, mix_came)]
            small = small + small_came
            mix_came, small_came = ([half.send() for half in mix], exchange(small, 4))
        up_came = up.send()
        up_came, mix_came, small_came = fence(up_came, mix_came, small_came)
        up = up.add(up_came)
        mix = [half.add(came) for half, came in zip(mix, mix_came)]
        small = small + small_came
        mix_came = [half.send() for half in mix]
        if bit < bits - 1:
            small_came = exchange(small, 4 << bit)
    mail = lax.ppermute(jnp.concatenate([small, lone[:conv_cut]], axis=0), "section", swap)
    mix_came, mail = fence(mix_came, mail)
    small = small + mail[: small.shape[0]]
    c_shard = jnp.where(first, mail[small.shape[0] :], lone[conv_cut:])
    shard_in, shard_out = [half.add(came).held[0] for half, came in zip(mix, mix_came)]
    shards_out = (
        shard_in, shard_out,
        scattered(gate_came), up.held[0], shard_down,
    )
    return (
        ends.reshape(1, 1, stretches, rows, width),
        small[:4].reshape(2, 2, width),
        small[7, :PAIR].reshape(2, HEAD),
        small[4:7],
        *[shard[None] for shard in shards_out],
        c_shard,
    )


def solution(mesh):
    return jax.shard_map(
        local,
        mesh=mesh,
        in_specs=(
            P("fsdp", None, "seq", None),
            P("fsdp", None, "seq", None),
            P("section", None, None),
            P(),
            P(),
            P("section", "fsdp", None),
            P("section", "fsdp", None),
            P("section", "fsdp", None),
            P("section", "fsdp", None),
            P("section", "fsdp", None),
            P(("section", "fsdp"), None),
        ),
        out_specs=(
            P("section", "fsdp", None, "seq", None),
            P(),
            P(),
            P(),
            P("section", ("seq", "fsdp"), None),
            P("section", ("seq", "fsdp"), None),
            P("section", ("seq", "fsdp"), None),
            P("section", ("seq", "fsdp"), None),
            P("section", ("seq", "fsdp"), None),
            P(("section", "seq", "fsdp"), None),
        ),
        check_vma=False,
    )
```

```python
import functools

import jax
import jax.numpy as jnp
from jax import lax
from jax.experimental import pallas as pl
from jax.experimental.pallas import tpu as pltpu
from jax.sharding import PartitionSpec as P

HEADS = 16
KV_HEADS = 8
HEAD = 64
PAIR = 2 * HEAD
GROUP = 2 * PAIR

EPSILON = 1e-05
THETA = 1000000.0
NEGATIVE = -1e30
SCALE = HEAD ** (-0.5)
BF16 = jnp.bfloat16
F32 = jnp.float32
VMEM_LIMIT = 56 * 1024 * 1024


def rms_scale(value):
    return lax.rsqrt(jnp.mean(value * value, axis=-1, keepdims=True) + EPSILON)


def norm_back(grad_out, value, scale, gain):
    inner = grad_out * gain
    return scale * (inner - value * scale * scale * jnp.mean(inner * value, axis=-1, keepdims=True))


def matmul(left, right):
    return jnp.dot(left, right, preferred_element_type=F32)


def matmul_t(left, right):
    return lax.dot_general(left, right, (((1,), (1,)), ((), ())), preferred_element_type=F32)


def outer_sum(left, right):
    return lax.dot_general(left, right, (((0,), (0,)), ((), ())), preferred_element_type=F32)


def params():
    return pltpu.CompilerParams(vmem_limit_bytes=VMEM_LIMIT)


def light():
    return pl.CostEstimate(flops=1 << 20, bytes_accessed=1 << 20, transcendentals=0)


def group_mean(value):
    row = lax.broadcasted_iota(jnp.int32, (PAIR, PAIR), 0) // HEAD
    col = lax.broadcasted_iota(jnp.int32, (PAIR, PAIR), 1) // HEAD
    ones = jnp.where(row == col, 1.0 / HEAD, 0.0).astype(F32)
    return jnp.dot(value, ones, precision=lax.Precision.HIGHEST, preferred_element_type=F32)


def lane_swap(value):
    lane = lax.broadcasted_iota(jnp.int32, value.shape, 1) % HEAD
    return jnp.where(
        lane < HEAD // 2, pltpu.roll(value, PAIR - HEAD // 2, 1), pltpu.roll(value, HEAD // 2, 1)
    )


def project_kernel(x_ref, w_ref, cos_ref, sin_ref, gain_ref, raw_ref, q_ref, kv_ref):
    raw = jnp.dot(x_ref[...], w_ref[...], preferred_element_type=F32).astype(BF16)
    raw_ref[...] = raw
    for part, out in ((0, q_ref), (1, kv_ref)):
        vec = raw[:, part * PAIR : (part + 1) * PAIR].astype(F32)
        normed = vec * lax.rsqrt(group_mean(vec * vec) + EPSILON) * gain_ref[part : part + 1, :]
        turned = normed * cos_ref[...] + lane_swap(normed) * sin_ref[...]
        if part == 1:
            lane = lax.broadcasted_iota(jnp.int32, vec.shape, 1)
            turned = jnp.where(lane < HEAD, turned, vec)
        out[...] = turned.astype(BF16)


def project(normed, weight, cosine, sine, gain_rows):
    tokens, width = normed.shape
    whole = lambda g: (0, 0)
    column = lambda g: (0, g)
    return pl.pallas_call(
        project_kernel,
        grid=(KV_HEADS,),
        in_specs=[
            pl.BlockSpec((tokens, width), whole),
            pl.BlockSpec((width, GROUP), column),
            pl.BlockSpec((tokens, PAIR), whole),
            pl.BlockSpec((tokens, PAIR), whole),
            pl.BlockSpec((8, PAIR), whole),
        ],
        out_specs=[
            pl.BlockSpec((tokens, GROUP), column),
            pl.BlockSpec((tokens, PAIR), column),
            pl.BlockSpec((tokens, PAIR), column),
        ],
        out_shape=[
            jax.ShapeDtypeStruct((tokens, KV_HEADS * GROUP), BF16),
            jax.ShapeDtypeStruct((tokens, KV_HEADS * PAIR), BF16),
            jax.ShapeDtypeStruct((tokens, KV_HEADS * PAIR), BF16),
        ],
        compiler_params=params(),
        cost_estimate=light(),
    )(normed, weight, cosine, sine, gain_rows)


def attend_kernel(rows, stretches, part_ref, q_ref, own_ref, peer_ref, out_ref):
    second = part_ref[0] == 1
    for stretch in range(stretches):
        blocks = []
        for s in range(stretch + 1):
            blocks += [own_ref[s * rows : (s + 1) * rows, :], peer_ref[s * rows : (s + 1) * rows, :]]
        pack = jnp.concatenate(blocks, axis=0)
        keys, values = (pack[:, :HEAD], pack[:, HEAD:])
        early = stretch * 2 * rows
        row = lax.broadcasted_iota(jnp.int32, (rows, 2 * rows), 0)
        col = lax.broadcasted_iota(jnp.int32, (rows, 2 * rows), 1)
        allowed = (col <= row) | ((col >= rows) & second)
        for j in range(2):
            query = q_ref[stretch * rows : (stretch + 1) * rows, j * HEAD : (j + 1) * HEAD]
            scores = matmul_t(query * SCALE, keys)
            last = jnp.where(allowed, scores[:, early:], NEGATIVE)
            scores = jnp.concatenate([scores[:, :early], last], axis=1) if early else last
            exponent = jnp.exp(scores - jnp.max(scores, axis=1, keepdims=True))
            total = jnp.sum(exponent, axis=1, keepdims=True)
            probs = (exponent * (1.0 / total)).astype(BF16)
            out_ref[stretch * rows : (stretch + 1) * rows, j * HEAD : (j + 1) * HEAD] = jnp.dot(
                probs, values, preferred_element_type=F32
            ).astype(BF16)


def attend(part, query, own, peer, rows, stretches):
    tokens = query.shape[0]
    column = lambda g: (0, g)
    return pl.pallas_call(
        functools.partial(attend_kernel, rows, stretches),
        grid=(KV_HEADS,),
        in_specs=[pl.BlockSpec(memory_space=pltpu.SMEM)]
        + [pl.BlockSpec((tokens, PAIR), column)] * 3,
        out_specs=pl.BlockSpec((tokens, PAIR), column),
        out_shape=jax.ShapeDtypeStruct((tokens, KV_HEADS * PAIR), BF16),
        compiler_params=params(),
        cost_estimate=light(),
    )(part, query, own, peer)


def attend_back_kernel(
    rows, stretches, part_ref, q_ref, own_ref, peer_ref, grad_ref, dq_ref, down_ref, dpeer_ref
):
    second = part_ref[0] == 1
    sums = {}
    for stretch in reversed(range(stretches)):
        blocks = []
        for s in range(stretch + 1):
            blocks += [own_ref[s * rows : (s + 1) * rows, :], peer_ref[s * rows : (s + 1) * rows, :]]
        pack = jnp.concatenate(blocks, axis=0)
        keys, values = (pack[:, :HEAD], pack[:, HEAD:])
        early = stretch * 2 * rows
        col = lax.broadcasted_iota(jnp.int32, (2 * rows, rows), 0)
        row = lax.broadcasted_iota(jnp.int32, (2 * rows, rows), 1)
        allowed = (col <= row) | ((col >= rows) & second)
        span = slice(stretch * rows, (stretch + 1) * rows)
        dkeys, dvalues, dquery = (0.0, 0.0, [])
        for j in range(2):
            query = q_ref[span, j * HEAD : (j + 1) * HEAD] * SCALE
            grad = grad_ref[span, j * HEAD : (j + 1) * HEAD]
            scores = matmul_t(keys, query)
            last = jnp.where(allowed, scores[early:], NEGATIVE)
            scores = jnp.concatenate([scores[:early], last], axis=0) if early else last
            exponent = jnp.exp(scores - jnp.max(scores, axis=0, keepdims=True))
            probs = exponent * (1.0 / jnp.sum(exponent, axis=0, keepdims=True))
            dprobs = matmul_t(values, grad)
            dscores = probs * (dprobs - jnp.sum(probs * dprobs, axis=0, keepdims=True))
            dscores = dscores.astype(BF16)
            dvalues += jnp.dot(probs.astype(BF16), grad, preferred_element_type=F32)
            dkeys += jnp.dot(dscores, query, preferred_element_type=F32)
            dquery.append(outer_sum(dscores, keys) * SCALE)
        dq_ref[span, :] = jnp.concatenate(dquery, axis=1)
        both = jnp.concatenate([dkeys, dvalues], axis=1)
        for s in range(stretch + 1):
            for side in range(2):
                piece = both[(2 * s + side) * rows : (2 * s + side + 1) * rows]
                sums[s, side] = sums[s, side] + piece if (s, side) in sums else piece
    for (s, side), value in sums.items():
        out = (down_ref, dpeer_ref)[side]
        out[s * rows : (s + 1) * rows, :] = value.astype(out.dtype)


def attend_back(part, query, own, peer, grad, rows, stretches, groups):
    tokens = query.shape[0]
    count = len(groups)
    column = lambda g: (0, g + groups.start)
    shape = lambda kind: jax.ShapeDtypeStruct((tokens, count * PAIR), kind)
    return pl.pallas_call(
        functools.partial(attend_back_kernel, rows, stretches),
        grid=(count,),
        in_specs=[pl.BlockSpec(memory_space=pltpu.SMEM)]
        + [pl.BlockSpec((tokens, PAIR), column)] * 4,
        out_specs=[pl.BlockSpec((tokens, PAIR), lambda g: (0, g))] * 3,
        out_shape=[shape(F32), shape(F32), shape(BF16)],
        compiler_params=params(),
        cost_estimate=light(),
    )(part, query, own, peer, grad)


def project_back_kernel(
    raw_ref, dq_ref, own_ref, recv_ref, cos_ref, sin_ref, gain_ref, w_ref, pack_ref, normed_ref, head_ref
):
    first = pl.program_id(0) == 0
    grads = []
    for part in range(2):
        vec = raw_ref[:, part * PAIR : (part + 1) * PAIR].astype(F32)
        if part == 0:
            grad = dq_ref[...]
        else:
            grad = own_ref[...] + recv_ref[...].astype(F32)
        gain = gain_ref[part : part + 1, :]
        scale = lax.rsqrt(group_mean(vec * vec) + EPSILON)
        turned = grad * cos_ref[...] - lane_swap(grad) * sin_ref[...]
        gain_sum = jnp.sum(turned * vec * scale, axis=0, keepdims=True)
        inner = turned * gain
        back = scale * (inner - vec * scale * scale * group_mean(inner * vec))
        if part == 1:
            lane = lax.broadcasted_iota(jnp.int32, vec.shape, 1)
            back = jnp.where(lane < HEAD, back, grad)
        back = back.astype(BF16)
        pack_ref[:, part * PAIR : (part + 1) * PAIR] = back
        grads.append((back, gain_sum))
    total = matmul_t(grads[0][0], w_ref[:, :PAIR]) + matmul_t(grads[1][0], w_ref[:, PAIR:])

    @pl.when(first)
    def _():
        normed_ref[...] = total
        head_ref[...] = jnp.zeros_like(head_ref)

    @pl.when(jnp.logical_not(first))
    def _():
        normed_ref[...] += total

    for part in range(2):
        head_ref[part : part + 1, :] += grads[part][1]


def project_back(raw, dquery, own, recv, cosine, sine, gain_rows, weight):
    tokens = raw.shape[0]
    width = weight.shape[0]
    whole = lambda g: (0, 0)
    column = lambda g: (0, g)
    return pl.pallas_call(
        project_back_kernel,
        grid=(KV_HEADS,),
        in_specs=[
            pl.BlockSpec((tokens, GROUP), column),
            pl.BlockSpec((tokens, PAIR), column),
            pl.BlockSpec((tokens, PAIR), column),
            pl.BlockSpec((tokens, PAIR), column),
            pl.BlockSpec((tokens, PAIR), whole),
            pl.BlockSpec((tokens, PAIR), whole),
            pl.BlockSpec((8, PAIR), whole),
            pl.BlockSpec((width, GROUP), column),
        ],
        out_specs=[
            pl.BlockSpec((tokens, GROUP), column),
            pl.BlockSpec((tokens, width), whole),
            pl.BlockSpec((8, PAIR), whole),
        ],
        out_shape=[
            jax.ShapeDtypeStruct((tokens, KV_HEADS * GROUP), BF16),
            jax.ShapeDtypeStruct((tokens, width), F32),
            jax.ShapeDtypeStruct((8, PAIR), F32),
        ],
        compiler_params=params(),
        cost_estimate=light(),
    )(raw, dquery, own, recv, cosine, sine, gain_rows, weight)


LANES = 128


def wide(ref, columns):
    if len(ref.shape) == 2:
        return ref[...]
    count = columns // LANES
    rows = ref.shape[1] // count
    parts = [ref[:, i * rows : (i + 1) * rows, :].reshape(-1, LANES) for i in range(count)]
    return jnp.concatenate(parts, axis=1)


def forward_kernel(x_ref, base_ref, g_ref, u_ref, d_ref, out_ref, act_ref, one_ref, two_ref):
    chunk, width = (act_ref.shape[1], out_ref.shape[1])
    gate_part, up_part, down_part = (wide(g_ref, chunk), wide(u_ref, chunk), wide(d_ref, width))
    down = 0.0
    for span in spans(act_ref.shape[1]):
        gate = jnp.dot(x_ref[...], gate_part[:, span], preferred_element_type=F32)
        upward = jnp.dot(x_ref[...], up_part[:, span], preferred_element_type=F32)
        sigma = jax.nn.sigmoid(gate)
        silu = gate * sigma
        active = (silu * upward).astype(BF16)
        act_ref[:, span] = active
        one_ref[:, span] = (upward * sigma * (1.0 + gate * (1.0 - sigma))).astype(BF16)
        two_ref[:, span] = silu.astype(BF16)
        down += jnp.dot(active, down_part[span], preferred_element_type=F32)

    @pl.when(pl.program_id(0) == 0)
    def _():
        out_ref[...] = base_ref[...] + down

    @pl.when(pl.program_id(0) > 0)
    def _():
        out_ref[...] += down


def store_outer(left_ref, dgate, dup, span, outs):
    half = left_ref.shape[0] // 2
    for right, leave_ref, stay_ref in ((dgate, *outs[:2]), (dup, *outs[2:])):
        product = jnp.dot(left_ref[...], right, preferred_element_type=F32).astype(BF16)
        leave_ref[:, span] = product[:half]
        stay_ref[:, span] = product[half:]


def backward_outer_kernel(grad_ref, left_ref, one_ref, two_ref, g_ref, u_ref, d_ref, out_ref, *outs):
    chunk, width = (one_ref.shape[1], out_ref.shape[1])
    gate_part, up_part, down_part = (wide(g_ref, chunk), wide(u_ref, chunk), wide(d_ref, width))
    total = 0.0
    for span in spans(one_ref.shape[1]):
        active = matmul_t(grad_ref[...], down_part[span])
        dgate = (active * one_ref[:, span].astype(F32)).astype(BF16)
        dup = (active * two_ref[:, span].astype(F32)).astype(BF16)
        store_outer(left_ref, dgate, dup, span, outs)
        total += matmul_t(dgate, gate_part[:, span]) + matmul_t(dup, up_part[:, span])

    @pl.when(pl.program_id(0) == 0)
    def _():
        out_ref[...] = total

    @pl.when(pl.program_id(0) > 0)
    def _():
        out_ref[...] += total


def outer_kernel(left_ref, dg_ref, du_ref, *outs):
    store_outer(left_ref, dg_ref[...], du_ref[...], slice(None), outs)


def both_ways_kernel(x_ref, grad_ref, g_ref, u_ref, d_ref, out_ref, act_ref, dg_ref, du_ref):
    chunk, width = (act_ref.shape[1], out_ref.shape[1])
    gate_part, up_part, down_part = (wide(g_ref, chunk), wide(u_ref, chunk), wide(d_ref, width))
    total = 0.0
    for span in spans(act_ref.shape[1]):
        gate = jnp.dot(x_ref[...], gate_part[:, span], preferred_element_type=F32)
        upward = jnp.dot(x_ref[...], up_part[:, span], preferred_element_type=F32)
        dactive = matmul_t(grad_ref[...], down_part[span])
        sigma = jax.nn.sigmoid(gate)
        silu = gate * sigma
        act_ref[:, span] = (silu * upward).astype(BF16)
        dgate = (dactive * upward * sigma * (1.0 + gate * (1.0 - sigma))).astype(BF16)
        dup = (dactive * silu).astype(BF16)
        dg_ref[:, span] = dgate
        du_ref[:, span] = dup
        total += matmul_t(dgate, gate_part[:, span]) + matmul_t(dup, up_part[:, span])

    @pl.when(pl.program_id(0) == 0)
    def _():
        out_ref[...] = total

    @pl.when(pl.program_id(0) > 0)
    def _():
        out_ref[...] += total


def down_kernel(base_ref, act_ref, d_ref, out_ref):
    down = jnp.dot(act_ref[...], wide(d_ref, out_ref.shape[1]), preferred_element_type=F32)

    @pl.when(pl.program_id(0) == 0)
    def _():
        out_ref[...] = base_ref[...] + down

    @pl.when(pl.program_id(0) > 0)
    def _():
        out_ref[...] += down


def spans(chunk):
    starts = list(range(0, max(chunk - 511, 1), 512))
    return [slice(a, b) for a, b in zip(starts, starts[1:] + [chunk])]


def sub_chunk(chunk):
    return next(size for size in (512, 384, 256, 128, chunk) if chunk % size == 0)


CHUNKS = 4


def can_pack(devices, width, hidden):
    gate_rows, down_rows = (width // devices, hidden // devices)
    return (
        devices % CHUNKS == 0
        and hidden % (CHUNKS * LANES) == 0
        and width % LANES == 0
        and gate_rows % 16 == 0
        and down_rows % 16 == 0
    )


def pack_halves(gate, upward, down):
    cut = lambda w: jnp.transpose(w.reshape(w.shape[0], -1, LANES), (1, 0, 2)).reshape(-1, LANES)
    return jnp.concatenate([cut(gate), cut(upward), cut(down)], axis=0)


def weight_specs(weights, tokens, width, hidden):
    if len(weights) == 3:
        chunk = sub_chunk(hidden)
        column = lambda j: (0, j)
        return (
            chunk,
            [
                pl.BlockSpec((width, chunk), column),
                pl.BlockSpec((width, chunk), column),
                pl.BlockSpec((chunk, width), lambda j: (j, 0)),
            ],
            weights,
        )
    devices = weights[0].shape[0]
    chunk = hidden // CHUNKS
    tall = width // devices * (hidden // LANES)
    piece = tall // CHUNKS
    return (
        chunk,
        [
            pl.BlockSpec((devices, piece, LANES), lambda j: (0, j, 0)),
            pl.BlockSpec((devices, piece, LANES), lambda j: (0, CHUNKS + j, 0)),
            pl.BlockSpec((devices // CHUNKS, tall, LANES), lambda j: (j, 2, 0)),
        ],
        (weights[0],) * 3,
    )


def ff_forward(normed, base, weights, hidden):
    tokens, width = normed.shape
    chunk, specs, operands = weight_specs(weights, tokens, width, hidden)
    whole = lambda j: (0, 0)
    column = lambda j: (0, j)
    saved = jax.ShapeDtypeStruct((tokens, hidden), BF16)
    return pl.pallas_call(
        forward_kernel,
        grid=(hidden // chunk,),
        in_specs=[pl.BlockSpec((tokens, width), whole), pl.BlockSpec((tokens, width), whole)]
        + specs,
        out_specs=[pl.BlockSpec((tokens, width), whole)]
        + [pl.BlockSpec((tokens, chunk), column)] * 3,
        out_shape=[jax.ShapeDtypeStruct((tokens, width), F32), saved, saved, saved],
        compiler_params=params(),
        cost_estimate=light(),
    )(normed, base, *operands)


def ff_both_ways(normed, grad, weights, hidden):
    tokens, width = normed.shape
    chunk, specs, operands = weight_specs(weights, tokens, width, hidden)
    whole = lambda j: (0, 0)
    column = lambda j: (0, j)
    saved = jax.ShapeDtypeStruct((tokens, hidden), BF16)
    return pl.pallas_call(
        both_ways_kernel,
        grid=(hidden // chunk,),
        in_specs=[pl.BlockSpec((tokens, width), whole), pl.BlockSpec((tokens, width), whole)]
        + specs,
        out_specs=[pl.BlockSpec((tokens, width), whole)]
        + [pl.BlockSpec((tokens, chunk), column)] * 3,
        out_shape=[jax.ShapeDtypeStruct((tokens, width), F32), saved, saved, saved],
        compiler_params=params(),
        cost_estimate=light(),
    )(normed, grad, *operands)


def ff_down(base, active, weights, hidden):
    tokens, width = base.shape
    chunk, specs, operands = weight_specs(weights, tokens, width, hidden)
    whole = lambda j: (0, 0)
    return pl.pallas_call(
        down_kernel,
        grid=(hidden // chunk,),
        in_specs=[
            pl.BlockSpec((tokens, width), whole),
            pl.BlockSpec((tokens, chunk), lambda j: (0, j)),
            specs[2],
        ],
        out_specs=pl.BlockSpec((tokens, width), whole),
        out_shape=jax.ShapeDtypeStruct((tokens, width), F32),
        compiler_params=params(),
        cost_estimate=light(),
    )(base, active, operands[2])


def ff_backward_outer(grad, left, one, two, weights, hidden):
    tokens, width = grad.shape
    chunk, specs, operands = weight_specs(weights, tokens, width, hidden)
    whole = lambda j: (0, 0)
    column = lambda j: (0, j)
    half = left.shape[0] // 2
    return pl.pallas_call(
        backward_outer_kernel,
        grid=(hidden // chunk,),
        in_specs=[
            pl.BlockSpec((tokens, width), whole),
            pl.BlockSpec(left.shape, whole),
            pl.BlockSpec((tokens, chunk), column),
            pl.BlockSpec((tokens, chunk), column),
        ]
        + specs,
        out_specs=[pl.BlockSpec((tokens, width), whole)]
        + [pl.BlockSpec((half, chunk), column)] * 4,
        out_shape=[jax.ShapeDtypeStruct((tokens, width), F32)]
        + [jax.ShapeDtypeStruct((half, hidden), BF16)] * 4,
        compiler_params=params(),
        cost_estimate=light(),
    )(grad, left, one, two, *operands)


def ff_outer(left, dgate, dup):
    tokens, hidden = dgate.shape
    chunk = sub_chunk(hidden)
    column = lambda j: (0, j)
    half = left.shape[0] // 2
    return pl.pallas_call(
        outer_kernel,
        grid=(hidden // chunk,),
        in_specs=[pl.BlockSpec(left.shape, lambda j: (0, 0))]
        + [pl.BlockSpec((tokens, chunk), column)] * 2,
        out_specs=[pl.BlockSpec((half, chunk), column)] * 4,
        out_shape=[jax.ShapeDtypeStruct((half, hidden), BF16)] * 4,
        compiler_params=params(),
        cost_estimate=light(),
    )(left, dgate, dup)


def local(
    tokens,
    cotangent,
    norm_gains,
    head_gains,
    conv_kernel,
    mix_in,
    mix_out,
    w_gate,
    w_up,
    w_down,
    conv_c,
):
    first = lax.axis_index("section") == 0
    part = lax.axis_index("seq")
    place = lax.axis_index("fsdp")
    fsdp = lax.axis_size("fsdp")
    chips = fsdp // 2
    chip, core = (place // 2, place % 2)
    stretches, rows, width = tokens.shape[1:]
    hidden = w_gate.shape[2]
    total = stretches * rows
    block = 2 * rows
    gains = norm_gains[0]

    cores = [(i, i ^ 1) for i in range(fsdp)]
    swap = [(0, 1), (1, 0)]

    def after(value, *earlier):
        return lax.optimization_barrier((value, *earlier))[0] if earlier else value

    def to_core(value):
        return lax.ppermute(value, "fsdp", cores)

    def to_peer(value):
        return lax.ppermute(value, "seq", swap)

    def exchange(value, offset):
        return lax.ppermute(value, "fsdp", [(i, i ^ offset) for i in range(fsdp)])

    def gather(shards):
        results = []
        for shard in shards:
            depth, columns = shard.shape
            half = depth // 2
            mine = lax.dynamic_slice_in_dim(shard, part * half, half, 0)
            if results:
                mine = after(mine, results[-1])
            batches = [([0], mine[None])]
            for bit in reversed(range(chips.bit_length() - 1)):
                offsets = [offset ^ (1 << bit) for known, rows_of in batches for offset in known]
                block_of = jnp.concatenate([rows_of for known, rows_of in batches], axis=0)
                batches.append((offsets, exchange(block_of, 2 << bit)))
            arrived = batches[1:]
            held = jnp.zeros((chips, 2, half, columns), BF16)
            held = lax.dynamic_update_slice(
                held, shard.reshape(1, 2, half, columns), (chip, 0, 0, 0)
            )
            for known, near in arrived:
                far = to_peer(near)
                for index, offset in enumerate(known):
                    for value, where in ((near, part), (far, 1 - part)):
                        held = lax.dynamic_update_slice(
                            held, value[index][None, None], (chip ^ offset, where, 0, 0)
                        )
            other = to_core(held)
            full = jnp.broadcast_to(held[:, None], (chips, 2, 2, half, columns))
            full = lax.dynamic_update_slice(full, other[:, None], (0, 1 - core, 0, 0, 0))
            results.append(full.reshape(fsdp * depth, columns))
        return results

    def turned(value):
        cut = value.shape[1] // (2 * fsdp)
        wide = value.reshape(value.shape[0], 2, chips, 2, cut)
        sides = [
            lax.dynamic_index_in_dim(wide, side, 3, keepdims=False) for side in (1 - core, core)
        ]
        return jnp.concatenate(
            [jnp.transpose(side.reshape(-1, 2 * chips * cut)) for side in sides], axis=0
        )

    def blocks(both):
        return both.astype(BF16).reshape(2, chips, -1, both.shape[1])

    def core_sum(left, right):
        half = left.shape[0] // 2
        leaving = matmul(left[:half], right).astype(BF16)
        return blocks(matmul(left[half:], right) + to_core(leaving).astype(F32))

    def core_add(leaving, staying):
        return blocks(staying.astype(F32) + leaving.astype(F32))

    def lone_swap(value, offset):
        pairs = []
        for side in range(2):
            for i in range(fsdp):
                other = (1 - side, i) if offset == "seq" else (side, i ^ offset)
                pairs.append(((2 + side) * fsdp + i, (2 + other[0]) * fsdp + other[1]))
        return lax.ppermute(value, ("section", "seq", "fsdp"), pairs)

    def sides(both):
        return [
            lax.dynamic_index_in_dim(both, side, 0, keepdims=False) for side in (1 - part, part)
        ]

    def crossed(staying, came):
        return (staying.astype(F32) + came.astype(F32)).astype(BF16)

    def fence(*groups):
        return lax.optimization_barrier(groups)

    def together(values, *others):
        return lax.optimization_barrier((*values, *others))[: len(values)]

    def zeros(*shape, kind=BF16):
        return jnp.zeros(shape, kind)

    conv_cut = width // (4 * fsdp)
    c_low = lax.ppermute(conv_c, "section", [(0, 1)])

    def half_of(shard):
        return lax.dynamic_slice_in_dim(shard, part * (shard.shape[0] // 2), shard.shape[0] // 2, 0)

    halves = (half_of(w_gate[0]), half_of(w_up[0]), half_of(w_down[0]))
    if can_pack(2 * fsdp, width, hidden):
        wide_weights = (lax.all_gather(pack_halves(*halves), ("fsdp", "seq"), axis=0),)
    else:
        wide_weights = tuple(
            lax.all_gather(half, ("fsdp", "seq"), axis=0, tiled=True) for half in halves
        )

    positions = (
        jnp.arange(stretches)[:, None] * block + part * rows + jnp.arange(rows)[None, :]
    ).reshape(total)
    part_ref = part.astype(jnp.int32).reshape(1)

    def rope():
        lane = jnp.arange(PAIR)
        frequency = THETA ** (-(lane % (HEAD // 2)).astype(F32) * 2.0 / HEAD)
        angle = positions.astype(F32)[:, None] * frequency[None, :]
        sign = jnp.where(lane % HEAD < HEAD // 2, -1.0, 1.0)
        return (jnp.cos(angle), jnp.sin(angle) * sign[None, :])

    def gain_rows():
        return jnp.zeros((8, PAIR), F32).at[:2].set(jnp.tile(head_gains, (1, 2)))

    def attention_mixer():
        w_in, w_out = gather((mix_in[0], mix_out[0]))
        source = tokens[0].reshape(total, width).astype(F32)
        normed = (source * rms_scale(source) * gains[0]).astype(BF16)
        cosine, sine = rope()
        raw, query, own = project(normed, w_in, cosine, sine, gain_rows())
        peer = to_peer(own)
        heads = attend(part_ref, query, own, peer, rows, stretches)
        resid = source + matmul(heads, w_out)
        normed_two = (resid * rms_scale(resid) * gains[1]).astype(BF16)
        weights = (w_in, w_out, zeros(width, width))
        kept = (normed, raw, query, own, peer, heads, resid, normed_two)
        return (weights, kept, cosine, sine)

    def conv_gather():
        both = jnp.concatenate([c_low, conv_c], axis=1)
        w_in, c_wide, w_out = gather((mix_in[0], both, mix_out[0]))
        w_c = jnp.concatenate([c_wide[:, :width], c_wide[:, width:]], axis=0)
        flat = lambda: zeros(total, width)
        kept = (
            flat(), zeros(total, KV_HEADS * GROUP), flat(), flat(), flat(), flat(),
            zeros(total, width, kind=F32), flat(),
        )
        table = lambda: zeros(total, PAIR, kind=F32)
        return ((w_in, w_out, w_c), kept, table(), table())

    weights, kept, cosine, sine = lax.cond(first, attention_mixer, conv_gather)

    def attention_hidden():
        result, *saved = ff_forward(kept[-1], kept[-2], wide_weights, hidden)
        return (result.astype(BF16), *saved)

    def conv_wait():
        return (zeros(total, width), *[zeros(total, hidden) for _ in range(3)])

    link, active, one, two = lax.cond(first, attention_hidden, conv_wait)
    link = lax.ppermute(link, "section", [(0, 1)])

    def tail_of(value, start):
        return to_peer(value.reshape(stretches, rows, width)[:, start : start + 2])

    def conv_both():
        w_in, w_out, w_c = weights
        source = link.astype(F32)
        scale_one = rms_scale(source)
        normed = (source * scale_one * gains[0]).astype(BF16)
        pair = matmul(normed, w_in)
        left, right = (pair[:, :width], pair[:, width:])
        product = (left * right).astype(BF16)
        tails = tail_of(product, rows - 2).astype(F32)
        conv_gate = matmul(normed, w_c).astype(BF16).astype(F32)
        early = jnp.concatenate([jnp.zeros_like(tails[:1]), tails[:-1]], axis=0)
        before = jnp.where(part == 0, early, tails)
        inner = product.astype(F32).reshape(stretches, rows, width)
        longer = jnp.concatenate([before, inner], axis=1)
        taps = [longer[:, i : i + rows] for i in range(3)]
        state = sum(conv_kernel[i] * taps[i] for i in range(3)).reshape(total, width)
        heads = (conv_gate * state).astype(BF16)
        resid = source + matmul(heads, w_out)
        scale_two = rms_scale(resid)
        normed_two = (resid * scale_two * gains[1]).astype(BF16)
        grad_ff = cotangent[0].reshape(total, width)
        grad_two, active, dgate, dup = ff_both_ways(normed_two, grad_ff, wide_weights, hidden)
        gain_two = jnp.sum(grad_two * resid * scale_two, axis=0)
        grad_resid = grad_ff.astype(F32) + norm_back(grad_two, resid, scale_two, gains[1])
        dmix = grad_resid.astype(BF16)
        dheads = matmul_t(dmix, w_out).astype(BF16).astype(F32)
        dgate_c = (dheads * state).astype(BF16)
        dstate = (dheads * conv_gate).reshape(stretches, rows, width)
        fronts = tail_of(dstate, 0)
        late = jnp.concatenate([fronts[1:], jnp.zeros_like(fronts[:1])], axis=0)
        after = jnp.where(part == 0, fronts, late)
        further = jnp.concatenate([dstate, after], axis=1)
        dproduct = sum(conv_kernel[2 - i] * further[:, i : i + rows] for i in range(3))
        dproduct = dproduct.reshape(total, width).astype(BF16).astype(F32)
        kernel_grad = jnp.stack([jnp.sum(dstate * taps[i], axis=(0, 1)) for i in range(3)])
        dproj = jnp.concatenate([dproduct * right, dproduct * left], axis=1).astype(BF16)
        grad_one = matmul_t(dproj, w_in) + matmul_t(dgate_c, w_c)
        gain_one = jnp.sum(grad_one * source * scale_one, axis=0)
        grad_source = grad_resid + norm_back(grad_one, source, scale_one, gains[0])
        small = jnp.concatenate(
            [jnp.zeros((2, width), F32), gain_one[None], gain_two[None], kernel_grad,
             jnp.zeros((1, width), F32)], axis=0
        )
        lefts = (normed, heads, normed_two, active)
        moved = (dproj, dgate_c, dmix, dgate, dup)
        return (resid, lefts, moved, small, grad_source.astype(BF16))

    def attention_idle():
        flat = lambda: zeros(total, width)
        wide = lambda: zeros(total, hidden)
        lefts = (kept[0], kept[5], kept[7], active)
        moved = (zeros(total, 2 * width), flat(), flat(), wide(), wide())
        back = cotangent[0].reshape(total, width)
        return (zeros(total, width, kind=F32), lefts, moved, zeros(8, width, kind=F32), back)

    conv_resid, lefts, moved, conv_small, grad_link = lax.cond(first, attention_idle, conv_both)
    normed, heads, normed_two, active_both = together(lefts, grad_link)
    grad_ff = lax.ppermute(grad_link, "section", swap)
    conv_dproj, dgate_c, conv_dmix, conv_dgate, conv_dup = moved
    left_down, left_two, left_heads, left_normed = [
        turned(value) for value in (active_both, normed_two, heads, normed)
    ]
    middle = width // 2
    down = [
        sides(core_sum(left_down, grad_ff[:, cut]))
        for cut in (slice(0, middle), slice(middle, None))
    ]
    groups = [[i for i in range(fsdp) if i % 2 == side] for side in range(2)]

    def cross(half):
        return to_peer(half[0])

    def along_all(own):
        return [lax.all_to_all(own, "fsdp", 0, 0, axis_index_groups=groups, tiled=True)]

    class Halving:
        def __init__(self, own):
            self.held, self.bit = (own, 0)
            self.split()

        def split(self):
            count, *shape = self.held.shape
            wide = self.held.reshape(count // 2, 2, *shape)
            side = (chip >> self.bit) % 2
            self.leaving, self.staying = [
                lax.dynamic_index_in_dim(wide, which, 1, keepdims=False)
                for which in (1 - side, side)
            ]

        def send(self, swap_with=exchange):
            return swap_with(self.leaving, 2 << self.bit)

        def add(self, came):
            last = self.staying.shape[0] == 1
            self.held = self.staying.astype(F32) + came.astype(F32)
            self.bit += 1
            if not last:
                self.held = self.held.astype(BF16)
                self.split()
            return self

    def scattered(came):
        return sum(jnp.sum(part.astype(F32), axis=0) for part in came)

    def halves_of(leaving, staying):
        return sides(core_add(to_core(leaving), staying))

    def attention_ff():
        grad_two, *products = ff_backward_outer(grad_ff, left_two, one, two, wide_weights, hidden)
        blank = zeros(chips, 2 * conv_cut, width)
        return (grad_two, halves_of(*products[:2]), *products[2:], [blank, blank])

    def conv_ff():
        products = ff_outer(left_two, conv_dgate, conv_dup)
        mixed = normed.reshape(total, 2, 2 * fsdp, conv_cut)
        mixed = jnp.transpose(mixed, (0, 2, 1, 3)).reshape(total, width)
        lone = sides(core_sum(turned(mixed), dgate_c))
        return (zeros(total, width, kind=F32), halves_of(*products[:2]), *products[2:], lone)

    step, down = fence(first, down)
    down_came = [cross(half) for half in down]
    result = lax.cond(step, attention_ff, conv_ff)
    down_came, (grad_two, gate, up_leaving, up_staying, lone) = fence(down_came, result)

    def sum_down():
        return jnp.concatenate(
            [crossed(half[1], came) for half, came in zip(down, down_came)], axis=2
        )

    def attention_core():
        unused, raw, query, own, peer, unused, resid, unused = kept
        scale_two = rms_scale(resid)
        gain_two = jnp.sum(grad_two * resid * scale_two, axis=0)
        grad_resid = grad_ff.astype(F32) + norm_back(grad_two, resid, scale_two, gains[1])
        dmix = grad_resid.astype(BF16)
        dheads = matmul_t(dmix, weights[1]).astype(BF16)
        up_came = to_core(up_leaving)
        dheads, own_down = fence(dheads, sum_down())
        came = along_all(own_down)
        half = KV_HEADS // 2
        back = functools.partial(attend_back, part_ref, query, own, peer)
        low, dheads = fence(back(dheads, rows, stretches, range(half)), dheads)
        low_recv = to_peer(low[2])
        high = back(dheads, rows, stretches, range(half, KV_HEADS))
        low_recv, high, up_came = fence(low_recv, high, up_came)
        high_recv = to_peer(high[2])
        up = sides(core_add(up_came, up_staying))
        dquery, down_kv = [jnp.concatenate([low[i], high[i]], axis=1) for i in range(2)]
        recv = jnp.concatenate([low_recv, high_recv], axis=1)
        came, recv = fence(came, recv)
        return (came, up, gain_two, grad_resid, dmix, dquery, down_kv, recv)

    def conv_core():
        output = ff_down(conv_resid, active_both, wide_weights, hidden)
        blanks = [zeros(total, width, kind=kind) for kind in (BF16, F32, F32, BF16)]
        up = halves_of(up_leaving, up_staying)
        came = along_all(sum_down())
        came, up, output, blanks = fence(came, up, output, blanks)
        return (came, up, zeros(width, kind=F32), output, *blanks)

    step, gate, lone = fence(first, gate, lone)
    lone_came, gate_came = (lone_swap(lone[0], "seq"), cross(gate))
    result = lax.cond(step, attention_core, conv_core)
    gate_came, lone_came, result = fence(gate_came, lone_came, result)
    down_came, up, gain_two, grad_resid, dmix, dquery, down_kv, recv = result

    def attention_project():
        dproj, grad_one, head_rows = project_back(
            kept[1], dquery, down_kv, recv, cosine, sine, gain_rows(), weights[0]
        )
        inward = sides(core_sum(left_normed, dproj))
        outward = sides(core_sum(left_heads, dmix))
        source = tokens[0].reshape(total, width).astype(F32)
        scale_one = rms_scale(source)
        gain_one = jnp.sum(grad_one * source * scale_one, axis=0)
        grad_source = grad_resid + norm_back(grad_one, source, scale_one, gains[0])
        head_grad = jnp.stack([head_rows[0, :HEAD] + head_rows[0, HEAD:], head_rows[1, :HEAD]])
        head_row = jnp.pad(head_grad.reshape(1, PAIR), ((0, 0), (0, width - PAIR)))
        small = jnp.concatenate(
            [gain_one[None], gain_two[None], jnp.zeros((5, width), F32), head_row], axis=0
        )
        return ([inward, outward], grad_source, small + to_core(small))

    def conv_project():
        outward = sides(core_sum(left_heads, conv_dmix))
        inward = sides(core_sum(left_normed, conv_dproj))
        output = grad_resid
        small = conv_small + to_core(conv_small)
        return ([inward, outward], output, small)

    gate = crossed(gate[1], gate_came)
    step, gate, up = fence(first, gate, up)
    gate_came, up_came = (along_all(gate), cross(up))
    result = lax.cond(step, attention_project, conv_project)
    gate_came, up_came, result = fence(gate_came, up_came, result)
    mix, ends, small = result

    up = Halving(crossed(up[1], up_came))
    mix_came = [cross(half) for half in mix]
    lone = Halving(crossed(lone[1], lone_came))
    up_came, lone_came = (up.send(), lone.send(lone_swap))
    up_came, lone_came, small_came = fence(up_came, lone_came, to_peer(small))
    up, lone, small = (up.add(up_came), lone.add(lone_came), small + small_came)
    small_came = exchange(small, 2)
    bits = chips.bit_length() - 1
    for bit in range(1, bits):
        if bit == 1:
            mix_came, small_came = fence(mix_came, small_came)
            mix = [Halving(crossed(half[1], came)) for half, came in zip(mix, mix_came)]
            small = small + small_came
            mix_came, small_came = ([half.send() for half in mix], exchange(small, 4))
        up_came, lone_came = (up.send(), lone.send(lone_swap))
        up_came, lone_came, mix_came, small_came = fence(
            up_came, lone_came, mix_came, small_came
        )
        up, lone = (up.add(up_came), lone.add(lone_came))
        mix = [half.add(came) for half, came in zip(mix, mix_came)]
        small = small + small_came
        mix_came = [half.send() for half in mix]
        if bit < bits - 1:
            small_came = exchange(small, 4 << bit)
    lone = lone.held[0]
    mail = lax.ppermute(jnp.concatenate([small, lone[:conv_cut]], axis=0), "section", swap)
    mix_came, mail = fence(mix_came, mail)
    small = small + mail[: small.shape[0]]
    c_shard = jnp.where(first, mail[small.shape[0] :], lone[conv_cut:])
    shard_in, shard_out = [half.add(came).held[0] for half, came in zip(mix, mix_came)]
    shards_out = (
        shard_in, shard_out,
        scattered(gate_came), up.held[0], scattered(down_came),
    )
    return (
        ends.reshape(1, 1, stretches, rows, width),
        small[:4].reshape(2, 2, width),
        small[7, :PAIR].reshape(2, HEAD),
        small[4:7],
        *[shard[None] for shard in shards_out],
        c_shard,
    )


def solution(mesh):
    return jax.shard_map(
        local,
        mesh=mesh,
        in_specs=(
            P("fsdp", None, "seq", None),
            P("fsdp", None, "seq", None),
            P("section", None, None),
            P(),
            P(),
            P("section", "fsdp", None),
            P("section", "fsdp", None),
            P("section", "fsdp", None),
            P("section", "fsdp", None),
            P("section", "fsdp", None),
            P(("section", "fsdp"), None),
        ),
        out_specs=(
            P("section", "fsdp", None, "seq", None),
            P(),
            P(),
            P(),
            P("section", ("seq", "fsdp"), None),
            P("section", ("seq", "fsdp"), None),
            P("section", ("seq", "fsdp"), None),
            P("section", ("seq", "fsdp"), None),
            P("section", ("seq", "fsdp"), None),
            P(("section", "seq", "fsdp"), None),
        ),
        check_vma=False,
    )
```

```python
import functools

import jax
import jax.numpy as jnp
from jax import lax
from jax.experimental import pallas as pl
from jax.experimental.pallas import tpu as pltpu
from jax.sharding import PartitionSpec as P

HEADS = 16
KV_HEADS = 8
HEAD = 64
PAIR = 2 * HEAD
GROUP = 2 * PAIR

EPSILON = 1e-05
THETA = 1000000.0
NEGATIVE = -1e30
SCALE = HEAD ** (-0.5)
BF16 = jnp.bfloat16
F32 = jnp.float32
VMEM_LIMIT = 56 * 1024 * 1024


def rms_scale(value):
    return lax.rsqrt(jnp.mean(value * value, axis=-1, keepdims=True) + EPSILON)


def norm_back(grad_out, value, scale, gain):
    inner = grad_out * gain
    return scale * (inner - value * scale * scale * jnp.mean(inner * value, axis=-1, keepdims=True))


def matmul(left, right):
    return jnp.dot(left, right, preferred_element_type=F32)


def matmul_t(left, right):
    return lax.dot_general(left, right, (((1,), (1,)), ((), ())), preferred_element_type=F32)


def outer_sum(left, right):
    return lax.dot_general(left, right, (((0,), (0,)), ((), ())), preferred_element_type=F32)


def params():
    return pltpu.CompilerParams(vmem_limit_bytes=VMEM_LIMIT)


def light():
    return pl.CostEstimate(flops=1 << 20, bytes_accessed=1 << 20, transcendentals=0)


def group_mean(value):
    row = lax.broadcasted_iota(jnp.int32, (PAIR, PAIR), 0) // HEAD
    col = lax.broadcasted_iota(jnp.int32, (PAIR, PAIR), 1) // HEAD
    ones = jnp.where(row == col, 1.0 / HEAD, 0.0).astype(F32)
    return jnp.dot(value, ones, precision=lax.Precision.HIGHEST, preferred_element_type=F32)


def lane_swap(value):
    lane = lax.broadcasted_iota(jnp.int32, value.shape, 1) % HEAD
    return jnp.where(
        lane < HEAD // 2, pltpu.roll(value, PAIR - HEAD // 2, 1), pltpu.roll(value, HEAD // 2, 1)
    )


def project_kernel(x_ref, w_ref, cos_ref, sin_ref, gain_ref, raw_ref, q_ref, kv_ref):
    raw = jnp.dot(x_ref[...], w_ref[...], preferred_element_type=F32).astype(BF16)
    raw_ref[...] = raw
    for part, out in ((0, q_ref), (1, kv_ref)):
        vec = raw[:, part * PAIR : (part + 1) * PAIR].astype(F32)
        normed = vec * lax.rsqrt(group_mean(vec * vec) + EPSILON) * gain_ref[part : part + 1, :]
        turned = normed * cos_ref[...] + lane_swap(normed) * sin_ref[...]
        if part == 1:
            lane = lax.broadcasted_iota(jnp.int32, vec.shape, 1)
            turned = jnp.where(lane < HEAD, turned, vec)
        out[...] = turned.astype(BF16)


def project(normed, weight, cosine, sine, gain_rows):
    tokens, width = normed.shape
    whole = lambda g: (0, 0)
    column = lambda g: (0, g)
    return pl.pallas_call(
        project_kernel,
        grid=(KV_HEADS,),
        in_specs=[
            pl.BlockSpec((tokens, width), whole),
            pl.BlockSpec((width, GROUP), column),
            pl.BlockSpec((tokens, PAIR), whole),
            pl.BlockSpec((tokens, PAIR), whole),
            pl.BlockSpec((8, PAIR), whole),
        ],
        out_specs=[
            pl.BlockSpec((tokens, GROUP), column),
            pl.BlockSpec((tokens, PAIR), column),
            pl.BlockSpec((tokens, PAIR), column),
        ],
        out_shape=[
            jax.ShapeDtypeStruct((tokens, KV_HEADS * GROUP), BF16),
            jax.ShapeDtypeStruct((tokens, KV_HEADS * PAIR), BF16),
            jax.ShapeDtypeStruct((tokens, KV_HEADS * PAIR), BF16),
        ],
        compiler_params=params(),
        cost_estimate=light(),
    )(normed, weight, cosine, sine, gain_rows)


def attend_kernel(rows, stretches, part_ref, q_ref, own_ref, peer_ref, out_ref):
    second = part_ref[0] == 1
    for stretch in range(stretches):
        blocks = []
        for s in range(stretch + 1):
            blocks += [own_ref[s * rows : (s + 1) * rows, :], peer_ref[s * rows : (s + 1) * rows, :]]
        pack = jnp.concatenate(blocks, axis=0)
        keys, values = (pack[:, :HEAD], pack[:, HEAD:])
        early = stretch * 2 * rows
        row = lax.broadcasted_iota(jnp.int32, (rows, 2 * rows), 0)
        col = lax.broadcasted_iota(jnp.int32, (rows, 2 * rows), 1)
        allowed = (col <= row) | ((col >= rows) & second)
        for j in range(2):
            query = q_ref[stretch * rows : (stretch + 1) * rows, j * HEAD : (j + 1) * HEAD]
            scores = matmul_t(query * SCALE, keys)
            last = jnp.where(allowed, scores[:, early:], NEGATIVE)
            scores = jnp.concatenate([scores[:, :early], last], axis=1) if early else last
            exponent = jnp.exp(scores - jnp.max(scores, axis=1, keepdims=True))
            total = jnp.sum(exponent, axis=1, keepdims=True)
            probs = (exponent * (1.0 / total)).astype(BF16)
            out_ref[stretch * rows : (stretch + 1) * rows, j * HEAD : (j + 1) * HEAD] = jnp.dot(
                probs, values, preferred_element_type=F32
            ).astype(BF16)


def attend(part, query, own, peer, rows, stretches):
    tokens = query.shape[0]
    column = lambda g: (0, g)
    return pl.pallas_call(
        functools.partial(attend_kernel, rows, stretches),
        grid=(KV_HEADS,),
        in_specs=[pl.BlockSpec(memory_space=pltpu.SMEM)]
        + [pl.BlockSpec((tokens, PAIR), column)] * 3,
        out_specs=pl.BlockSpec((tokens, PAIR), column),
        out_shape=jax.ShapeDtypeStruct((tokens, KV_HEADS * PAIR), BF16),
        compiler_params=params(),
        cost_estimate=light(),
    )(part, query, own, peer)


def attend_back_kernel(
    rows, stretches, part_ref, q_ref, own_ref, peer_ref, grad_ref, dq_ref, down_ref, dpeer_ref
):
    second = part_ref[0] == 1
    sums = {}
    for stretch in reversed(range(stretches)):
        blocks = []
        for s in range(stretch + 1):
            blocks += [own_ref[s * rows : (s + 1) * rows, :], peer_ref[s * rows : (s + 1) * rows, :]]
        pack = jnp.concatenate(blocks, axis=0)
        keys, values = (pack[:, :HEAD], pack[:, HEAD:])
        early = stretch * 2 * rows
        col = lax.broadcasted_iota(jnp.int32, (2 * rows, rows), 0)
        row = lax.broadcasted_iota(jnp.int32, (2 * rows, rows), 1)
        allowed = (col <= row) | ((col >= rows) & second)
        span = slice(stretch * rows, (stretch + 1) * rows)
        dkeys, dvalues, dquery = (0.0, 0.0, [])
        for j in range(2):
            query = q_ref[span, j * HEAD : (j + 1) * HEAD] * SCALE
            grad = grad_ref[span, j * HEAD : (j + 1) * HEAD]
            scores = matmul_t(keys, query)
            last = jnp.where(allowed, scores[early:], NEGATIVE)
            scores = jnp.concatenate([scores[:early], last], axis=0) if early else last
            exponent = jnp.exp(scores - jnp.max(scores, axis=0, keepdims=True))
            probs = exponent * (1.0 / jnp.sum(exponent, axis=0, keepdims=True))
            dprobs = matmul_t(values, grad)
            dscores = probs * (dprobs - jnp.sum(probs * dprobs, axis=0, keepdims=True))
            dscores = dscores.astype(BF16)
            dvalues += jnp.dot(probs.astype(BF16), grad, preferred_element_type=F32)
            dkeys += jnp.dot(dscores, query, preferred_element_type=F32)
            dquery.append(outer_sum(dscores, keys) * SCALE)
        dq_ref[span, :] = jnp.concatenate(dquery, axis=1)
        both = jnp.concatenate([dkeys, dvalues], axis=1)
        for s in range(stretch + 1):
            for side in range(2):
                piece = both[(2 * s + side) * rows : (2 * s + side + 1) * rows]
                sums[s, side] = sums[s, side] + piece if (s, side) in sums else piece
    for (s, side), value in sums.items():
        out = (down_ref, dpeer_ref)[side]
        out[s * rows : (s + 1) * rows, :] = value.astype(out.dtype)


def attend_back(part, query, own, peer, grad, rows, stretches, groups):
    tokens = query.shape[0]
    count = len(groups)
    column = lambda g: (0, g + groups.start)
    shape = lambda kind: jax.ShapeDtypeStruct((tokens, count * PAIR), kind)
    return pl.pallas_call(
        functools.partial(attend_back_kernel, rows, stretches),
        grid=(count,),
        in_specs=[pl.BlockSpec(memory_space=pltpu.SMEM)]
        + [pl.BlockSpec((tokens, PAIR), column)] * 4,
        out_specs=[pl.BlockSpec((tokens, PAIR), lambda g: (0, g))] * 3,
        out_shape=[shape(F32), shape(F32), shape(BF16)],
        compiler_params=params(),
        cost_estimate=light(),
    )(part, query, own, peer, grad)


def project_back_kernel(
    raw_ref, dq_ref, own_ref, recv_ref, cos_ref, sin_ref, gain_ref, w_ref, pack_ref, normed_ref, head_ref
):
    first = pl.program_id(0) == 0
    grads = []
    for part in range(2):
        vec = raw_ref[:, part * PAIR : (part + 1) * PAIR].astype(F32)
        if part == 0:
            grad = dq_ref[...]
        else:
            grad = own_ref[...] + recv_ref[...].astype(F32)
        gain = gain_ref[part : part + 1, :]
        scale = lax.rsqrt(group_mean(vec * vec) + EPSILON)
        turned = grad * cos_ref[...] - lane_swap(grad) * sin_ref[...]
        gain_sum = jnp.sum(turned * vec * scale, axis=0, keepdims=True)
        inner = turned * gain
        back = scale * (inner - vec * scale * scale * group_mean(inner * vec))
        if part == 1:
            lane = lax.broadcasted_iota(jnp.int32, vec.shape, 1)
            back = jnp.where(lane < HEAD, back, grad)
        back = back.astype(BF16)
        pack_ref[:, part * PAIR : (part + 1) * PAIR] = back
        grads.append((back, gain_sum))
    total = matmul_t(grads[0][0], w_ref[:, :PAIR]) + matmul_t(grads[1][0], w_ref[:, PAIR:])

    @pl.when(first)
    def _():
        normed_ref[...] = total
        head_ref[...] = jnp.zeros_like(head_ref)

    @pl.when(jnp.logical_not(first))
    def _():
        normed_ref[...] += total

    for part in range(2):
        head_ref[part : part + 1, :] += grads[part][1]


def project_back(raw, dquery, own, recv, cosine, sine, gain_rows, weight):
    tokens = raw.shape[0]
    width = weight.shape[0]
    whole = lambda g: (0, 0)
    column = lambda g: (0, g)
    return pl.pallas_call(
        project_back_kernel,
        grid=(KV_HEADS,),
        in_specs=[
            pl.BlockSpec((tokens, GROUP), column),
            pl.BlockSpec((tokens, PAIR), column),
            pl.BlockSpec((tokens, PAIR), column),
            pl.BlockSpec((tokens, PAIR), column),
            pl.BlockSpec((tokens, PAIR), whole),
            pl.BlockSpec((tokens, PAIR), whole),
            pl.BlockSpec((8, PAIR), whole),
            pl.BlockSpec((width, GROUP), column),
        ],
        out_specs=[
            pl.BlockSpec((tokens, GROUP), column),
            pl.BlockSpec((tokens, width), whole),
            pl.BlockSpec((8, PAIR), whole),
        ],
        out_shape=[
            jax.ShapeDtypeStruct((tokens, KV_HEADS * GROUP), BF16),
            jax.ShapeDtypeStruct((tokens, width), F32),
            jax.ShapeDtypeStruct((8, PAIR), F32),
        ],
        compiler_params=params(),
        cost_estimate=light(),
    )(raw, dquery, own, recv, cosine, sine, gain_rows, weight)


LANES = 128


def wide(ref, columns):
    if len(ref.shape) == 2:
        return ref[...]
    count = columns // LANES
    rows = ref.shape[1] // count
    parts = [ref[:, i * rows : (i + 1) * rows, :].reshape(-1, LANES) for i in range(count)]
    return jnp.concatenate(parts, axis=1)


def forward_kernel(
    x_ref, base_ref, g_ref, u_ref, d_ref, out_ref, act_ref, one_ref, two_ref, total_ref
):
    chunk, width = (act_ref.shape[1], out_ref.shape[1])
    gate_part, up_part, down_part = (wide(g_ref, chunk), wide(u_ref, chunk), wide(d_ref, width))
    down = 0.0
    for span in spans(act_ref.shape[1]):
        gate = jnp.dot(x_ref[...], gate_part[:, span], preferred_element_type=F32)
        upward = jnp.dot(x_ref[...], up_part[:, span], preferred_element_type=F32)
        sigma = jax.nn.sigmoid(gate)
        silu = gate * sigma
        active = (silu * upward).astype(BF16)
        act_ref[:, span] = active
        one_ref[:, span] = (upward * sigma * (1.0 + gate * (1.0 - sigma))).astype(BF16)
        two_ref[:, span] = silu.astype(BF16)
        down += jnp.dot(active, down_part[span], preferred_element_type=F32)

    @pl.when(pl.program_id(0) == 0)
    def _():
        total_ref[...] = base_ref[...] + down

    @pl.when(pl.program_id(0) > 0)
    def _():
        total_ref[...] += down

    @pl.when(pl.program_id(0) == pl.num_programs(0) - 1)
    def _():
        out_ref[...] = total_ref[...].astype(BF16)


def store_outer(left_ref, dgate, dup, span, outs):
    half = left_ref.shape[0] // 2
    for right, leave_ref, stay_ref in ((dgate, *outs[:2]), (dup, *outs[2:])):
        product = jnp.dot(left_ref[...], right, preferred_element_type=F32).astype(BF16)
        leave_ref[:, span] = product[:half]
        stay_ref[:, span] = product[half:]


def backward_outer_kernel(grad_ref, left_ref, one_ref, two_ref, g_ref, u_ref, d_ref, out_ref, *outs):
    chunk, width = (one_ref.shape[1], out_ref.shape[1])
    gate_part, up_part, down_part = (wide(g_ref, chunk), wide(u_ref, chunk), wide(d_ref, width))
    total = 0.0
    for span in spans(one_ref.shape[1]):
        active = matmul_t(grad_ref[...], down_part[span])
        dgate = (active * one_ref[:, span].astype(F32)).astype(BF16)
        dup = (active * two_ref[:, span].astype(F32)).astype(BF16)
        store_outer(left_ref, dgate, dup, span, outs)
        total += matmul_t(dgate, gate_part[:, span]) + matmul_t(dup, up_part[:, span])

    @pl.when(pl.program_id(0) == 0)
    def _():
        out_ref[...] = total

    @pl.when(pl.program_id(0) > 0)
    def _():
        out_ref[...] += total


def outer_kernel(left_ref, dg_ref, du_ref, *outs):
    store_outer(left_ref, dg_ref[...], du_ref[...], slice(None), outs)


def both_ways_kernel(x_ref, grad_ref, g_ref, u_ref, d_ref, out_ref, act_ref, dg_ref, du_ref):
    chunk, width = (act_ref.shape[1], out_ref.shape[1])
    gate_part, up_part, down_part = (wide(g_ref, chunk), wide(u_ref, chunk), wide(d_ref, width))
    total = 0.0
    for span in spans(act_ref.shape[1]):
        gate = jnp.dot(x_ref[...], gate_part[:, span], preferred_element_type=F32)
        upward = jnp.dot(x_ref[...], up_part[:, span], preferred_element_type=F32)
        dactive = matmul_t(grad_ref[...], down_part[span])
        sigma = jax.nn.sigmoid(gate)
        silu = gate * sigma
        act_ref[:, span] = (silu * upward).astype(BF16)
        dgate = (dactive * upward * sigma * (1.0 + gate * (1.0 - sigma))).astype(BF16)
        dup = (dactive * silu).astype(BF16)
        dg_ref[:, span] = dgate
        du_ref[:, span] = dup
        total += matmul_t(dgate, gate_part[:, span]) + matmul_t(dup, up_part[:, span])

    @pl.when(pl.program_id(0) == 0)
    def _():
        out_ref[...] = total

    @pl.when(pl.program_id(0) > 0)
    def _():
        out_ref[...] += total


def down_kernel(base_ref, act_ref, d_ref, out_ref):
    down = jnp.dot(act_ref[...], wide(d_ref, out_ref.shape[1]), preferred_element_type=F32)

    @pl.when(pl.program_id(0) == 0)
    def _():
        out_ref[...] = base_ref[...] + down

    @pl.when(pl.program_id(0) > 0)
    def _():
        out_ref[...] += down


def spans(chunk):
    starts = list(range(0, max(chunk - 511, 1), 512))
    return [slice(a, b) for a, b in zip(starts, starts[1:] + [chunk])]


def sub_chunk(chunk):
    return next(size for size in (512, 384, 256, 128, chunk) if chunk % size == 0)


CHUNKS = 4


def can_pack(devices, width, hidden):
    gate_rows, down_rows = (width // devices, hidden // devices)
    return (
        devices % CHUNKS == 0
        and hidden % (CHUNKS * LANES) == 0
        and width % LANES == 0
        and gate_rows % 16 == 0
        and down_rows % 16 == 0
    )


def pack_halves(gate, upward, down):
    cut = lambda w: jnp.transpose(w.reshape(w.shape[0], -1, LANES), (1, 0, 2)).reshape(-1, LANES)
    return jnp.concatenate([cut(gate), cut(upward), cut(down)], axis=0)


def weight_specs(weights, tokens, width, hidden):
    if len(weights) == 3:
        chunk = sub_chunk(hidden)
        column = lambda j: (0, j)
        return (
            chunk,
            [
                pl.BlockSpec((width, chunk), column),
                pl.BlockSpec((width, chunk), column),
                pl.BlockSpec((chunk, width), lambda j: (j, 0)),
            ],
            weights,
        )
    devices = weights[0].shape[0]
    chunk = hidden // CHUNKS
    tall = width // devices * (hidden // LANES)
    piece = tall // CHUNKS
    return (
        chunk,
        [
            pl.BlockSpec((devices, piece, LANES), lambda j: (0, j, 0)),
            pl.BlockSpec((devices, piece, LANES), lambda j: (0, CHUNKS + j, 0)),
            pl.BlockSpec((devices // CHUNKS, tall, LANES), lambda j: (j, 2, 0)),
        ],
        (weights[0],) * 3,
    )


def ff_forward(normed, base, weights, hidden):
    tokens, width = normed.shape
    chunk, specs, operands = weight_specs(weights, tokens, width, hidden)
    whole = lambda j: (0, 0)
    column = lambda j: (0, j)
    saved = jax.ShapeDtypeStruct((tokens, hidden), BF16)
    return pl.pallas_call(
        forward_kernel,
        grid=(hidden // chunk,),
        in_specs=[pl.BlockSpec((tokens, width), whole), pl.BlockSpec((tokens, width), whole)]
        + specs,
        out_specs=[pl.BlockSpec((tokens, width), whole)]
        + [pl.BlockSpec((tokens, chunk), column)] * 3,
        out_shape=[jax.ShapeDtypeStruct((tokens, width), BF16), saved, saved, saved],
        scratch_shapes=[pltpu.VMEM((tokens, width), F32)],
        compiler_params=params(),
        cost_estimate=light(),
    )(normed, base, *operands)


def ff_both_ways(normed, grad, weights, hidden):
    tokens, width = normed.shape
    chunk, specs, operands = weight_specs(weights, tokens, width, hidden)
    whole = lambda j: (0, 0)
    column = lambda j: (0, j)
    saved = jax.ShapeDtypeStruct((tokens, hidden), BF16)
    return pl.pallas_call(
        both_ways_kernel,
        grid=(hidden // chunk,),
        in_specs=[pl.BlockSpec((tokens, width), whole), pl.BlockSpec((tokens, width), whole)]
        + specs,
        out_specs=[pl.BlockSpec((tokens, width), whole)]
        + [pl.BlockSpec((tokens, chunk), column)] * 3,
        out_shape=[jax.ShapeDtypeStruct((tokens, width), F32), saved, saved, saved],
        compiler_params=params(),
        cost_estimate=light(),
    )(normed, grad, *operands)


def ff_down(base, active, weights, hidden):
    tokens, width = base.shape
    chunk, specs, operands = weight_specs(weights, tokens, width, hidden)
    whole = lambda j: (0, 0)
    return pl.pallas_call(
        down_kernel,
        grid=(hidden // chunk,),
        in_specs=[
            pl.BlockSpec((tokens, width), whole),
            pl.BlockSpec((tokens, chunk), lambda j: (0, j)),
            specs[2],
        ],
        out_specs=pl.BlockSpec((tokens, width), whole),
        out_shape=jax.ShapeDtypeStruct((tokens, width), F32),
        compiler_params=params(),
        cost_estimate=light(),
    )(base, active, operands[2])


def ff_backward_outer(grad, left, one, two, weights, hidden):
    tokens, width = grad.shape
    chunk, specs, operands = weight_specs(weights, tokens, width, hidden)
    whole = lambda j: (0, 0)
    column = lambda j: (0, j)
    half = left.shape[0] // 2
    return pl.pallas_call(
        backward_outer_kernel,
        grid=(hidden // chunk,),
        in_specs=[
            pl.BlockSpec((tokens, width), whole),
            pl.BlockSpec(left.shape, whole),
            pl.BlockSpec((tokens, chunk), column),
            pl.BlockSpec((tokens, chunk), column),
        ]
        + specs,
        out_specs=[pl.BlockSpec((tokens, width), whole)]
        + [pl.BlockSpec((half, chunk), column)] * 4,
        out_shape=[jax.ShapeDtypeStruct((tokens, width), F32)]
        + [jax.ShapeDtypeStruct((half, hidden), BF16)] * 4,
        compiler_params=params(),
        cost_estimate=light(),
    )(grad, left, one, two, *operands)


def ff_outer(left, dgate, dup):
    tokens, hidden = dgate.shape
    chunk = sub_chunk(hidden)
    column = lambda j: (0, j)
    half = left.shape[0] // 2
    return pl.pallas_call(
        outer_kernel,
        grid=(hidden // chunk,),
        in_specs=[pl.BlockSpec(left.shape, lambda j: (0, 0))]
        + [pl.BlockSpec((tokens, chunk), column)] * 2,
        out_specs=[pl.BlockSpec((half, chunk), column)] * 4,
        out_shape=[jax.ShapeDtypeStruct((half, hidden), BF16)] * 4,
        compiler_params=params(),
        cost_estimate=light(),
    )(left, dgate, dup)


def local(
    tokens,
    cotangent,
    norm_gains,
    head_gains,
    conv_kernel,
    mix_in,
    mix_out,
    w_gate,
    w_up,
    w_down,
    conv_c,
):
    first = lax.axis_index("section") == 0
    part = lax.axis_index("seq")
    place = lax.axis_index("fsdp")
    fsdp = lax.axis_size("fsdp")
    chips = fsdp // 2
    chip, core = (place // 2, place % 2)
    stretches, rows, width = tokens.shape[1:]
    hidden = w_gate.shape[2]
    total = stretches * rows
    block = 2 * rows
    gains = norm_gains[0]

    cores = [(i, i ^ 1) for i in range(fsdp)]
    swap = [(0, 1), (1, 0)]

    def after(value, *earlier):
        return lax.optimization_barrier((value, *earlier))[0] if earlier else value

    def to_core(value):
        return lax.ppermute(value, "fsdp", cores)

    def to_peer(value):
        return lax.ppermute(value, "seq", swap)

    def exchange(value, offset):
        return lax.ppermute(value, "fsdp", [(i, i ^ offset) for i in range(fsdp)])

    def gather(shards):
        results = []
        for shard in shards:
            depth, columns = shard.shape
            half = depth // 2
            mine = lax.dynamic_slice_in_dim(shard, part * half, half, 0)
            if results:
                mine = after(mine, results[-1])
            batches = [([0], mine[None])]
            for bit in reversed(range(chips.bit_length() - 1)):
                offsets = [offset ^ (1 << bit) for known, rows_of in batches for offset in known]
                block_of = jnp.concatenate([rows_of for known, rows_of in batches], axis=0)
                batches.append((offsets, exchange(block_of, 2 << bit)))
            arrived = batches[1:]
            held = jnp.zeros((chips, 2, half, columns), BF16)
            held = lax.dynamic_update_slice(
                held, shard.reshape(1, 2, half, columns), (chip, 0, 0, 0)
            )
            for known, near in arrived:
                far = to_peer(near)
                for index, offset in enumerate(known):
                    for value, where in ((near, part), (far, 1 - part)):
                        held = lax.dynamic_update_slice(
                            held, value[index][None, None], (chip ^ offset, where, 0, 0)
                        )
            other = to_core(held)
            full = jnp.broadcast_to(held[:, None], (chips, 2, 2, half, columns))
            full = lax.dynamic_update_slice(full, other[:, None], (0, 1 - core, 0, 0, 0))
            results.append(full.reshape(fsdp * depth, columns))
        return results

    def turned(value):
        cut = value.shape[1] // (2 * fsdp)
        wide = value.reshape(value.shape[0], 2, chips, 2, cut)
        sides = [
            lax.dynamic_index_in_dim(wide, side, 3, keepdims=False) for side in (1 - core, core)
        ]
        return jnp.concatenate(
            [jnp.transpose(side.reshape(-1, 2 * chips * cut)) for side in sides], axis=0
        )

    def blocks(both):
        return both.astype(BF16).reshape(2, chips, -1, both.shape[1])

    def core_sum(left, right):
        half = left.shape[0] // 2
        leaving = matmul(left[:half], right).astype(BF16)
        return blocks(matmul(left[half:], right) + to_core(leaving).astype(F32))

    def core_add(leaving, staying):
        return blocks(staying.astype(F32) + leaving.astype(F32))

    def lone_swap(value, offset):
        pairs = []
        for side in range(2):
            for i in range(fsdp):
                other = (1 - side, i) if offset == "seq" else (side, i ^ offset)
                pairs.append(((2 + side) * fsdp + i, (2 + other[0]) * fsdp + other[1]))
        return lax.ppermute(value, ("section", "seq", "fsdp"), pairs)

    def sides(both):
        return [
            lax.dynamic_index_in_dim(both, side, 0, keepdims=False) for side in (1 - part, part)
        ]

    def crossed(staying, came):
        return (staying.astype(F32) + came.astype(F32)).astype(BF16)

    def fence(*groups):
        return lax.optimization_barrier(groups)

    def together(values, *others):
        return lax.optimization_barrier((*values, *others))[: len(values)]

    def zeros(*shape, kind=BF16):
        return jnp.zeros(shape, kind)

    conv_cut = width // (4 * fsdp)
    c_low = lax.ppermute(conv_c, "section", [(0, 1)])

    def half_of(shard):
        return lax.dynamic_slice_in_dim(shard, part * (shard.shape[0] // 2), shard.shape[0] // 2, 0)

    halves = (half_of(w_gate[0]), half_of(w_up[0]), half_of(w_down[0]))
    if can_pack(2 * fsdp, width, hidden):
        wide_weights = (lax.all_gather(pack_halves(*halves), ("fsdp", "seq"), axis=0),)
    else:
        wide_weights = tuple(
            lax.all_gather(half, ("fsdp", "seq"), axis=0, tiled=True) for half in halves
        )

    positions = (
        jnp.arange(stretches)[:, None] * block + part * rows + jnp.arange(rows)[None, :]
    ).reshape(total)
    part_ref = part.astype(jnp.int32).reshape(1)

    def rope():
        lane = jnp.arange(PAIR)
        frequency = THETA ** (-(lane % (HEAD // 2)).astype(F32) * 2.0 / HEAD)
        angle = positions.astype(F32)[:, None] * frequency[None, :]
        sign = jnp.where(lane % HEAD < HEAD // 2, -1.0, 1.0)
        return (jnp.cos(angle), jnp.sin(angle) * sign[None, :])

    def gain_rows():
        return jnp.zeros((8, PAIR), F32).at[:2].set(jnp.tile(head_gains, (1, 2)))

    def attention_mixer():
        w_in, w_out = gather((mix_in[0], mix_out[0]))
        source = tokens[0].reshape(total, width).astype(F32)
        normed = (source * rms_scale(source) * gains[0]).astype(BF16)
        cosine, sine = rope()
        raw, query, own = project(normed, w_in, cosine, sine, gain_rows())
        peer = to_peer(own)
        heads = attend(part_ref, query, own, peer, rows, stretches)
        resid = source + matmul(heads, w_out)
        normed_two = (resid * rms_scale(resid) * gains[1]).astype(BF16)
        weights = (w_in, w_out, zeros(width, width))
        kept = (normed, raw, query, own, peer, heads, resid, normed_two)
        return (weights, kept, cosine, sine)

    def conv_gather():
        both = jnp.concatenate([c_low, conv_c], axis=1)
        w_in, c_wide, w_out = gather((mix_in[0], both, mix_out[0]))
        w_c = jnp.concatenate([c_wide[:, :width], c_wide[:, width:]], axis=0)
        flat = lambda: zeros(total, width)
        kept = (
            flat(), zeros(total, KV_HEADS * GROUP), flat(), flat(), flat(), flat(),
            zeros(total, width, kind=F32), flat(),
        )
        table = lambda: zeros(total, PAIR, kind=F32)
        return ((w_in, w_out, w_c), kept, table(), table())

    weights, kept, cosine, sine = lax.cond(first, attention_mixer, conv_gather)

    def attention_hidden():
        result, *saved = ff_forward(kept[-1], kept[-2], wide_weights, hidden)
        return (result, *saved)

    def conv_wait():
        return (zeros(total, width), *[zeros(total, hidden) for _ in range(3)])

    link, active, one, two = lax.cond(first, attention_hidden, conv_wait)
    link = lax.ppermute(link, "section", [(0, 1)])

    def tail_of(value, start):
        return to_peer(value.reshape(stretches, rows, width)[:, start : start + 2])

    def conv_both():
        w_in, w_out, w_c = weights
        source = link.astype(F32)
        scale_one = rms_scale(source)
        normed = (source * scale_one * gains[0]).astype(BF16)
        pair = matmul(normed, w_in)
        left, right = (pair[:, :width], pair[:, width:])
        product = (left * right).astype(BF16)
        tails = tail_of(product, rows - 2).astype(F32)
        conv_gate = matmul(normed, w_c).astype(BF16).astype(F32)
        early = jnp.concatenate([jnp.zeros_like(tails[:1]), tails[:-1]], axis=0)
        before = jnp.where(part == 0, early, tails)
        inner = product.astype(F32).reshape(stretches, rows, width)
        longer = jnp.concatenate([before, inner], axis=1)
        taps = [longer[:, i : i + rows] for i in range(3)]
        state = sum(conv_kernel[i] * taps[i] for i in range(3)).reshape(total, width)
        heads = (conv_gate * state).astype(BF16)
        resid = source + matmul(heads, w_out)
        scale_two = rms_scale(resid)
        normed_two = (resid * scale_two * gains[1]).astype(BF16)
        grad_ff = cotangent[0].reshape(total, width)
        grad_two, active, dgate, dup = ff_both_ways(normed_two, grad_ff, wide_weights, hidden)
        gain_two = jnp.sum(grad_two * resid * scale_two, axis=0)
        grad_resid = grad_ff.astype(F32) + norm_back(grad_two, resid, scale_two, gains[1])
        dmix = grad_resid.astype(BF16)
        dheads = matmul_t(dmix, w_out).astype(BF16).astype(F32)
        dgate_c = (dheads * state).astype(BF16)
        dstate = (dheads * conv_gate).reshape(stretches, rows, width)
        fronts = tail_of(dstate, 0)
        late = jnp.concatenate([fronts[1:], jnp.zeros_like(fronts[:1])], axis=0)
        after = jnp.where(part == 0, fronts, late)
        further = jnp.concatenate([dstate, after], axis=1)
        dproduct = sum(conv_kernel[2 - i] * further[:, i : i + rows] for i in range(3))
        dproduct = dproduct.reshape(total, width).astype(BF16).astype(F32)
        kernel_grad = jnp.stack([jnp.sum(dstate * taps[i], axis=(0, 1)) for i in range(3)])
        dproj = jnp.concatenate([dproduct * right, dproduct * left], axis=1).astype(BF16)
        grad_one = matmul_t(dproj, w_in) + matmul_t(dgate_c, w_c)
        gain_one = jnp.sum(grad_one * source * scale_one, axis=0)
        grad_source = grad_resid + norm_back(grad_one, source, scale_one, gains[0])
        small = jnp.concatenate(
            [jnp.zeros((2, width), F32), gain_one[None], gain_two[None], kernel_grad,
             jnp.zeros((1, width), F32)], axis=0
        )
        lefts = (normed, heads, normed_two, active)
        moved = (dproj, dgate_c, dmix, dgate, dup)
        return (resid, lefts, moved, small, grad_source.astype(BF16))

    def attention_idle():
        flat = lambda: zeros(total, width)
        wide = lambda: zeros(total, hidden)
        lefts = (kept[0], kept[5], kept[7], active)
        moved = (zeros(total, 2 * width), flat(), flat(), wide(), wide())
        back = cotangent[0].reshape(total, width)
        return (zeros(total, width, kind=F32), lefts, moved, zeros(8, width, kind=F32), back)

    conv_resid, lefts, moved, conv_small, grad_link = lax.cond(first, attention_idle, conv_both)
    normed, heads, normed_two, active_both = together(lefts, grad_link)
    grad_ff = lax.ppermute(grad_link, "section", swap)
    conv_dproj, dgate_c, conv_dmix, conv_dgate, conv_dup = moved
    left_down, left_two, left_heads, left_normed = [
        turned(value) for value in (active_both, normed_two, heads, normed)
    ]
    middle = width // 2
    down = [
        sides(core_sum(left_down, grad_ff[:, cut]))
        for cut in (slice(0, middle), slice(middle, None))
    ]
    groups = [[i for i in range(fsdp) if i % 2 == side] for side in range(2)]

    def cross(half):
        return to_peer(half[0])

    def along_all(own):
        return [lax.all_to_all(own, "fsdp", 0, 0, axis_index_groups=groups, tiled=True)]

    class Halving:
        def __init__(self, own):
            self.held, self.bit = (own, 0)
            self.split()

        def split(self):
            count, *shape = self.held.shape
            wide = self.held.reshape(count // 2, 2, *shape)
            side = (chip >> self.bit) % 2
            self.leaving, self.staying = [
                lax.dynamic_index_in_dim(wide, which, 1, keepdims=False)
                for which in (1 - side, side)
            ]

        def send(self, swap_with=exchange):
            return swap_with(self.leaving, 2 << self.bit)

        def add(self, came):
            last = self.staying.shape[0] == 1
            self.held = self.staying.astype(F32) + came.astype(F32)
            self.bit += 1
            if not last:
                self.held = self.held.astype(BF16)
                self.split()
            return self

    def scattered(came):
        return sum(jnp.sum(part.astype(F32), axis=0) for part in came)

    def halves_of(leaving, staying):
        return sides(core_add(to_core(leaving), staying))

    def attention_ff():
        grad_two, *products = ff_backward_outer(grad_ff, left_two, one, two, wide_weights, hidden)
        blank = zeros(chips, 2 * conv_cut, width)
        return (grad_two, halves_of(*products[:2]), *products[2:], [blank, blank])

    def conv_ff():
        products = ff_outer(left_two, conv_dgate, conv_dup)
        mixed = normed.reshape(total, 2, 2 * fsdp, conv_cut)
        mixed = jnp.transpose(mixed, (0, 2, 1, 3)).reshape(total, width)
        lone = sides(core_sum(turned(mixed), dgate_c))
        return (zeros(total, width, kind=F32), halves_of(*products[:2]), *products[2:], lone)

    step, down = fence(first, down)
    down_came = [cross(half) for half in down]
    result = lax.cond(step, attention_ff, conv_ff)
    down_came, (grad_two, gate, up_leaving, up_staying, lone) = fence(down_came, result)

    def sum_down():
        return jnp.concatenate(
            [crossed(half[1], came) for half, came in zip(down, down_came)], axis=2
        )

    def attention_core():
        unused, raw, query, own, peer, unused, resid, unused = kept
        scale_two = rms_scale(resid)
        gain_two = jnp.sum(grad_two * resid * scale_two, axis=0)
        grad_resid = grad_ff.astype(F32) + norm_back(grad_two, resid, scale_two, gains[1])
        dmix = grad_resid.astype(BF16)
        dheads = matmul_t(dmix, weights[1]).astype(BF16)
        up_came = to_core(up_leaving)
        dheads, own_down = fence(dheads, sum_down())
        came = along_all(own_down)
        half = KV_HEADS // 2
        back = functools.partial(attend_back, part_ref, query, own, peer)
        low, dheads = fence(back(dheads, rows, stretches, range(half)), dheads)
        low_recv = to_peer(low[2])
        high = back(dheads, rows, stretches, range(half, KV_HEADS))
        low_recv, high, up_came = fence(low_recv, high, up_came)
        high_recv = to_peer(high[2])
        up = sides(core_add(up_came, up_staying))
        dquery, down_kv = [jnp.concatenate([low[i], high[i]], axis=1) for i in range(2)]
        recv = jnp.concatenate([low_recv, high_recv], axis=1)
        came, recv = fence(came, recv)
        return (came, up, gain_two, grad_resid, dmix, dquery, down_kv, recv)

    def conv_core():
        output = ff_down(conv_resid, active_both, wide_weights, hidden)
        blanks = [zeros(total, width, kind=kind) for kind in (BF16, F32, F32, BF16)]
        up = halves_of(up_leaving, up_staying)
        came = along_all(sum_down())
        came, up, output, blanks = fence(came, up, output, blanks)
        return (came, up, zeros(width, kind=F32), output, *blanks)

    step, gate, lone = fence(first, gate, lone)
    lone_came, gate_came = (lone_swap(lone[0], "seq"), cross(gate))
    result = lax.cond(step, attention_core, conv_core)
    gate_came, lone_came, result = fence(gate_came, lone_came, result)
    down_came, up, gain_two, grad_resid, dmix, dquery, down_kv, recv = result

    def attention_project():
        dproj, grad_one, head_rows = project_back(
            kept[1], dquery, down_kv, recv, cosine, sine, gain_rows(), weights[0]
        )
        inward = sides(core_sum(left_normed, dproj))
        outward = sides(core_sum(left_heads, dmix))
        source = tokens[0].reshape(total, width).astype(F32)
        scale_one = rms_scale(source)
        gain_one = jnp.sum(grad_one * source * scale_one, axis=0)
        grad_source = grad_resid + norm_back(grad_one, source, scale_one, gains[0])
        head_grad = jnp.stack([head_rows[0, :HEAD] + head_rows[0, HEAD:], head_rows[1, :HEAD]])
        head_row = jnp.pad(head_grad.reshape(1, PAIR), ((0, 0), (0, width - PAIR)))
        small = jnp.concatenate(
            [gain_one[None], gain_two[None], jnp.zeros((5, width), F32), head_row], axis=0
        )
        return ([inward, outward], grad_source, small + to_core(small))

    def conv_project():
        outward = sides(core_sum(left_heads, conv_dmix))
        inward = sides(core_sum(left_normed, conv_dproj))
        output = grad_resid
        small = conv_small + to_core(conv_small)
        return ([inward, outward], output, small)

    gate = crossed(gate[1], gate_came)
    step, gate, up = fence(first, gate, up)
    gate_came, up_came = (along_all(gate), cross(up))
    result = lax.cond(step, attention_project, conv_project)
    gate_came, up_came, result = fence(gate_came, up_came, result)
    mix, ends, small = result

    up = Halving(crossed(up[1], up_came))
    mix_came = [cross(half) for half in mix]
    lone = Halving(crossed(lone[1], lone_came))
    up_came, lone_came = (up.send(), lone.send(lone_swap))
    up_came, lone_came, small_came = fence(up_came, lone_came, to_peer(small))
    up, lone, small = (up.add(up_came), lone.add(lone_came), small + small_came)
    small_came = exchange(small, 2)
    bits = chips.bit_length() - 1
    for bit in range(1, bits):
        if bit == 1:
            mix_came, small_came = fence(mix_came, small_came)
            mix = [Halving(crossed(half[1], came)) for half, came in zip(mix, mix_came)]
            small = small + small_came
            mix_came, small_came = ([half.send() for half in mix], exchange(small, 4))
        up_came, lone_came = (up.send(), lone.send(lone_swap))
        up_came, lone_came, mix_came, small_came = fence(
            up_came, lone_came, mix_came, small_came
        )
        up, lone = (up.add(up_came), lone.add(lone_came))
        mix = [half.add(came) for half, came in zip(mix, mix_came)]
        small = small + small_came
        mix_came = [half.send() for half in mix]
        if bit < bits - 1:
            small_came = exchange(small, 4 << bit)
    lone = lone.held[0]
    mail = lax.ppermute(jnp.concatenate([small, lone[:conv_cut]], axis=0), "section", swap)
    mix_came, mail = fence(mix_came, mail)
    small = small + mail[: small.shape[0]]
    c_shard = jnp.where(first, mail[small.shape[0] :], lone[conv_cut:])
    shard_in, shard_out = [half.add(came).held[0] for half, came in zip(mix, mix_came)]
    shards_out = (
        shard_in, shard_out,
        scattered(gate_came), up.held[0], scattered(down_came),
    )
    return (
        ends.reshape(1, 1, stretches, rows, width),
        small[:4].reshape(2, 2, width),
        small[7, :PAIR].reshape(2, HEAD),
        small[4:7],
        *[shard[None] for shard in shards_out],
        c_shard,
    )


def solution(mesh):
    return jax.shard_map(
        local,
        mesh=mesh,
        in_specs=(
            P("fsdp", None, "seq", None),
            P("fsdp", None, "seq", None),
            P("section", None, None),
            P(),
            P(),
            P("section", "fsdp", None),
            P("section", "fsdp", None),
            P("section", "fsdp", None),
            P("section", "fsdp", None),
            P("section", "fsdp", None),
            P(("section", "fsdp"), None),
        ),
        out_specs=(
            P("section", "fsdp", None, "seq", None),
            P(),
            P(),
            P(),
            P("section", ("seq", "fsdp"), None),
            P("section", ("seq", "fsdp"), None),
            P("section", ("seq", "fsdp"), None),
            P("section", ("seq", "fsdp"), None),
            P("section", ("seq", "fsdp"), None),
            P(("section", "seq", "fsdp"), None),
        ),
        check_vma=False,
    )
```
